32 devices in a mesh: pool: 2 (over y), row: 4 (over z), col: 4 (over x, core).
Axes of the slice: x: 2, y: 2, z: 4, core: 2. Of those that a mesh axis runs over, the one named last changes fastest.
Arguments:
- trial_vectors: bfloat16 [256, 16384], P('col', ('pool', 'row')), parts along dimension 1, may hold values from -6 to 6
- hamiltonian_blocks: bfloat16 [128, 9, 128, 128], P(('pool', 'row')), parts along dimension 0, may hold values from -0.09375 to 0.09375
- correlation_offset: bfloat16 [128, 9, 128, 128], P(('pool', 'row')), parts along dimension 0, may hold values from -0.0625 to 0.0625
- block_columns: int32 [128, 9], P(('pool', 'row')), parts along dimension 0, may hold values from 0 to 63, as said below
- block_phases: int32 [128, 9], P(('pool', 'row')), parts along dimension 0, may hold values from 0 to 1
- block_sizes: int32 [128], P(('pool', 'row')), parts along dimension 0, may hold values from 64 to 128
- shift: float32 [2], P('pool'), parts along dimension 0, may hold values from -0.25 to 0.25
- halfwidth: float32 [2], P('pool'), parts along dimension 0, may hold values from 0.6 to 0.9
Outputs:
- basis: bfloat16 [256, 16384], P('col', ('pool', 'row')), parts along dimension 1
- reduced_h: float32 [512, 256], P('pool', 'col'), parts along dimension 0
The draws below stay inside these ranges and needn't reach their ends.
There are 2 independent parts, one for each index of `pool`. The reference program is written for one: setup_inputs(seed, part) draws one part's arguments, and reference() takes and returns one part's arrays. A program takes and returns all parts, laid end to end along the dimension named above; each array names one. Nothing has to cross between parts.
Inputs may be any that keep to these rules, and one draw needn't show every extreme that they name: `block_columns`: counted periodically over 64 block rows, every entry of row r lies within 5 of r; the first three slots of row r hold r, r - 5 and r + 5, in this order, and no row holds a block column twice.
All inputs are finite; a program needn't handle non-finite values.
Results may differ from the reference program's by a relative error of at most 0.013.
Values may be sent and summed in bfloat16 or wider, within the bound.
No kernel may reach another device: no remote copies, remote signals or barrier semaphores. Data moves between devices by JAX's collectives and lax.ppermute only.
A program may use at most 64 MiB of HBM per device.

```python
import jax
import jax.numpy as jnp
from jax import lax

VECTORS = 256
BLOCK_ORBS = 128
SLOTS_ROW = 9
HALF_BAND = 5
DEGREE = 4
BLOCK_ROWS = 64
ORBITALS = 8192


def draw_block_columns(key, part):
    key = jax.random.fold_in(key, 11)
    spread = 2 * HALF_BAND - 2
    scores = jax.random.randint(key, (BLOCK_ROWS, spread), 0, 1 << 20) * spread + jnp.arange(spread, dtype=jnp.int32)[None, :]
    ranking = jnp.argsort(scores, axis=1)[:, :SLOTS_ROW - 3]
    candidates = jnp.concatenate([jnp.arange(1 - HALF_BAND, 0, dtype=jnp.int32), jnp.arange(1, HALF_BAND, dtype=jnp.int32)])
    chosen = candidates[ranking]
    leading = jnp.broadcast_to(jnp.array([0, -HALF_BAND, HALF_BAND], dtype=jnp.int32)[None, :], (BLOCK_ROWS, 3))
    offsets = jnp.concatenate([leading, chosen], axis=1)
    row_ids = jnp.arange(BLOCK_ROWS, dtype=jnp.int32)[:, None]
    return ((row_ids + offsets) % BLOCK_ROWS).astype(jnp.int32)


def draw_block_sizes(key, part):
    key = jax.random.fold_in(key, 23)
    key_sizes, key_full, key_low = jax.random.split(key, 3)
    orbital_counts = BLOCK_ORBS - jax.random.randint(key_sizes, (BLOCK_ROWS,), 0, BLOCK_ORBS // 2 + 1)
    full_at = jax.random.randint(key_full, (), 0, BLOCK_ROWS)
    low_at = (full_at + 1 + jax.random.randint(key_low, (), 0, BLOCK_ROWS - 1)) % BLOCK_ROWS
    orbital_counts = orbital_counts.at[full_at].set(BLOCK_ORBS).at[low_at].set(BLOCK_ORBS // 2)
    return orbital_counts.astype(jnp.int32)


def with_ends(entries, stream_key, low, high):
    index_at = [jax.random.randint(jax.random.fold_in(stream_key, axis), (), 0, length) for axis, length in enumerate(entries.shape)]
    main_axis = entries.shape.index(max(entries.shape))
    next_to = index_at[:main_axis] + [(index_at[main_axis] + 1) % entries.shape[main_axis]] + index_at[main_axis + 1:]
    return entries.at[tuple(index_at)].set(low).at[tuple(next_to)].set(high)


def level_of(stream_key, shape, cuts, smallest, largest):
    factor_of, own = 1.0, jax.random.fold_in(stream_key, 6)
    for dim, parts in cuts:
        heights = jnp.exp(jax.random.uniform(jax.random.fold_in(own, dim), (parts,), jnp.float32, smallest / len(cuts), largest / len(cuts)))
        factor_of = factor_of * jnp.repeat(heights, shape[dim] // parts).reshape([-1 if axis == dim else 1 for axis in range(len(shape))])
    return factor_of


def normal_values(key, extent, deviation, most, shards=(), kind=jnp.bfloat16):
    factor_of = level_of(key, extent, shards, -0.22, 0.18) if shards else 1.0
    entries = jax.random.normal(key, extent, jnp.float32) * deviation * factor_of
    return jnp.minimum(jnp.maximum(entries, -most), most).astype(kind)


def setup_inputs(seed: int = 0, part: int = 0) -> dict:
    arg_keys = jax.random.split(jax.random.key(seed), 9)
    part_keys = jax.random.split(jax.random.fold_in(arg_keys[8], part), 9)
    return {
        "trial_vectors": normal_values(part_keys[0], (VECTORS, ORBITALS), 1.0, 6.0, ((0, 4), (1, 4))),
        "hamiltonian_blocks": normal_values(part_keys[1], (BLOCK_ROWS, SLOTS_ROW, BLOCK_ORBS, BLOCK_ORBS), (4 * SLOTS_ROW * BLOCK_ORBS) ** -0.5, 0.09375, ((0, 4),)),
        "correlation_offset": normal_values(part_keys[2], (BLOCK_ROWS, SLOTS_ROW, BLOCK_ORBS, BLOCK_ORBS), (9 * SLOTS_ROW * BLOCK_ORBS) ** -0.5, 0.0625, ((0, 4),)),
        "block_columns": draw_block_columns(jax.random.fold_in(jax.random.fold_in(arg_keys[8], part), 71), part),
        "block_phases": with_ends(jax.random.randint(part_keys[4], (BLOCK_ROWS, SLOTS_ROW), 0, 2), jax.random.fold_in(part_keys[4], 1), 0, 1).astype(jnp.int32),
        "block_sizes": draw_block_sizes(jax.random.fold_in(jax.random.fold_in(arg_keys[8], part), 71), part),
        "shift": jnp.clip(jax.random.uniform(part_keys[6], (1,), jnp.float32, -0.25, 0.25), -0.25, 0.25),
        "halfwidth": jnp.clip(jax.random.uniform(part_keys[7], (1,), jnp.float32, 0.6, 0.9), 0.6, 0.9),
    }


def apply_blocks(signed, vectors, columns):
    num_vecs = vectors.shape[0]
    block_grid = vectors.reshape(num_vecs, BLOCK_ROWS, BLOCK_ORBS)

    def one_row(packed):
        block_row, col_ids = packed
        picked = block_grid[:, col_ids].reshape(num_vecs, SLOTS_ROW * BLOCK_ORBS).astype(jnp.float32)
        matrix = jnp.transpose(block_row, (0, 2, 1)).reshape(SLOTS_ROW * BLOCK_ORBS, BLOCK_ORBS).astype(jnp.float32)
        return jnp.dot(picked, matrix, precision=lax.Precision.HIGHEST)
    row_out = lax.map(one_row, (signed, columns))
    return jnp.transpose(row_out, (1, 0, 2)).reshape(num_vecs, BLOCK_ROWS * BLOCK_ORBS)

def reference(trial_vectors, hamiltonian_blocks, correlation_offset, block_columns, block_phases, block_sizes, shift, halfwidth):
    phase_sign = (1 - 2 * block_phases).astype(jnp.bfloat16)[:, :, None, None]
    signed_h = hamiltonian_blocks * phase_sign
    signed_e = correlation_offset * phase_sign
    live_mask = (jnp.arange(BLOCK_ORBS, dtype=jnp.int32)[None, :] < block_sizes[:, None]).astype(jnp.float32).reshape(-1)
    current = trial_vectors * live_mask.astype(jnp.bfloat16)
    previous = current
    for degree in range(DEGREE):
        ham_image = apply_blocks(signed_h, current, block_columns)
        ovl_image = apply_blocks(signed_e, current, block_columns)
        scaled = ((ham_image - shift[0] * (current.astype(jnp.float32) + ovl_image)) / halfwidth[0]).astype(jnp.bfloat16)
        term_one = (-apply_blocks(signed_e, scaled, block_columns)).astype(jnp.bfloat16)
        term_two = -apply_blocks(signed_e, term_one, block_columns)
        filtered = scaled.astype(jnp.float32) + term_one.astype(jnp.float32) + term_two
        if degree == 0:
            updated = live_mask * filtered
        else:
            updated = live_mask * (2.0 * filtered - previous.astype(jnp.float32))
        previous, current = (current, updated.astype(jnp.bfloat16))
    image_h = apply_blocks(signed_h, current, block_columns).astype(jnp.bfloat16)
    image_s = (current.astype(jnp.float32) + apply_blocks(signed_e, current, block_columns)).astype(jnp.bfloat16)
    pair_s = jnp.dot(current.astype(jnp.float32), image_s.T.astype(jnp.float32), preferred_element_type=jnp.float32) / ORBITALS
    pair_h = jnp.dot(current.astype(jnp.float32), image_h.T.astype(jnp.float32), preferred_element_type=jnp.float32) / ORBITALS
    gram_s = 0.5 * (pair_s + pair_s.T)
    gram_h = 0.5 * (pair_h + pair_h.T)
    lower = jnp.linalg.cholesky(gram_s)
    inverse = jax.scipy.linalg.solve_triangular(lower, jnp.eye(VECTORS, dtype=jnp.float32), lower=True)
    reduced = jnp.dot(jnp.dot(inverse, gram_h, precision=lax.Precision.HIGHEST), inverse.T, precision=lax.Precision.HIGHEST)
    rotation = inverse.astype(jnp.bfloat16)
    new_basis = jnp.dot(rotation.astype(jnp.float32), current.astype(jnp.float32), preferred_element_type=jnp.float32).astype(jnp.bfloat16)
    return (new_basis, reduced)
```

```python
import functools

import jax
import jax.numpy as jnp
from jax import lax
from jax.experimental import pallas as pl
from jax.experimental.pallas import tpu as pltpu
from jax.sharding import PartitionSpec as P

HALF_BAND = 5
DEGREE = 4
CORES = 2
PANEL = 32
GROUP = 8

BF16 = jnp.bfloat16
F32 = jnp.float32
NT = (((1,), (1,)), ((), ()))
TN = (((0,), (0,)), ((), ()))

SMEM = pl.BlockSpec(memory_space=pltpu.SMEM)
VMEM = pl.BlockSpec(memory_space=pltpu.VMEM)


def vmem(shape, dtype):
    return pltpu.VMEM(shape, dtype)


def fill_ext(core, own, intra, inter, ext):
    half = own.shape[0]
    ext[HALF_BAND : HALF_BAND + half] = own[...]
    ext[pl.ds((half + HALF_BAND) * (1 - core), HALF_BAND)] = intra[...]
    ext[pl.ds((half + HALF_BAND) * core, HALF_BAND)] = inter[...]


def picked(index, ext, row, slots):
    return jnp.concatenate([ext[index[row, s]] for s in range(slots)], axis=1)


def row_matrix(blocks, row, slots):
    return jnp.concatenate([blocks[row, s] for s in range(slots)], axis=1)


def send_ends(core, full, intra_out, inter_out):
    spare = full.shape[0] - HALF_BAND
    intra_out[...] = full[pl.ds(spare * (1 - core), HALF_BAND)]
    inter_out[...] = full[pl.ds(spare * core, HALF_BAND)]


def both_rows(index, ext, ham, ovl, row):
    slots = ham.shape[1]
    orbs = ham.shape[2]
    matrix = jnp.concatenate([row_matrix(ham, row, slots), row_matrix(ovl, row, slots)], axis=0)
    image = lax.dot_general(picked(index, ext, row, slots), matrix, NT, preferred_element_type=F32)
    return image[:, :orbs], image[:, orbs:]


def one_row(index, ext, ovl, row):
    slots = ovl.shape[1]
    return lax.dot_general(
        picked(index, ext, row, slots), row_matrix(ovl, row, slots), NT, preferred_element_type=F32
    )


def scaled_kernel(index, ints, scal, own, intra, inter, ham, ovl, out, intra_out, inter_out, ext):
    core = ints[0]
    fill_ext(core, own, intra, inter, ext)
    shift, inv = scal[0], scal[1]
    for row in range(own.shape[0]):
        image_h, image_e = both_rows(index, ext, ham, ovl, row)
        mine = own[row].astype(F32)
        out[row] = ((image_h - shift * (mine + image_e)) * inv).astype(BF16)
    send_ends(core, out, intra_out, inter_out)


def term_kernel(index, ints, own, intra, inter, ovl, out, intra_out, inter_out, ext):
    core = ints[0]
    fill_ext(core, own, intra, inter, ext)
    for row in range(own.shape[0]):
        out[row] = (-one_row(index, ext, ovl, row)).astype(BF16)
    send_ends(core, out, intra_out, inter_out)


def update_kernel(first, index, ints, own, intra, inter, scaled, *rest):
    if first:
        ovl, out, intra_out, inter_out, ext = rest
    else:
        previous, ovl, out, intra_out, inter_out, ext = rest
    core = ints[0]
    fill_ext(core, own, intra, inter, ext)
    lane = lax.broadcasted_iota(jnp.int32, own.shape[1:], 1)
    for row in range(own.shape[0]):
        filtered = scaled[row].astype(F32) + own[row].astype(F32) - one_row(index, ext, ovl, row)
        if not first:
            filtered = 2.0 * filtered - previous[row].astype(F32)
        out[row] = jnp.where(lane < ints[2 + row], filtered, 0.0).astype(BF16)
    send_ends(core, out, intra_out, inter_out)


def gram_kernel(others, index, ints, own, intra, inter, *rest):
    y_others, (ham, ovl, keep, send, ext, images, both) = rest[:others], rest[others:]
    core, chip = ints[0], ints[1]
    fill_ext(core, own, intra, inter, ext)
    half, _, orbs = own.shape
    for row in range(half):
        image_h, image_e = both_rows(index, ext, ham, ovl, row)
        images[0, :, row * orbs : (row + 1) * orbs] = (own[row].astype(F32) + image_e).astype(BF16)
        images[1, :, row * orbs : (row + 1) * orbs] = image_h.astype(BF16)
    for step, vecs in enumerate((own, *y_others)):
        where = lax.rem(chip + step, others + 1)
        flat = jnp.concatenate([vecs[row] for row in range(half)], axis=1)
        for matrix in range(2):
            both[matrix, where] = lax.dot_general(
                images[matrix], flat, NT, preferred_element_type=F32
            )
    keep[...] = both[core]
    send[...] = both[1 - core]


def split3(value):
    high = value.astype(BF16)
    rest = value - high.astype(F32)
    middle = rest.astype(BF16)
    low = (rest - middle.astype(F32)).astype(BF16)
    return high, middle, low


def reciprocal(value):
    guess = pl.reciprocal(value, approx=True)
    return guess * (2.0 - value * guess)


def panel_inverse(block):
    lane = lax.broadcasted_iota(jnp.int32, (PANEL, 128), 1)
    rows = lax.broadcasted_iota(jnp.int32, (PANEL, 128), 0)
    work = jnp.where(lane < PANEL, block, jnp.where(lax.rem(lane, PANEL) == rows, 1.0, 0.0))
    pieces = [work[g * GROUP : (g + 1) * GROUP] for g in range(PANEL // GROUP)]
    sub = lax.broadcasted_iota(jnp.int32, (GROUP, 128), 0)
    groups = PANEL // GROUP
    pivots = []
    for g in range(groups):
        columns = [
            [
                jnp.broadcast_to(pieces[v][:, g * GROUP + j : g * GROUP + j + 1], (GROUP, 128))
                for v in range(g, groups)
            ]
            for j in range(GROUP)
        ]
        pivot = jnp.ones((GROUP, 128), F32)
        for j in range(GROUP):
            at = jnp.broadcast_to(columns[j][0][j : j + 1], (GROUP, 128))
            pivot = jnp.where(sub == j, at, pivot)
            inv = reciprocal(at)
            factors = [c * inv for c in columns[j]]
            factors[0] = jnp.where(sub > j, factors[0], 0.0)
            for later in range(j + 1, GROUP):
                top = jnp.broadcast_to(columns[later][0][j : j + 1], (GROUP, 128))
                columns[later] = [c - f * top for c, f in zip(columns[later], factors)]
            top = jnp.broadcast_to(pieces[g][j : j + 1], (GROUP, 128))
            for v in range(g, groups):
                pieces[v] = pieces[v] - factors[v - g] * top
        pivots.append(pivot)
    pivot = jnp.concatenate(pivots, axis=0)
    root = lax.rsqrt(pivot)
    root = root * (1.5 - 0.5 * ((pivot * root) * root))
    return jnp.concatenate(pieces, axis=0) * root


def factor(work, inverse):
    size = work.shape[0]
    wide = lax.broadcasted_iota(jnp.int32, (PANEL, size), 1)
    tall = lax.broadcasted_iota(jnp.int32, (PANEL, size), 0)
    lane = lax.broadcasted_iota(jnp.int32, (PANEL, 128), 1)
    zero = jnp.zeros((PANEL, size), BF16)
    for start in range(0, size, PANEL):
        rows = work[start : start + PANEL, :]
        tile = start // 128 * 128
        block = work[start : start + PANEL, tile : tile + 128]
        if start % 128:
            block = pltpu.roll(block, 128 - start % 128, axis=1)
        t_high, t_mid, t_low = split3(panel_inverse(block))
        first = jnp.where(lane < 2 * PANEL, t_high, jnp.where(lane < 3 * PANEL, t_mid, t_low))
        second = jnp.where(lane < 2 * PANEL, t_high, jnp.where(lane < 3 * PANEL, t_mid, t_high))
        left = jnp.concatenate([first, second], axis=1)
        spread = jnp.where(lax.rem(wide, 128) < PANEL, jnp.zeros_like(left[:, :1]), jnp.ones_like(left[:, :1]))
        left = left * spread[:, : left.shape[1]]
        inside = (wide >= start) & (wide < start + PANEL)
        rows = jnp.where(inside, jnp.where(wide - start == tall, 1.0, 0.0), rows)
        r_high, r_mid, r_low = split3(rows)
        right = jnp.concatenate([zero, r_high, r_high, r_high, zero, r_mid, r_mid, r_low], axis=0)
        new = jnp.dot(left, right, preferred_element_type=F32)
        inverse[start : start + PANEL, :] = jnp.where(wide < start + PANEL, new, 0.0)
        after = start + PANEL
        if after < size:
            high, middle, low = split3(new)
            base = after // 128 * 128
            lhs = jnp.concatenate([high, high, middle, middle, high, low], axis=0)[:, base:]
            rhs = jnp.concatenate([high, middle, high, middle, low, high], axis=0)
            change = lax.dot_general(lhs, rhs, TN, preferred_element_type=F32)[after - base :]
            columns = lax.broadcasted_iota(jnp.int32, change.shape, 1)
            old = work[after:, :]
            work[after:, :] = jnp.where((columns >= start) & (columns < after), 0.0, old) - change


def finish_kernel(chips, scale, ints, *refs):
    mine, theirs = refs[:chips], refs[chips : 2 * chips]
    (y_mine, y_theirs, basis, reduced, pair, work, inverse) = (
        refs[2 * chips : 3 * chips],
        refs[3 * chips : 4 * chips],
        *refs[4 * chips :],
    )
    core, chip, col = ints[0], ints[1], ints[2]
    vecs = y_mine[0].shape[1]
    half, orbs = y_mine[0].shape[0], y_mine[0].shape[2]
    local_vecs = basis.shape[0]
    for step in range(chips):
        where = pl.multiple_of(lax.rem(chip + step, chips) * vecs, vecs)
        for k in range(chips):
            pair[core, pl.ds(where, vecs), k * vecs : (k + 1) * vecs] = mine[step][k]
            pair[1 - core, pl.ds(where, vecs), k * vecs : (k + 1) * vecs] = theirs[step][k]
    work[...] = (pair[0] + pair[0].T) * scale
    factor(work, inverse)
    start = pl.multiple_of(col * local_vecs, local_vecs)
    own_rows = inverse[pl.ds(start, local_vecs), :]
    gram_h = (pair[1] + pair[1].T) * scale
    half_way = lax.dot_general(
        gram_h, own_rows, NT, precision=lax.Precision.HIGHEST, preferred_element_type=F32
    )
    reduced[...] = jnp.dot(
        inverse[...], half_way, precision=lax.Precision.HIGHEST, preferred_element_type=F32
    )
    rotation = own_rows.astype(BF16)
    turned = []
    for step in range(chips):
        which = lax.rem(chip + step, chips)
        part = rotation[:, :vecs]
        for k in range(1, chips):
            part = jnp.where(which == k, rotation[:, k * vecs : (k + 1) * vecs], part)
        turned.append(part)
    turned = jnp.concatenate(turned, axis=1)
    for which, group in ((core, y_mine), (1 - core, y_theirs)):
        for row in range(half):
            everything = jnp.concatenate([group[step][row] for step in range(chips)], axis=0)
            result = jnp.dot(turned, everything, preferred_element_type=F32).astype(BF16)
            at = pl.multiple_of((which * half + row) * orbs, orbs)
            basis[:, pl.ds(at, orbs)] = result


def local(
    trial_vectors,
    hamiltonian_blocks,
    correlation_offset,
    block_columns,
    block_phases,
    block_sizes,
    shift,
    halfwidth,
):
    blocks_dev, slots = block_columns.shape
    orbs = hamiltonian_blocks.shape[2]
    num_rows, num_cols = lax.axis_size("row"), lax.axis_size("col")
    total_blocks = blocks_dev * num_rows
    half = blocks_dev // CORES
    chips = num_cols // CORES
    local_vecs = trial_vectors.shape[0]
    vecs = local_vecs * CORES
    size = local_vecs * num_cols
    row, col = lax.axis_index("row"), lax.axis_index("col")
    core, chip = col % CORES, col // CORES

    def swap_cores(value):
        return lax.ppermute(value, "col", [(c, c ^ 1) for c in range(num_cols)])

    def swap_chips(value):
        pairs = []
        for r in range(num_rows):
            for x in range(chips):
                upper = r * num_cols + x * CORES + 1
                lower = (r + 1) % num_rows * num_cols + x * CORES
                pairs += [(upper, lower), (lower, upper)]
        return lax.ppermute(value, ("row", "col"), pairs)

    def from_chip(value, step):
        pairs = [((c + step * CORES) % num_cols, c) for c in range(num_cols)]
        return lax.ppermute(value, "col", pairs)

    live = jnp.arange(orbs, dtype=jnp.int32)[None, :] < block_sizes[:, None]
    blocks = jnp.swapaxes(trial_vectors.reshape(local_vecs, blocks_dev, orbs), 0, 1)
    blocks = jnp.where(live[:, None, :], blocks, jnp.zeros((), BF16))
    got = swap_cores(lax.dynamic_slice_in_dim(blocks, (1 - core) * half, half, 0))
    own = lax.dynamic_slice_in_dim(blocks, core * half, half, 0)
    current = jnp.where(
        core == 0, jnp.concatenate([own, got], axis=1), jnp.concatenate([got, own], axis=1)
    )
    spare = half - HALF_BAND
    ends = (
        lax.dynamic_slice_in_dim(current, spare * (1 - core), HALF_BAND, 0),
        lax.dynamic_slice_in_dim(current, spare * core, HALF_BAND, 0),
    )

    def own_half(value):
        return lax.dynamic_slice_in_dim(value, core * half, half, 0)

    sign = (1 - 2 * own_half(block_phases)).astype(BF16)[:, :, None, None]
    ham = pltpu.with_memory_space_constraint(own_half(hamiltonian_blocks) * sign, pltpu.VMEM)
    ovl = pltpu.with_memory_space_constraint(own_half(correlation_offset) * sign, pltpu.VMEM)
    local_rows = jnp.arange(half, dtype=jnp.int32)[:, None]
    global_rows = row * blocks_dev + core * half + local_rows
    index = local_rows + (own_half(block_columns) - global_rows + HALF_BAND) % total_blocks
    ints = jnp.concatenate(
        [jnp.stack([core, chip]).astype(jnp.int32), own_half(block_sizes).astype(jnp.int32)]
    )
    scal = jnp.concatenate([shift, 1.0 / halfwidth])

    state = jax.ShapeDtypeStruct((half, vecs, orbs), BF16)
    end = jax.ShapeDtypeStruct((HALF_BAND, vecs, orbs), BF16)
    ext = pltpu.VMEM((half + 2 * HALF_BAND, vecs, orbs), BF16)
    params = pltpu.CompilerParams(vmem_limit_bytes=16 << 20)

    def step_call(kernel, name, scalars, arrays):
        return pl.pallas_call(
            kernel,
            name=name,
            out_shape=(state, end, end),
            in_specs=[SMEM] * len(scalars) + [VMEM] * len(arrays),
            out_specs=(VMEM, VMEM, VMEM),
            scratch_shapes=[ext],
            compiler_params=params,
        )(*scalars, *arrays)

    def exchange(ends):
        inter = swap_chips(ends[1])
        return swap_cores(ends[0]), inter

    previous = current
    for degree in range(DEGREE):
        halo = exchange(ends)
        scaled, *ends = step_call(
            scaled_kernel, "scaled", (index, ints, scal), (current, *halo, ham, ovl)
        )
        halo = exchange(ends)
        term, *ends = step_call(term_kernel, "term", (index, ints), (scaled, *halo, ovl))
        halo = exchange(ends)
        first = degree == 0
        arrays = (term, *halo, scaled) + (() if first else (previous,)) + (ovl,)
        updated, *ends = step_call(
            functools.partial(update_kernel, first), "update", (index, ints), arrays
        )
        previous, current = current, updated

    halo = exchange(ends)
    y_mine = [current] + [from_chip(current, step) for step in range(1, chips)]
    part = jax.ShapeDtypeStruct((chips, vecs, vecs), F32)
    keep, send = pl.pallas_call(
        functools.partial(gram_kernel, chips - 1),
        name="gram",
        out_shape=(part, part),
        in_specs=[SMEM] * 2 + [VMEM] * (4 + chips),
        out_specs=(VMEM, VMEM),
        scratch_shapes=[
            ext,
            pltpu.VMEM((2, vecs, half * orbs), BF16),
            pltpu.VMEM((2, chips, vecs, vecs), F32),
        ],
        compiler_params=params,
    )(index, ints, current, *halo, *y_mine[1:], ham, ovl)
    summed = keep + swap_cores(send)
    if num_rows & (num_rows - 1):
        summed = lax.psum(summed, "row")
    else:
        bit = 1
        while bit < num_rows:
            summed = summed + lax.ppermute(
                summed, "row", [(r, r ^ bit) for r in range(num_rows)]
            )
            bit *= 2
    mine = [summed] + [from_chip(summed, step) for step in range(1, chips)]
    theirs = [swap_cores(value) for value in mine]
    y_theirs = [swap_cores(value) for value in y_mine]
    basis, reduced = pl.pallas_call(
        functools.partial(finish_kernel, chips, 0.5 / (total_blocks * orbs)),
        name="finish",
        out_shape=(
            jax.ShapeDtypeStruct((local_vecs, blocks_dev * orbs), BF16),
            jax.ShapeDtypeStruct((size, local_vecs), F32),
        ),
        in_specs=[SMEM] + [VMEM] * (4 * chips),
        out_specs=(VMEM, VMEM),
        scratch_shapes=[
            pltpu.VMEM((2, size, size), F32),
            pltpu.VMEM((size, size), F32),
            pltpu.VMEM((size, size), F32),
        ],
        compiler_params=params,
    )(jnp.stack([core, chip, col]).astype(jnp.int32), *mine, *theirs, *y_mine, *y_theirs)
    return basis, reduced


def solution(mesh):
    return jax.shard_map(
        local,
        mesh=mesh,
        in_specs=(
            P("col", ("pool", "row")),
            P(("pool", "row"), None, None, None),
            P(("pool", "row"), None, None, None),
            P(("pool", "row"), None),
            P(("pool", "row"), None),
            P(("pool", "row")),
            P("pool"),
            P("pool"),
        ),
        out_specs=(P("col", ("pool", "row")), P("pool", "col")),
        check_vma=False,
    )
```

```python
import functools

import jax
import jax.numpy as jnp
from jax import lax
from jax.experimental import pallas as pl
from jax.experimental.pallas import tpu as pltpu
from jax.sharding import PartitionSpec as P

HALF_BAND = 5
DEGREE = 4
CORES = 2
PANEL = 32
GROUP = 8
DIAGONAL_ROWS = 16

BF16 = jnp.bfloat16
F32 = jnp.float32
NT = (((1,), (1,)), ((), ()))
TN = (((0,), (0,)), ((), ()))

SMEM = pl.BlockSpec(memory_space=pltpu.SMEM)
VMEM = pl.BlockSpec(memory_space=pltpu.VMEM)
HBM = pl.BlockSpec(memory_space=pltpu.HBM)


def vmem(shape, dtype):
    return pltpu.VMEM(shape, dtype)


def fill_ext(core, own, intra, inter, ext):
    half = own.shape[0]
    ext[HALF_BAND : HALF_BAND + half] = own[...]
    ext[pl.ds((half + HALF_BAND) * (1 - core), HALF_BAND)] = intra[...]
    ext[pl.ds((half + HALF_BAND) * core, HALF_BAND)] = inter[...]


def picked(table, ext, row):
    index, signs = table
    slots = index.shape[1]
    return jnp.concatenate(
        [ext[index[row, s]] * signs[row, s].astype(BF16) for s in range(slots)], axis=1
    )


def row_matrix(blocks, row):
    return jnp.concatenate([blocks[row, s] for s in range(blocks.shape[1])], axis=1)


def send_ends(core, full, intra_out, inter_out):
    spare = full.shape[0] - HALF_BAND
    intra_out[...] = full[pl.ds(spare * (1 - core), HALF_BAND)]
    inter_out[...] = full[pl.ds(spare * core, HALF_BAND)]


def image_of(table, ext, matrices, row):
    matrix = jnp.concatenate([row_matrix(blocks, row) for blocks in matrices], axis=0)
    return lax.dot_general(matrix, picked(table, ext, row), NT, preferred_element_type=F32)


def both_rows(table, ext, ham, ovl, row):
    orbs = ham.shape[2]
    image = image_of(table, ext, (ham, ovl), row)
    return image[:orbs].T, image[orbs:].T


def one_row(table, ext, ovl, row):
    return image_of(table, ext, (ovl,), row).T


def cut_kernel(ints, sizes, trial, keep, give):
    half, _, orbs = keep.shape
    core = ints[0]
    lane = lax.broadcasted_iota(jnp.int32, keep.shape[1:], 1)
    for out, which in ((give, 1 - core), (keep, core)):
        for row in range(half):
            at = which * half + row
            values = trial[:, pl.ds(pl.multiple_of(at * orbs, orbs), orbs)].astype(F32)
            out[row] = jnp.where(lane < sizes[at], values, 0.0).astype(BF16)


def load_kernel(total, ints, columns, phases, ham, ovl, ham_out, ovl_out, index, signs, sems):
    half, slots = index.shape
    first = ints[0] * half
    copies = []
    for row in range(half):
        for matrix, (source, target) in enumerate(((ham, ham_out), (ovl, ovl_out))):
            copies.append(
                pltpu.make_async_copy(
                    source.at[first + row], target.at[row], sems.at[matrix, row]
                )
            )
    for copy in copies:
        copy.start()
    start = ints[3] + first

    def fill(row, _):
        for slot in range(slots):
            away = columns[first + row, slot] - (start + row) + HALF_BAND
            away = jnp.where(away < 0, away + total, away)
            away = jnp.where(away >= total, away - total, away)
            index[row, slot] = row + away
            signs[row, slot] = (1 - 2 * phases[first + row, slot]).astype(F32)
        return 0

    lax.fori_loop(0, half, fill, 0)
    for copy in copies:
        copy.wait()


def scaled_kernel(
    ints, index, signs, shift, width, own, intra, inter, ham, ovl, out, intra_out, inter_out, ext
):
    core = ints[0]
    fill_ext(core, own, intra, inter, ext)
    inv = 1.0 / (jnp.zeros(own.shape[1:], F32) + width[0])
    for row in range(own.shape[0]):
        image_h, image_e = both_rows((index, signs), ext, ham, ovl, row)
        mine = own[row].astype(F32)
        out[row] = ((image_h - shift[0] * (mine + image_e)) * inv).astype(BF16)
    send_ends(core, out, intra_out, inter_out)


def term_kernel(ints, index, signs, own, intra, inter, ovl, out, intra_out, inter_out, ext):
    core = ints[0]
    fill_ext(core, own, intra, inter, ext)
    for row in range(own.shape[0]):
        out[row] = (-one_row((index, signs), ext, ovl, row)).astype(BF16)
    send_ends(core, out, intra_out, inter_out)


def update_kernel(first, ints, index, signs, sizes, own, intra, inter, scaled, *rest):
    if first:
        ovl, out, intra_out, inter_out, ext = rest
    else:
        previous, ovl, out, intra_out, inter_out, ext = rest
    core = ints[0]
    half = own.shape[0]
    fill_ext(core, own, intra, inter, ext)
    lane = lax.broadcasted_iota(jnp.int32, own.shape[1:], 1)
    for row in range(half):
        image = one_row((index, signs), ext, ovl, row)
        filtered = scaled[row].astype(F32) + own[row].astype(F32) - image
        if not first:
            filtered = 2.0 * filtered - previous[row].astype(F32)
        out[row] = jnp.where(lane < sizes[core * half + row], filtered, 0.0).astype(BF16)
    send_ends(core, out, intra_out, inter_out)


def images_kernel(ints, index, signs, own, intra, inter, ham, ovl, out, ext):
    core = ints[0]
    fill_ext(core, own, intra, inter, ext)
    half, _, orbs = own.shape
    for row in range(half):
        image_h, image_e = both_rows((index, signs), ext, ham, ovl, row)
        at = slice(row * orbs, (row + 1) * orbs)
        out[0, :, at] = (own[row].astype(F32) + image_e).astype(BF16)
        out[1, :, at] = image_h.astype(BF16)


def gram_kernel(chips, ints, index, signs, own, intra, inter, ham, ovl, ready, *rest):
    first, *others = rest[:chips]
    keep, send, ext, images, both = rest[chips:]
    images_kernel(ints, index, signs, own, intra, inter, ham, ovl, images, ext)
    core, chip = ints[0], ints[1]
    half, local_vecs, _ = own.shape
    vecs = CORES * local_vecs
    groups = [[first[row] for row in range(half)], [own[row] for row in range(half)]]
    for other in others:
        groups += [[other[g, row] for row in range(half)] for g in range(CORES)]
    flat = jnp.concatenate([jnp.concatenate(group, axis=1) for group in groups], axis=0)
    eye = lax.broadcasted_iota(jnp.int32, (vecs, vecs), 0) == lax.broadcasted_iota(
        jnp.int32, (vecs, vecs), 1
    )
    for matrix in range(2):
        mine = jnp.concatenate([ready[matrix], images[matrix]], axis=0)
        pair = lax.dot_general(mine, flat, NT, preferred_element_type=F32)
        for step in range(chips):
            where = pl.multiple_of(lax.rem(chip + step, chips) * vecs, vecs)
            block = pair[:, step * vecs : (step + 1) * vecs]
            both[matrix, pl.ds(where, vecs), :] = block.astype(BF16)
        diagonal = jnp.sum(jnp.where(eye, pair[:, :vecs], 0.0), axis=0, keepdims=True)
        both[matrix, chips * vecs :, :] = diagonal_parts(diagonal)
    keep[...] = both[core]
    send[...] = both[1 - core]


def diagonal_parts(diagonal):
    high, middle, low = (part.astype(F32) for part in split3(diagonal))
    rows = lax.broadcasted_iota(jnp.int32, (DIAGONAL_ROWS, diagonal.shape[1]), 0)
    parts = jnp.where(rows == 0, high, jnp.where(rows == 1, middle, jnp.where(rows == 2, low, 0.0)))
    return parts.astype(BF16)


def diagonal_of(payload):
    parts = payload[payload.shape[0] - DIAGONAL_ROWS :, :].astype(F32)
    return parts[0:1] + (parts[1:2] + parts[2:3])


def add_kernel(left, right, out):
    body = left.shape[0] - DIAGONAL_ROWS
    out[:body] = (left[:body, :].astype(F32) + right[:body, :].astype(F32)).astype(BF16)
    out[body:] = diagonal_parts(diagonal_of(left) + diagonal_of(right))


def split3(value):
    high = value.astype(BF16)
    rest = value - high.astype(F32)
    middle = rest.astype(BF16)
    low = (rest - middle.astype(F32)).astype(BF16)
    return high, middle, low


def reciprocal(value):
    guess = pl.reciprocal(value, approx=True)
    return guess * (2.0 - value * guess)


def panel_inverse(block):
    lane = lax.broadcasted_iota(jnp.int32, (PANEL, 128), 1)
    rows = lax.broadcasted_iota(jnp.int32, (PANEL, 128), 0)
    work = jnp.where(lane < PANEL, block, jnp.where(lax.rem(lane, PANEL) == rows, 1.0, 0.0))
    pieces = [work[g * GROUP : (g + 1) * GROUP] for g in range(PANEL // GROUP)]
    sub = lax.broadcasted_iota(jnp.int32, (GROUP, 128), 0)
    groups = PANEL // GROUP
    pivots = []
    for g in range(groups):
        columns = [
            [
                jnp.broadcast_to(pieces[v][:, g * GROUP + j : g * GROUP + j + 1], (GROUP, 128))
                for v in range(g, groups)
            ]
            for j in range(GROUP)
        ]
        pivot = jnp.ones((GROUP, 128), F32)
        for j in range(GROUP):
            at = jnp.broadcast_to(columns[j][0][j : j + 1], (GROUP, 128))
            pivot = jnp.where(sub == j, at, pivot)
            inv = reciprocal(at)
            factors = [c * inv for c in columns[j]]
            factors[0] = jnp.where(sub > j, factors[0], 0.0)
            for later in range(j + 1, GROUP):
                top = jnp.broadcast_to(columns[later][0][j : j + 1], (GROUP, 128))
                columns[later] = [c - f * top for c, f in zip(columns[later], factors)]
            top = jnp.broadcast_to(pieces[g][j : j + 1], (GROUP, 128))
            for v in range(g, groups):
                pieces[v] = pieces[v] - factors[v - g] * top
        pivots.append(pivot)
    pivot = jnp.concatenate(pivots, axis=0)
    root = lax.rsqrt(pivot)
    root = root * (1.5 - 0.5 * ((pivot * root) * root))
    return jnp.concatenate(pieces, axis=0) * root


def factor(work, inverse):
    size = work.shape[0]
    wide = lax.broadcasted_iota(jnp.int32, (PANEL, size), 1)
    tall = lax.broadcasted_iota(jnp.int32, (PANEL, size), 0)
    lane = lax.broadcasted_iota(jnp.int32, (PANEL, 128), 1)
    zero = jnp.zeros((PANEL, size), BF16)
    for start in range(0, size, PANEL):
        rows = work[start : start + PANEL, :]
        tile = start // 128 * 128
        block = work[start : start + PANEL, tile : tile + 128]
        if start % 128:
            block = pltpu.roll(block, 128 - start % 128, axis=1)
        t_high, t_mid, t_low = split3(panel_inverse(block))
        first = jnp.where(lane < 2 * PANEL, t_high, jnp.where(lane < 3 * PANEL, t_mid, t_low))
        second = jnp.where(lane < 2 * PANEL, t_high, jnp.where(lane < 3 * PANEL, t_mid, t_high))
        left = jnp.concatenate([first, second], axis=1)
        spread = jnp.where(lax.rem(wide, 128) < PANEL, jnp.zeros_like(left[:, :1]), jnp.ones_like(left[:, :1]))
        left = left * spread[:, : left.shape[1]]
        inside = (wide >= start) & (wide < start + PANEL)
        rows = jnp.where(inside, jnp.where(wide - start == tall, 1.0, 0.0), rows)
        r_high, r_mid, r_low = split3(rows)
        right = jnp.concatenate([zero, r_high, r_high, r_high, zero, r_mid, r_mid, r_low], axis=0)
        new = jnp.dot(left, right, preferred_element_type=F32)
        inverse[start : start + PANEL, :] = jnp.where(wide < start + PANEL, new, 0.0)
        after = start + PANEL
        if after < size:
            high, middle, low = split3(new)
            base = after // 128 * 128
            lhs = jnp.concatenate([high, high, middle, middle, high, low], axis=0)[:, base:]
            rhs = jnp.concatenate([high, middle, high, middle, low, high], axis=0)
            change = lax.dot_general(lhs, rhs, TN, preferred_element_type=F32)[after - base :]
            columns = lax.broadcasted_iota(jnp.int32, change.shape, 1)
            old = work[after:, :]
            work[after:, :] = jnp.where((columns >= start) & (columns < after), 0.0, old) - change


def finish_kernel(chips, scale, ints, *refs):
    mine, theirs = refs[:chips], refs[chips : 2 * chips]
    y_mine, y_theirs = refs[2 * chips : 3 * chips + 1], refs[3 * chips + 1 : 4 * chips + 1]
    basis, reduced, pair, work, inverse = refs[4 * chips + 1 :]
    core, chip, col = ints[0], ints[1], ints[2]
    half, local_vecs, orbs = y_mine[0].shape
    vecs = CORES * local_vecs
    eye = lax.broadcasted_iota(jnp.int32, (vecs, vecs), 0) == lax.broadcasted_iota(
        jnp.int32, (vecs, vecs), 1
    )
    for step in range(chips):
        which = lax.rem(chip + step, chips)
        rows = pl.ds(pl.multiple_of(which * vecs, vecs), vecs)
        for matrix, payload in ((core, mine[step]), (1 - core, theirs[step])):
            diagonal = diagonal_of(payload)
            for k in range(chips):
                block = payload[k * vecs : (k + 1) * vecs, :].astype(F32)
                block = jnp.where(eye & (which == k), diagonal, block)
                pair[matrix, rows, k * vecs : (k + 1) * vecs] = block
    work[...] = (pair[0] + pair[0].T) * scale
    factor(work, inverse)
    start = pl.multiple_of(col * local_vecs, local_vecs)
    own_rows = inverse[pl.ds(start, local_vecs), :]
    gram_h = (pair[1] + pair[1].T) * scale
    half_way = lax.dot_general(
        gram_h, own_rows, NT, precision=lax.Precision.HIGHEST, preferred_element_type=F32
    )
    reduced[...] = jnp.dot(
        inverse[...], half_way, precision=lax.Precision.HIGHEST, preferred_element_type=F32
    )
    rotation = own_rows.astype(BF16)
    turned = []
    for step in range(chips):
        which = lax.rem(chip + step, chips)
        part = rotation[:, :vecs]
        for k in range(1, chips):
            part = jnp.where(which == k, rotation[:, k * vecs : (k + 1) * vecs], part)
        turned.append(part)
    turned = jnp.concatenate(turned, axis=1)
    mine_groups = [y_mine[0], y_mine[1]]
    for other in y_mine[2:]:
        mine_groups += [other.at[g] for g in range(CORES)]
    their_groups = [other.at[g] for other in y_theirs for g in range(CORES)]
    for which, group in ((core, mine_groups), (1 - core, their_groups)):
        for row in range(half):
            everything = jnp.concatenate([vectors[row] for vectors in group], axis=0)
            result = jnp.dot(turned, everything, preferred_element_type=F32).astype(BF16)
            at = pl.multiple_of((which * half + row) * orbs, orbs)
            basis[:, pl.ds(at, orbs)] = result


def local(
    trial_vectors,
    hamiltonian_blocks,
    correlation_offset,
    block_columns,
    block_phases,
    block_sizes,
    shift,
    halfwidth,
):
    blocks_dev, slots = block_columns.shape
    orbs = hamiltonian_blocks.shape[2]
    num_rows, num_cols = lax.axis_size("row"), lax.axis_size("col")
    total_blocks = blocks_dev * num_rows
    half = blocks_dev // CORES
    chips = num_cols // CORES
    local_vecs = trial_vectors.shape[0]
    vecs = local_vecs * CORES
    size = local_vecs * num_cols
    row, col = lax.axis_index("row"), lax.axis_index("col")
    core, chip = lax.rem(col, CORES), lax.div(col, CORES)

    def swap_cores(value):
        return lax.ppermute(value, "col", [(c, c ^ 1) for c in range(num_cols)])

    def swap_chips(value):
        pairs = []
        for r in range(num_rows):
            for x in range(chips):
                upper = r * num_cols + x * CORES + 1
                lower = (r + 1) % num_rows * num_cols + x * CORES
                pairs += [(upper, lower), (lower, upper)]
        return lax.ppermute(value, ("row", "col"), pairs)

    def from_chip(value, step):
        pairs = [((c + step * CORES) % num_cols, c) for c in range(num_cols)]
        return lax.ppermute(value, "col", pairs)

    state = jax.ShapeDtypeStruct((half, local_vecs, orbs), BF16)
    end = jax.ShapeDtypeStruct((HALF_BAND, local_vecs, orbs), BF16)
    ext = pltpu.VMEM((half + 2 * HALF_BAND, local_vecs, orbs), BF16)
    params = pltpu.CompilerParams(vmem_limit_bytes=16 << 20)
    row_flops = 2 * half * slots * local_vecs * orbs * orbs

    def call(kernel, name, scalars, arrays, outs, scratch, flops):
        return pl.pallas_call(
            kernel,
            name=name,
            out_shape=outs,
            in_specs=[SMEM] * len(scalars) + [VMEM] * len(arrays),
            out_specs=(VMEM,) * len(outs),
            scratch_shapes=scratch,
            compiler_params=params,
            cost_estimate=pl.CostEstimate(
                flops=flops, bytes_accessed=flops // 128, transcendentals=0
            ),
        )(*scalars, *arrays)

    def step_call(kernel, name, scalars, arrays, flops):
        return call(kernel, name, scalars, arrays, (state, end, end), [ext], flops)

    def exchange(ends):
        inter = swap_chips(ends[1])
        return swap_cores(ends[0]), inter

    def scalars(value):
        return pltpu.with_memory_space_constraint(value, pltpu.SMEM)

    ints = scalars(jnp.stack([core, chip, col, row * blocks_dev]).astype(jnp.int32))
    block_sizes, shift, halfwidth = (scalars(x) for x in (block_sizes, shift, halfwidth))
    block_columns, block_phases = scalars(block_columns), scalars(block_phases)
    own, give = call(
        cut_kernel, "cut", (ints, block_sizes), (trial_vectors,), (state, state), [], row_flops
    )
    got = swap_cores(give)
    matrix = vmem((half, *hamiltonian_blocks.shape[1:]), BF16)
    ham, ovl, index, signs = pl.pallas_call(
        functools.partial(load_kernel, total_blocks),
        name="load",
        out_shape=(
            matrix,
            matrix,
            pltpu.SMEM((half, slots), jnp.int32),
            pltpu.SMEM((half, slots), F32),
        ),
        in_specs=[SMEM, SMEM, SMEM, HBM, HBM],
        out_specs=(VMEM, VMEM, SMEM, SMEM),
        scratch_shapes=[pltpu.SemaphoreType.DMA((2, half))],
        compiler_params=params,
        cost_estimate=pl.CostEstimate(
            flops=0, bytes_accessed=4 * hamiltonian_blocks.size, transcendentals=0
        ),
    )(
        ints,
        block_columns,
        block_phases,
        pltpu.with_memory_space_constraint(hamiltonian_blocks, pltpu.HBM),
        pltpu.with_memory_space_constraint(correlation_offset, pltpu.HBM),
    )
    got, ham, ovl = lax.optimization_barrier((got, ham, ovl))
    current = [jnp.where(core == 0, own, got), jnp.where(core == 0, got, own)]
    spare = half - HALF_BAND
    ends = [
        (
            lax.dynamic_slice_in_dim(value, spare * (1 - core), HALF_BAND, 0),
            lax.dynamic_slice_in_dim(value, spare * core, HALF_BAND, 0),
        )
        for value in current
    ]
    table = (ints, index, signs)
    scaled, term, previous = [None] * CORES, [None] * CORES, list(current)
    halo = [exchange(ends[g]) for g in range(CORES)]
    for degree in range(DEGREE):
        for g in range(CORES):
            scaled[g], *ends = step_call(
                scaled_kernel,
                "scaled",
                (*table, shift, halfwidth),
                (current[g], *halo[g], ham, ovl),
                2 * row_flops,
            )
            halo[g] = exchange(ends)
        for g in range(CORES):
            term[g], *ends = step_call(
                term_kernel, "term", table, (scaled[g], *halo[g], ovl), row_flops
            )
            halo[g] = exchange(ends)
        for g in range(CORES):
            first = degree == 0
            arrays = (term[g], *halo[g], scaled[g]) + (() if first else (previous[g],)) + (ovl,)
            updated, *ends = step_call(
                functools.partial(update_kernel, first),
                "update",
                (*table, block_sizes),
                arrays,
                row_flops,
            )
            halo[g] = exchange(ends)
            previous[g], current[g] = current[g], updated

    stacked = jnp.stack(current)
    y_others = [from_chip(stacked, step) for step in range(1, chips)]
    image = jax.ShapeDtypeStruct((2, local_vecs, half * orbs), BF16)
    (ready,) = call(
        images_kernel,
        "images",
        table,
        (current[0], *halo[0], ham, ovl),
        (image,),
        [ext],
        2 * row_flops,
    )
    payload = jax.ShapeDtypeStruct((size + DIAGONAL_ROWS, vecs), BF16)
    keep, send = call(
        functools.partial(gram_kernel, chips),
        "gram",
        table,
        (current[1], *halo[1], ham, ovl, ready, current[0], *y_others),
        (payload, payload),
        [ext, pltpu.VMEM(image.shape, BF16), pltpu.VMEM((2, *payload.shape), BF16)],
        3 * row_flops,
    )

    def add(left, right):
        return call(add_kernel, "add", (), (left, right), (payload,), [], row_flops // 8)[0]

    summed = add(keep, swap_cores(send))
    if num_rows & (num_rows - 1):
        every = lax.all_gather(summed, "row")
        summed = every[0]
        for r in range(1, num_rows):
            summed = add(summed, every[r])
    else:
        bit = 1
        while bit < num_rows:
            other = lax.ppermute(summed, "row", [(r, r ^ bit) for r in range(num_rows)])
            summed = add(summed, other)
            bit *= 2
    mine = [summed] + [from_chip(summed, step) for step in range(1, chips)]
    theirs = [swap_cores(value) for value in mine]
    y_theirs = [swap_cores(value) for value in (stacked, *y_others)]
    return call(
        functools.partial(finish_kernel, chips, 0.5 / (total_blocks * orbs)),
        "finish",
        (ints,),
        (*mine, *theirs, *current, *y_others, *y_theirs),
        (
            jax.ShapeDtypeStruct((local_vecs, blocks_dev * orbs), BF16),
            jax.ShapeDtypeStruct((size, local_vecs), F32),
        ),
        [
            pltpu.VMEM((2, size, size), F32),
            pltpu.VMEM((size, size), F32),
            pltpu.VMEM((size, size), F32),
        ],
        10 * row_flops,
    )


def solution(mesh):
    return jax.shard_map(
        local,
        mesh=mesh,
        in_specs=(
            P("col", ("pool", "row")),
            P(("pool", "row"), None, None, None),
            P(("pool", "row"), None, None, None),
            P(("pool", "row"), None),
            P(("pool", "row"), None),
            P(("pool", "row")),
            P("pool"),
            P("pool"),
        ),
        out_specs=(P("col", ("pool", "row")), P("pool", "col")),
        check_vma=False,
    )
```

```python
import functools

import jax
import jax.numpy as jnp
from jax import lax
from jax.experimental import pallas as pl
from jax.experimental.pallas import tpu as pltpu
from jax.sharding import PartitionSpec as P

HALF_BAND = 5
DEGREE = 4
CORES = 2
PANEL = 64
SLOWER = 24
SUBLANES = 8
DIAGONAL_ROWS = 16

BF16 = jnp.bfloat16
F32 = jnp.float32
NT = (((1,), (1,)), ((), ()))
TN = (((0,), (0,)), ((), ()))

SMEM = pl.BlockSpec(memory_space=pltpu.SMEM)
VMEM = pl.BlockSpec(memory_space=pltpu.VMEM)
HBM = pl.BlockSpec(memory_space=pltpu.HBM)


def vmem(shape, dtype):
    return pltpu.VMEM(shape, dtype)


def fill_ext(core, own, intra, inter, ext):
    half = own.shape[0]
    ext[HALF_BAND : HALF_BAND + half] = own[...]
    ext[pl.ds((half + HALF_BAND) * (1 - core), HALF_BAND)] = intra[...]
    ext[pl.ds((half + HALF_BAND) * core, HALF_BAND)] = inter[...]


def picked(table, ext, row):
    index, signs = table
    slots = index.shape[1]
    return jnp.concatenate(
        [ext[index[row, s]] * signs[row, s].astype(BF16) for s in range(slots)], axis=1
    )


def row_matrix(blocks, row):
    return jnp.concatenate([blocks[row, s] for s in range(blocks.shape[1])], axis=1)


def send_ends(core, full, intra_out, inter_out):
    spare = full.shape[0] - HALF_BAND
    intra_out[...] = full[pl.ds(spare * (1 - core), HALF_BAND)]
    inter_out[...] = full[pl.ds(spare * core, HALF_BAND)]


def image_of(table, ext, matrices, row):
    matrix = jnp.concatenate([row_matrix(blocks, row) for blocks in matrices], axis=0)
    return lax.dot_general(matrix, picked(table, ext, row), NT, preferred_element_type=F32)


def both_rows(table, ext, ham, ovl, row):
    orbs = ham.shape[2]
    image = image_of(table, ext, (ham, ovl), row)
    return image[:orbs].T, image[orbs:].T


def one_row(table, ext, ovl, row):
    return image_of(table, ext, (ovl,), row).T


def cut_kernel(ints, sizes, trial, keep, give, sizes_here, trial_here, sems):
    copies = [
        pltpu.make_async_copy(sizes, sizes_here, sems.at[0]),
        pltpu.make_async_copy(trial, trial_here, sems.at[1]),
    ]
    for copy in copies:
        copy.start()
    for copy in copies:
        copy.wait()
    half, _, orbs = keep.shape
    core = ints[0]
    lane = lax.broadcasted_iota(jnp.int32, keep.shape[1:], 1)
    for out, which in ((give, 1 - core), (keep, core)):
        for row in range(half):
            at = which * half + row
            values = trial_here[:, pl.ds(pl.multiple_of(at * orbs, orbs), orbs)].astype(F32)
            out[row] = jnp.where(lane < sizes_here[at], values, 0.0).astype(BF16)


def load_kernel(total, ints, shift, width, columns, phases, sizes, ham, ovl, *rest):
    ham_out, ovl_out, index, signs, place, scal, columns_here, phases_here, sizes_here = rest[:9]
    sems, more_sems = rest[9:]
    half, slots = index.shape
    first = ints[0] * half
    small = [
        pltpu.make_async_copy(source, target, more_sems.at[i])
        for i, (source, target) in enumerate(
            ((columns, columns_here), (phases, phases_here), (sizes, sizes_here))
        )
    ]
    large = [
        pltpu.make_async_copy(source.at[first + row], target.at[row], sems.at[matrix, row])
        for row in range(half)
        for matrix, (source, target) in enumerate(((ham, ham_out), (ovl, ovl_out)))
    ]
    for copy in small + large:
        copy.start()
    scal[0] = shift[0]
    scal[1] = width[0]
    for i in range(3):
        place[i] = ints[i]
    for copy in small:
        copy.wait()
    start = ints[3] + first

    def fill(row, _):
        place[3 + row] = sizes_here[first + row]
        for slot in range(slots):
            away = columns_here[first + row, slot] - (start + row) + HALF_BAND
            away = jnp.where(away < 0, away + total, away)
            away = jnp.where(away >= total, away - total, away)
            index[row, slot] = row + away
            signs[row, slot] = (1 - 2 * phases_here[first + row, slot]).astype(F32)
        return 0

    lax.fori_loop(0, half, fill, 0)
    for copy in large:
        copy.wait()


def scaled_kernel(
    ints, index, signs, scal, own, inter, intra, ham, ovl, out, inter_out, intra_out, ext
):
    core = ints[0]
    fill_ext(core, own, intra, inter, ext)
    inv = 1.0 / (jnp.zeros(own.shape[1:], F32) + scal[1])
    for row in range(own.shape[0]):
        image_h, image_e = both_rows((index, signs), ext, ham, ovl, row)
        mine = own[row].astype(F32)
        out[row] = ((image_h - scal[0] * (mine + image_e)) * inv).astype(BF16)
    send_ends(core, out, intra_out, inter_out)


def term_kernel(ints, index, signs, own, inter, intra, ovl, out, inter_out, intra_out, ext):
    core = ints[0]
    fill_ext(core, own, intra, inter, ext)
    for row in range(own.shape[0]):
        out[row] = (-one_row((index, signs), ext, ovl, row)).astype(BF16)
    send_ends(core, out, intra_out, inter_out)


def update_kernel(first, ints, index, signs, own, inter, intra, scaled, *rest):
    if first:
        ovl, out, inter_out, intra_out, ext = rest
    else:
        previous, ovl, out, inter_out, intra_out, ext = rest
    core = ints[0]
    half = own.shape[0]
    fill_ext(core, own, intra, inter, ext)
    lane = lax.broadcasted_iota(jnp.int32, own.shape[1:], 1)
    for row in range(half):
        image = one_row((index, signs), ext, ovl, row)
        filtered = scaled[row].astype(F32) + own[row].astype(F32) - image
        if not first:
            filtered = 2.0 * filtered - previous[row].astype(F32)
        out[row] = jnp.where(lane < ints[3 + row], filtered, 0.0).astype(BF16)
    send_ends(core, out, intra_out, inter_out)


def images_kernel(ints, index, signs, own, inter, intra, ham, ovl, out, ext):
    core = ints[0]
    fill_ext(core, own, intra, inter, ext)
    half, _, orbs = own.shape
    for row in range(half):
        image_h, image_e = both_rows((index, signs), ext, ham, ovl, row)
        at = slice(row * orbs, (row + 1) * orbs)
        out[0, :, at] = (own[row].astype(F32) + image_e).astype(BF16)
        out[1, :, at] = image_h.astype(BF16)


def gram_kernel(chips, ints, index, signs, own, inter, intra, ham, ovl, ready, *rest):
    first, *others = rest[:chips]
    keep, send, ext, images, both = rest[chips:]
    images_kernel(ints, index, signs, own, inter, intra, ham, ovl, images, ext)
    core, chip = ints[0], ints[1]
    half, local_vecs, _ = own.shape
    vecs = CORES * local_vecs
    groups = [[first[row] for row in range(half)], [own[row] for row in range(half)]]
    for other in others:
        groups += [[other[g, row] for row in range(half)] for g in range(CORES)]
    flat = jnp.concatenate([jnp.concatenate(group, axis=1) for group in groups], axis=0)
    eye = lax.broadcasted_iota(jnp.int32, (vecs, vecs), 0) == lax.broadcasted_iota(
        jnp.int32, (vecs, vecs), 1
    )
    for matrix in range(2):
        mine = jnp.concatenate([ready[matrix], images[matrix]], axis=0)
        pair = lax.dot_general(mine, flat, NT, preferred_element_type=F32)
        for step in range(chips):
            where = pl.multiple_of(lax.rem(chip + step, chips) * vecs, vecs)
            block = pair[:, step * vecs : (step + 1) * vecs]
            both[matrix, pl.ds(where, vecs), :] = block.astype(BF16)
        diagonal = jnp.sum(jnp.where(eye, pair[:, :vecs], 0.0), axis=0, keepdims=True)
        both[matrix, chips * vecs :, :] = diagonal_parts(diagonal)
    keep[...] = both[core]
    send[...] = both[1 - core]


def diagonal_parts(diagonal):
    high, middle, low = (part.astype(F32) for part in split3(diagonal))
    rows = lax.broadcasted_iota(jnp.int32, (DIAGONAL_ROWS, diagonal.shape[1]), 0)
    parts = jnp.where(rows == 0, high, jnp.where(rows == 1, middle, jnp.where(rows == 2, low, 0.0)))
    return parts.astype(BF16)


def diagonal_of(payload):
    parts = payload[payload.shape[0] - DIAGONAL_ROWS :, :].astype(F32)
    return parts[0:1] + (parts[1:2] + parts[2:3])


def add_kernel(left, right, out):
    body = left.shape[0] - DIAGONAL_ROWS
    out[:body] = (left[:body, :].astype(F32) + right[:body, :].astype(F32)).astype(BF16)
    out[body:] = diagonal_parts(diagonal_of(left) + diagonal_of(right))


def split3(value):
    high = value.astype(BF16)
    rest = value - high.astype(F32)
    middle = rest.astype(BF16)
    low = (rest - middle.astype(F32)).astype(BF16)
    return high, middle, low


def reciprocal(value):
    guess = pl.reciprocal(value, approx=True)
    return guess * (2.0 - value * guess)


def panel_inverse(block):
    lane = lax.broadcasted_iota(jnp.int32, (PANEL, 128), 1)
    rows = lax.broadcasted_iota(jnp.int32, (PANEL, 128), 0)
    work = jnp.where(lane < PANEL, block, jnp.where(lax.rem(lane, PANEL) == rows, 1.0, 0.0))
    count = PANEL // SUBLANES
    pieces = [work[v * SUBLANES : (v + 1) * SUBLANES] for v in range(count)]
    sub = lax.broadcasted_iota(jnp.int32, (SUBLANES, 128), 0)

    def spread(value, k):
        return jnp.broadcast_to(value[k % SUBLANES : k % SUBLANES + 1], (SUBLANES, 128))

    pivots = [jnp.ones((SUBLANES, 128), F32) for _ in range(count)]
    for start, group in ((0, 8), (8, 8), (16, 8), (24, 8), (32, 16), (48, 16)):
        columns = {
            k: {
                v: jnp.broadcast_to(pieces[v][:, k : k + 1], (SUBLANES, 128))
                for v in range(start // SUBLANES, count)
            }
            for k in range(start, start + group)
        }
        at = spread(columns[start][start // SUBLANES], start)
        for k in range(start, start + group):
            here = k // SUBLANES
            pivots[here] = jnp.where(sub == k % SUBLANES, at, pivots[here])
            inv = reciprocal(at)
            if k + 1 < start + group:
                below = (k + 1) // SUBLANES
                product = spread(columns[k][below], k + 1) * spread(columns[k + 1][here], k)
                at = spread(columns[k + 1][below], k + 1) - product * inv
            factors = {v: columns[k][v] * inv for v in range(here, count)}
            factors[here] = jnp.where(sub > k % SUBLANES, factors[here], 0.0)
            for later in range(k + 1, start + group):
                top = spread(columns[later][here], k)
                for v in range(here, count):
                    columns[later][v] = columns[later][v] - factors[v] * top
            top = spread(pieces[here], k)
            for v in range(here, count):
                pieces[v] = pieces[v] - factors[v] * top
    pivot = jnp.concatenate(pivots, axis=0)
    root = lax.rsqrt(pivot)
    root = root * (1.5 - 0.5 * ((pivot * root) * root))
    return jnp.concatenate(pieces, axis=0) * root


def factor(work, inverse):
    size = work.shape[0]
    wide = lax.broadcasted_iota(jnp.int32, (PANEL, size), 1)
    tall = lax.broadcasted_iota(jnp.int32, (PANEL, size), 0)
    lane = lax.broadcasted_iota(jnp.int32, (PANEL, 128), 1)
    zero = jnp.zeros((PANEL, size), BF16)
    for start in range(0, size, PANEL):
        rows = work[start : start + PANEL, :]
        tile = start // 128 * 128
        block = work[start : start + PANEL, tile : tile + 128]
        if start % 128:
            block = pltpu.roll(block, 128 - start % 128, axis=1)
        t_high, t_mid, t_low = split3(jnp.where(lane < PANEL, 0.0, panel_inverse(block)))
        left = jnp.concatenate([t_high, t_mid, t_low, t_high, t_mid, t_high], axis=1)
        inside = (wide >= start) & (wide < start + PANEL)
        rows = jnp.where(inside, jnp.where(wide - start == tall, 1.0, 0.0), rows)
        r_high, r_mid, r_low = split3(rows)
        right = [part for r in (r_high, r_high, r_high, r_mid, r_mid, r_low) for part in (zero, r)]
        right = jnp.concatenate(right, axis=0)
        new = jnp.dot(left, right, preferred_element_type=F32)
        inverse[start : start + PANEL, :] = jnp.where(wide < start + PANEL, new, 0.0)
        after = start + PANEL
        if after < size:
            high, middle, low = split3(new)
            base = after // 128 * 128
            lhs = jnp.concatenate([high, high, middle, middle, high, low], axis=0)[:, base:]
            rhs = jnp.concatenate([high, middle, high, middle, low, high], axis=0)
            change = lax.dot_general(lhs, rhs, TN, preferred_element_type=F32)[after - base :]
            columns = lax.broadcasted_iota(jnp.int32, change.shape, 1)
            old = work[after:, :]
            work[after:, :] = jnp.where((columns >= start) & (columns < after), 0.0, old) - change


def finish_kernel(chips, scale, ints, *refs):
    mine, theirs = refs[:chips], refs[chips : 2 * chips]
    y_mine, y_theirs = refs[2 * chips : 3 * chips + 1], refs[3 * chips + 1 : 4 * chips + 1]
    basis, reduced, pair, work, inverse = refs[4 * chips + 1 :]
    core, chip, col = ints[0], ints[1], ints[2]
    half, local_vecs, orbs = y_mine[0].shape
    vecs = CORES * local_vecs
    eye = lax.broadcasted_iota(jnp.int32, (vecs, vecs), 0) == lax.broadcasted_iota(
        jnp.int32, (vecs, vecs), 1
    )
    for step in range(chips):
        which = lax.rem(chip + step, chips)
        rows = pl.ds(pl.multiple_of(which * vecs, vecs), vecs)
        for matrix, payload in ((core, mine[step]), (1 - core, theirs[step])):
            diagonal = diagonal_of(payload)
            for k in range(chips):
                block = payload[k * vecs : (k + 1) * vecs, :].astype(F32)
                block = jnp.where(eye & (which == k), diagonal, block)
                pair[matrix, rows, k * vecs : (k + 1) * vecs] = block
    work[...] = (pair[0] + pair[0].T) * scale
    factor(work, inverse)
    start = pl.multiple_of(col * local_vecs, local_vecs)
    own_rows = inverse[pl.ds(start, local_vecs), :]
    gram_h = (pair[1] + pair[1].T) * scale
    half_way = jnp.dot(
        own_rows, gram_h, precision=lax.Precision.HIGHEST, preferred_element_type=F32
    )
    reduced[...] = lax.dot_general(
        half_way, inverse[...], NT, precision=lax.Precision.HIGHEST, preferred_element_type=F32
    )
    rotation = own_rows.astype(BF16)
    turned = []
    for step in range(chips):
        which = lax.rem(chip + step, chips)
        part = rotation[:, :vecs]
        for k in range(1, chips):
            part = jnp.where(which == k, rotation[:, k * vecs : (k + 1) * vecs], part)
        turned.append(part)
    turned = jnp.concatenate(turned, axis=1)
    mine_groups = [y_mine[0], y_mine[1]]
    for other in y_mine[2:]:
        mine_groups += [other.at[g] for g in range(CORES)]
    their_groups = [other.at[g] for other in y_theirs for g in range(CORES)]
    for which, group in ((core, mine_groups), (1 - core, their_groups)):
        for row in range(half):
            everything = jnp.concatenate([vectors[row] for vectors in group], axis=0)
            result = jnp.dot(turned, everything, preferred_element_type=F32).astype(BF16)
            at = pl.multiple_of((which * half + row) * orbs, orbs)
            basis[:, pl.ds(at, orbs)] = result


def local(
    trial_vectors,
    hamiltonian_blocks,
    correlation_offset,
    block_columns,
    block_phases,
    block_sizes,
    shift,
    halfwidth,
):
    blocks_dev, slots = block_columns.shape
    orbs = hamiltonian_blocks.shape[2]
    num_rows, num_cols = lax.axis_size("row"), lax.axis_size("col")
    total_blocks = blocks_dev * num_rows
    half = blocks_dev // CORES
    chips = num_cols // CORES
    local_vecs = trial_vectors.shape[0]
    vecs = local_vecs * CORES
    size = local_vecs * num_cols
    row, col = lax.axis_index("row"), lax.axis_index("col")
    core, chip = lax.rem(col, CORES), lax.div(col, CORES)

    def swap_cores(value):
        return lax.ppermute(value, "col", [(c, c ^ 1) for c in range(num_cols)])

    def swap_chips(value):
        pairs = []
        for r in range(num_rows):
            for x in range(chips):
                upper = r * num_cols + x * CORES + 1
                lower = (r + 1) % num_rows * num_cols + x * CORES
                pairs += [(upper, lower), (lower, upper)]
        return lax.ppermute(value, ("row", "col"), pairs)

    def from_chip(value, step):
        pairs = [((c + step * CORES) % num_cols, c) for c in range(num_cols)]
        return lax.ppermute(value, "col", pairs)

    state = jax.ShapeDtypeStruct((half, local_vecs, orbs), BF16)
    end = jax.ShapeDtypeStruct((HALF_BAND, local_vecs, orbs), BF16)
    ext = pltpu.VMEM((half + 2 * HALF_BAND, local_vecs, orbs), BF16)
    params = pltpu.CompilerParams(vmem_limit_bytes=16 << 20)
    row_flops = SLOWER * 2 * half * slots * local_vecs * orbs * orbs

    def call(kernel, name, scalars, arrays, outs, scratch, flops):
        return pl.pallas_call(
            kernel,
            name=name,
            out_shape=outs,
            in_specs=[SMEM] * len(scalars) + [VMEM] * len(arrays),
            out_specs=(VMEM,) * len(outs),
            scratch_shapes=scratch,
            compiler_params=params,
            cost_estimate=pl.CostEstimate(
                flops=flops, bytes_accessed=flops // 128, transcendentals=0
            ),
        )(*scalars, *arrays)

    def step_call(kernel, name, scalars, arrays, flops):
        return call(kernel, name, scalars, arrays, (state, end, end), [ext], flops)

    def exchange(ends):
        return swap_chips(ends[0]), swap_cores(ends[1])

    def scalars(value):
        return pltpu.with_memory_space_constraint(value, pltpu.SMEM)

    ints = scalars(jnp.stack([core, chip, col, row * blocks_dev]).astype(jnp.int32))
    shift, halfwidth = scalars(shift), scalars(halfwidth)

    def stays(value):
        return pltpu.with_memory_space_constraint(value, pltpu.HBM)

    own, give = pl.pallas_call(
        cut_kernel,
        name="cut",
        out_shape=(state, state),
        in_specs=[SMEM, HBM, HBM],
        out_specs=(VMEM, VMEM),
        scratch_shapes=[
            pltpu.SMEM(block_sizes.shape, jnp.int32),
            pltpu.VMEM(trial_vectors.shape, BF16),
            pltpu.SemaphoreType.DMA((2,)),
        ],
        compiler_params=params,
    )(ints, stays(block_sizes), stays(trial_vectors))
    got = swap_cores(give)
    matrix = vmem((half, *hamiltonian_blocks.shape[1:]), BF16)
    ham, ovl, index, signs, place, scal = pl.pallas_call(
        functools.partial(load_kernel, total_blocks),
        name="load",
        out_shape=(
            matrix,
            matrix,
            pltpu.SMEM((half, slots), jnp.int32),
            pltpu.SMEM((half, slots), F32),
            pltpu.SMEM((3 + half,), jnp.int32),
            pltpu.SMEM((2,), F32),
        ),
        in_specs=[SMEM] * 3 + [HBM] * 5,
        out_specs=(VMEM, VMEM, SMEM, SMEM, SMEM, SMEM),
        scratch_shapes=[
            pltpu.SMEM(block_columns.shape, jnp.int32),
            pltpu.SMEM(block_phases.shape, jnp.int32),
            pltpu.SMEM(block_sizes.shape, jnp.int32),
            pltpu.SemaphoreType.DMA((2, half)),
            pltpu.SemaphoreType.DMA((3,)),
        ],
        compiler_params=params,
        cost_estimate=pl.CostEstimate(
            flops=0, bytes_accessed=4 * hamiltonian_blocks.size, transcendentals=0
        ),
    )(
        ints,
        shift,
        halfwidth,
        stays(block_columns),
        stays(block_phases),
        stays(block_sizes),
        stays(hamiltonian_blocks),
        stays(correlation_offset),
    )
    current = [jnp.where(core == 0, own, got), jnp.where(core == 0, got, own)]
    spare = half - HALF_BAND
    ends = [
        (
            lax.dynamic_slice_in_dim(value, spare * core, HALF_BAND, 0),
            lax.dynamic_slice_in_dim(value, spare * (1 - core), HALF_BAND, 0),
        )
        for value in current
    ]
    table = (place, index, signs)
    scaled, term, previous = [None] * CORES, [None] * CORES, list(current)
    halo = [exchange(ends[g]) for g in range(CORES)]
    for degree in range(DEGREE):
        for g in range(CORES):
            scaled[g], *ends = step_call(
                scaled_kernel,
                "scaled",
                (*table, scal),
                (current[g], *halo[g], ham, ovl),
                2 * row_flops,
            )
            halo[g] = exchange(ends)
        for g in range(CORES):
            term[g], *ends = step_call(
                term_kernel, "term", table, (scaled[g], *halo[g], ovl), row_flops
            )
            halo[g] = exchange(ends)
        for g in range(CORES):
            first = degree == 0
            arrays = (term[g], *halo[g], scaled[g]) + (() if first else (previous[g],)) + (ovl,)
            updated, *ends = step_call(
                functools.partial(update_kernel, first),
                "update",
                table,
                arrays,
                row_flops,
            )
            halo[g] = exchange(ends)
            previous[g], current[g] = current[g], updated

    stacked = jnp.stack(current)
    y_others = [from_chip(stacked, step) for step in range(1, chips)]
    image = jax.ShapeDtypeStruct((2, local_vecs, half * orbs), BF16)
    (ready,) = call(
        images_kernel,
        "images",
        table,
        (current[0], *halo[0], ham, ovl),
        (image,),
        [ext],
        2 * row_flops,
    )
    payload = jax.ShapeDtypeStruct((size + DIAGONAL_ROWS, vecs), BF16)
    keep, send = call(
        functools.partial(gram_kernel, chips),
        "gram",
        table,
        (current[1], *halo[1], ham, ovl, ready, current[0], *y_others),
        (payload, payload),
        [ext, pltpu.VMEM(image.shape, BF16), pltpu.VMEM((2, *payload.shape), BF16)],
        3 * row_flops,
    )

    def add(left, right):
        return call(add_kernel, "add", (), (left, right), (payload,), [], row_flops // 8)[0]

    summed = add(keep, swap_cores(send))
    if num_rows & (num_rows - 1):
        every = lax.all_gather(summed, "row")
        summed = every[0]
        for r in range(1, num_rows):
            summed = add(summed, every[r])
    else:
        bit = 1
        while bit < num_rows:
            other = lax.ppermute(summed, "row", [(r, r ^ bit) for r in range(num_rows)])
            summed = add(summed, other)
            bit *= 2
    mine = [summed] + [from_chip(summed, step) for step in range(1, chips)]
    theirs = [swap_cores(value) for value in mine]
    y_theirs = [swap_cores(value) for value in (stacked, *y_others)]
    basis, reduced = call(
        functools.partial(finish_kernel, chips, 0.5 / (total_blocks * orbs)),
        "finish",
        (place,),
        (*mine, *theirs, *current, *y_others, *y_theirs),
        (
            jax.ShapeDtypeStruct((local_vecs, blocks_dev * orbs), BF16),
            jax.ShapeDtypeStruct((local_vecs, size), F32),
        ),
        [
            pltpu.VMEM((2, size, size), F32),
            pltpu.VMEM((size, size), F32),
            pltpu.VMEM((size, size), F32),
        ],
        10 * row_flops,
    )
    return basis, reduced.T


def solution(mesh):
    return jax.shard_map(
        local,
        mesh=mesh,
        in_specs=(
            P("col", ("pool", "row")),
            P(("pool", "row"), None, None, None),
            P(("pool", "row"), None, None, None),
            P(("pool", "row"), None),
            P(("pool", "row"), None),
            P(("pool", "row")),
            P("pool"),
            P("pool"),
        ),
        out_specs=(P("col", ("pool", "row")), P("pool", "col")),
        check_vma=False,
    )
```

```python
import functools

import jax
import jax.numpy as jnp
from jax import lax
from jax.experimental import pallas as pl
from jax.experimental.pallas import tpu as pltpu
from jax.sharding import PartitionSpec as P

HALF_BAND = 5
DEGREE = 4
CORES = 2
PANEL = 32
SLOWER = 24
SUBLANES = 8
DIAGONAL_ROWS = 16

BF16 = jnp.bfloat16
F32 = jnp.float32
NT = (((1,), (1,)), ((), ()))
TN = (((0,), (0,)), ((), ()))

SMEM = pl.BlockSpec(memory_space=pltpu.SMEM)
VMEM = pl.BlockSpec(memory_space=pltpu.VMEM)
HBM = pl.BlockSpec(memory_space=pltpu.HBM)


def vmem(shape, dtype):
    return pltpu.VMEM(shape, dtype)


def fill_ext(core, own, intra, inter, ext):
    half = own.shape[0]
    ext[HALF_BAND : HALF_BAND + half] = own[...]
    ext[pl.ds((half + HALF_BAND) * (1 - core), HALF_BAND)] = intra[...]
    ext[pl.ds((half + HALF_BAND) * core, HALF_BAND)] = inter[...]


def picked(table, ext, row):
    index, signs = table
    slots = index.shape[1]
    return jnp.concatenate(
        [ext[index[row, s]] * signs[row, s].astype(BF16) for s in range(slots)], axis=1
    )


def row_matrix(blocks, row):
    return jnp.concatenate([blocks[row, s] for s in range(blocks.shape[1])], axis=1)


def send_ends(core, full, intra_out, inter_out):
    spare = full.shape[0] - HALF_BAND
    intra_out[...] = full[pl.ds(spare * (1 - core), HALF_BAND)]
    inter_out[...] = full[pl.ds(spare * core, HALF_BAND)]


def image_of(table, ext, matrices, row):
    matrix = jnp.concatenate([row_matrix(blocks, row) for blocks in matrices], axis=0)
    return lax.dot_general(matrix, picked(table, ext, row), NT, preferred_element_type=F32)


def both_rows(table, ext, ham, ovl, row):
    orbs = ham.shape[2]
    image = image_of(table, ext, (ham, ovl), row)
    return image[:orbs].T, image[orbs:].T


def one_row(table, ext, ovl, row):
    return image_of(table, ext, (ovl,), row).T


def cut_kernel(ints, sizes, trial, keep, give, sizes_here, trial_here, sems):
    copies = [
        pltpu.make_async_copy(sizes, sizes_here, sems.at[0]),
        pltpu.make_async_copy(trial, trial_here, sems.at[1]),
    ]
    for copy in copies:
        copy.start()
    for copy in copies:
        copy.wait()
    half, _, orbs = keep.shape
    core = ints[0]
    lane = lax.broadcasted_iota(jnp.int32, keep.shape[1:], 1)
    for out, which in ((give, 1 - core), (keep, core)):
        for row in range(half):
            at = which * half + row
            values = trial_here[:, pl.ds(pl.multiple_of(at * orbs, orbs), orbs)].astype(F32)
            out[row] = jnp.where(lane < sizes_here[at], values, 0.0).astype(BF16)


def load_kernel(total, ints, shift, width, columns, phases, sizes, ham, ovl, *rest):
    ham_out, ovl_out, index, signs, place, scal, columns_here, phases_here, sizes_here = rest[:9]
    sems, more_sems = rest[9:]
    half, slots = index.shape
    first = ints[0] * half
    small = [
        pltpu.make_async_copy(source, target, more_sems.at[i])
        for i, (source, target) in enumerate(
            ((columns, columns_here), (phases, phases_here), (sizes, sizes_here))
        )
    ]
    large = [
        pltpu.make_async_copy(source.at[first + row], target.at[row], sems.at[matrix, row])
        for row in range(half)
        for matrix, (source, target) in enumerate(((ham, ham_out), (ovl, ovl_out)))
    ]
    for copy in small + large:
        copy.start()
    scal[0] = shift[0]
    scal[1] = width[0]
    for i in range(3):
        place[i] = ints[i]
    for copy in small:
        copy.wait()
    start = ints[3] + first

    def fill(row, _):
        place[3 + row] = sizes_here[first + row]
        for slot in range(slots):
            away = columns_here[first + row, slot] - (start + row) + HALF_BAND
            away = jnp.where(away < 0, away + total, away)
            away = jnp.where(away >= total, away - total, away)
            index[row, slot] = row + away
            signs[row, slot] = (1 - 2 * phases_here[first + row, slot]).astype(F32)
        return 0

    lax.fori_loop(0, half, fill, 0)
    for copy in large:
        copy.wait()


def scaled_kernel(
    ints, index, signs, scal, own, inter, intra, ham, ovl, out, inter_out, intra_out, ext
):
    core = ints[0]
    fill_ext(core, own, intra, inter, ext)
    inv = 1.0 / (jnp.zeros(own.shape[1:], F32) + scal[1])
    for row in range(own.shape[0]):
        image_h, image_e = both_rows((index, signs), ext, ham, ovl, row)
        mine = own[row].astype(F32)
        out[row] = ((image_h - scal[0] * (mine + image_e)) * inv).astype(BF16)
    send_ends(core, out, intra_out, inter_out)


def term_kernel(ints, index, signs, own, inter, intra, ovl, out, inter_out, intra_out, ext):
    core = ints[0]
    fill_ext(core, own, intra, inter, ext)
    for row in range(own.shape[0]):
        out[row] = (-one_row((index, signs), ext, ovl, row)).astype(BF16)
    send_ends(core, out, intra_out, inter_out)


def update_kernel(first, ints, index, signs, own, inter, intra, scaled, *rest):
    if first:
        ovl, out, inter_out, intra_out, ext = rest
    else:
        previous, ovl, out, inter_out, intra_out, ext = rest
    core = ints[0]
    half = own.shape[0]
    fill_ext(core, own, intra, inter, ext)
    lane = lax.broadcasted_iota(jnp.int32, own.shape[1:], 1)
    for row in range(half):
        image = one_row((index, signs), ext, ovl, row)
        filtered = scaled[row].astype(F32) + own[row].astype(F32) - image
        if not first:
            filtered = 2.0 * filtered - previous[row].astype(F32)
        out[row] = jnp.where(lane < ints[3 + row], filtered, 0.0).astype(BF16)
    send_ends(core, out, intra_out, inter_out)


def images_kernel(ints, index, signs, own, inter, intra, ham, ovl, out, ext):
    core = ints[0]
    fill_ext(core, own, intra, inter, ext)
    half, _, orbs = own.shape
    for row in range(half):
        image_h, image_e = both_rows((index, signs), ext, ham, ovl, row)
        at = slice(row * orbs, (row + 1) * orbs)
        out[0, :, at] = (own[row].astype(F32) + image_e).astype(BF16)
        out[1, :, at] = image_h.astype(BF16)


def gram_kernel(chips, ints, index, signs, own, inter, intra, ham, ovl, ready, *rest):
    count = CORES * chips - 1
    first, *others = rest[:count]
    keep, send, ext, images, both = rest[count:]
    images_kernel(ints, index, signs, own, inter, intra, ham, ovl, images, ext)
    core, chip = ints[0], ints[1]
    half, local_vecs, _ = own.shape
    vecs = CORES * local_vecs
    groups = [[first[row] for row in range(half)], [own[row] for row in range(half)]]
    groups += [[other[row] for row in range(half)] for other in others]
    flat = jnp.concatenate([jnp.concatenate(group, axis=1) for group in groups], axis=0)
    eye = lax.broadcasted_iota(jnp.int32, (vecs, vecs), 0) == lax.broadcasted_iota(
        jnp.int32, (vecs, vecs), 1
    )
    for matrix in range(2):
        mine = jnp.concatenate([ready[matrix], images[matrix]], axis=0)
        pair = lax.dot_general(mine, flat, NT, preferred_element_type=F32)
        for step in range(chips):
            where = pl.multiple_of(lax.rem(chip + step, chips) * vecs, vecs)
            block = pair[:, step * vecs : (step + 1) * vecs]
            both[matrix, pl.ds(where, vecs), :] = block.astype(BF16)
        diagonal = jnp.sum(jnp.where(eye, pair[:, :vecs], 0.0), axis=0, keepdims=True)
        both[matrix, chips * vecs :, :] = diagonal_parts(diagonal)
    keep[...] = both[core]
    send[...] = both[1 - core]


def diagonal_parts(diagonal):
    high, middle, low = (part.astype(F32) for part in split3(diagonal))
    rows = lax.broadcasted_iota(jnp.int32, (DIAGONAL_ROWS, diagonal.shape[1]), 0)
    parts = jnp.where(rows == 0, high, jnp.where(rows == 1, middle, jnp.where(rows == 2, low, 0.0)))
    return parts.astype(BF16)


def diagonal_of(payload):
    parts = payload[payload.shape[0] - DIAGONAL_ROWS :, :].astype(F32)
    return parts[0:1] + (parts[1:2] + parts[2:3])


def add_kernel(left, right, out):
    body = left.shape[0] - DIAGONAL_ROWS
    out[:body] = (left[:body, :].astype(F32) + right[:body, :].astype(F32)).astype(BF16)
    out[body:] = diagonal_parts(diagonal_of(left) + diagonal_of(right))


def split3(value):
    high = value.astype(BF16)
    rest = value - high.astype(F32)
    middle = rest.astype(BF16)
    low = (rest - middle.astype(F32)).astype(BF16)
    return high, middle, low


def reciprocal(value):
    guess = pl.reciprocal(value, approx=True)
    return guess * (2.0 - value * guess)


def panel_inverse(block):
    lane = lax.broadcasted_iota(jnp.int32, (PANEL, 128), 1)
    rows = lax.broadcasted_iota(jnp.int32, (PANEL, 128), 0)
    work = jnp.where(lane < PANEL, block, jnp.where(lax.rem(lane, PANEL) == rows, 1.0, 0.0))
    count = PANEL // SUBLANES
    pieces = [work[v * SUBLANES : (v + 1) * SUBLANES] for v in range(count)]
    sub = lax.broadcasted_iota(jnp.int32, (SUBLANES, 128), 0)

    def spread(value, k):
        return jnp.broadcast_to(value[k % SUBLANES : k % SUBLANES + 1], (SUBLANES, 128))

    pivots = [jnp.ones((SUBLANES, 128), F32) for _ in range(count)]
    for start, group in ((0, 16), (16, 16)):
        columns = {
            k: {
                v: jnp.broadcast_to(pieces[v][:, k : k + 1], (SUBLANES, 128))
                for v in range(start // SUBLANES, count)
            }
            for k in range(start, start + group)
        }
        at = spread(columns[start][start // SUBLANES], start)
        for k in range(start, start + group):
            here = k // SUBLANES
            pivots[here] = jnp.where(sub == k % SUBLANES, at, pivots[here])
            inv = reciprocal(at)
            if k + 1 < start + group:
                below = (k + 1) // SUBLANES
                product = spread(columns[k][below], k + 1) * spread(columns[k + 1][here], k)
                at = spread(columns[k + 1][below], k + 1) - product * inv
            factors = {v: columns[k][v] * inv for v in range(here, count)}
            factors[here] = jnp.where(sub > k % SUBLANES, factors[here], 0.0)
            for later in range(k + 1, start + group):
                top = spread(columns[later][here], k)
                for v in range(here, count):
                    columns[later][v] = columns[later][v] - factors[v] * top
            top = spread(pieces[here], k)
            for v in range(here, count):
                pieces[v] = pieces[v] - factors[v] * top
    pivot = jnp.concatenate(pivots, axis=0)
    root = lax.rsqrt(pivot)
    root = root * (1.5 - 0.5 * ((pivot * root) * root))
    return jnp.concatenate(pieces, axis=0) * root


def factor(work, inverse):
    size = work.shape[0]
    wide = lax.broadcasted_iota(jnp.int32, (PANEL, size), 1)
    tall = lax.broadcasted_iota(jnp.int32, (PANEL, size), 0)
    lane = lax.broadcasted_iota(jnp.int32, (PANEL, 128), 1)
    zero = jnp.zeros((PANEL, size), BF16)
    for start in range(0, size, PANEL):
        rows = work[start : start + PANEL, :]
        tile = start // 128 * 128
        block = work[start : start + PANEL, tile : tile + 128]
        if start % 128:
            block = pltpu.roll(block, 128 - start % 128, axis=1)
        t_high, t_mid, t_low = split3(jnp.where(lane < PANEL, 0.0, panel_inverse(block)))
        first = jnp.where(lane < 2 * PANEL, t_high, jnp.where(lane < 3 * PANEL, t_mid, t_low))
        second = jnp.where(lane < 2 * PANEL, t_high, jnp.where(lane < 3 * PANEL, t_mid, t_high))
        left = jnp.concatenate([first, second], axis=1)
        inside = (wide >= start) & (wide < start + PANEL)
        rows = jnp.where(inside, jnp.where(wide - start == tall, 1.0, 0.0), rows)
        r_high, r_mid, r_low = split3(rows)
        right = jnp.concatenate([zero, r_high, r_high, r_high, zero, r_mid, r_mid, r_low], axis=0)
        new = jnp.dot(left, right, preferred_element_type=F32)
        inverse[start : start + PANEL, :] = jnp.where(wide < start + PANEL, new, 0.0)
        after = start + PANEL
        if after < size:
            high, middle, low = split3(new)
            base = after // 128 * 128
            lhs = jnp.concatenate([high, high, middle, middle, high, low], axis=0)[:, base:]
            rhs = jnp.concatenate([high, middle, high, middle, low, high], axis=0)
            change = lax.dot_general(lhs, rhs, TN, preferred_element_type=F32)[after - base :]
            columns = lax.broadcasted_iota(jnp.int32, change.shape, 1)
            old = work[after:, :]
            work[after:, :] = jnp.where((columns >= start) & (columns < after), 0.0, old) - change


def finish_kernel(chips, scale, ints, *refs):
    mine, theirs = refs[:chips], refs[chips : 2 * chips]
    y_mine = refs[2 * chips : (2 + CORES) * chips]
    y_theirs = refs[(2 + CORES) * chips : (2 + 2 * CORES) * chips]
    basis, reduced, pair, work, inverse = refs[(2 + 2 * CORES) * chips :]
    core, chip, col = ints[0], ints[1], ints[2]
    half, local_vecs, orbs = y_mine[0].shape
    vecs = CORES * local_vecs
    eye = lax.broadcasted_iota(jnp.int32, (vecs, vecs), 0) == lax.broadcasted_iota(
        jnp.int32, (vecs, vecs), 1
    )
    for step in range(chips):
        which = lax.rem(chip + step, chips)
        rows = pl.ds(pl.multiple_of(which * vecs, vecs), vecs)
        for matrix, payload in ((core, mine[step]), (1 - core, theirs[step])):
            diagonal = diagonal_of(payload)
            for k in range(chips):
                block = payload[k * vecs : (k + 1) * vecs, :].astype(F32)
                block = jnp.where(eye & (which == k), diagonal, block)
                pair[matrix, rows, k * vecs : (k + 1) * vecs] = block
    work[...] = (pair[0] + pair[0].T) * scale
    factor(work, inverse)
    start = pl.multiple_of(col * local_vecs, local_vecs)
    own_rows = inverse[pl.ds(start, local_vecs), :]
    gram_h = (pair[1] + pair[1].T) * scale
    half_way = jnp.dot(
        own_rows, gram_h, precision=lax.Precision.HIGHEST, preferred_element_type=F32
    )
    reduced[...] = lax.dot_general(
        half_way, inverse[...], NT, precision=lax.Precision.HIGHEST, preferred_element_type=F32
    )
    rotation = own_rows.astype(BF16)
    turned = []
    for step in range(chips):
        which = lax.rem(chip + step, chips)
        part = rotation[:, :vecs]
        for k in range(1, chips):
            part = jnp.where(which == k, rotation[:, k * vecs : (k + 1) * vecs], part)
        turned.append(part)
    turned = jnp.concatenate(turned, axis=1)
    for which, group in ((core, y_mine), (1 - core, y_theirs)):
        for row in range(half):
            everything = jnp.concatenate([vectors[row] for vectors in group], axis=0)
            result = jnp.dot(turned, everything, preferred_element_type=F32).astype(BF16)
            at = pl.multiple_of((which * half + row) * orbs, orbs)
            basis[:, pl.ds(at, orbs)] = result


def local(
    trial_vectors,
    hamiltonian_blocks,
    correlation_offset,
    block_columns,
    block_phases,
    block_sizes,
    shift,
    halfwidth,
):
    blocks_dev, slots = block_columns.shape
    orbs = hamiltonian_blocks.shape[2]
    num_rows, num_cols = lax.axis_size("row"), lax.axis_size("col")
    total_blocks = blocks_dev * num_rows
    half = blocks_dev // CORES
    chips = num_cols // CORES
    local_vecs = trial_vectors.shape[0]
    vecs = local_vecs * CORES
    size = local_vecs * num_cols
    row, col = lax.axis_index("row"), lax.axis_index("col")
    core, chip = lax.rem(col, CORES), lax.div(col, CORES)

    def swap_cores(value):
        return lax.ppermute(value, "col", [(c, c ^ 1) for c in range(num_cols)])

    def swap_chips(value):
        pairs = []
        for r in range(num_rows):
            for x in range(chips):
                upper = r * num_cols + x * CORES + 1
                lower = (r + 1) % num_rows * num_cols + x * CORES
                pairs += [(upper, lower), (lower, upper)]
        return lax.ppermute(value, ("row", "col"), pairs)

    def from_chip(value, step):
        pairs = [((c + step * CORES) % num_cols, c) for c in range(num_cols)]
        return lax.ppermute(value, "col", pairs)

    state = jax.ShapeDtypeStruct((half, local_vecs, orbs), BF16)
    end = jax.ShapeDtypeStruct((HALF_BAND, local_vecs, orbs), BF16)
    ext = pltpu.VMEM((half + 2 * HALF_BAND, local_vecs, orbs), BF16)
    params = pltpu.CompilerParams(vmem_limit_bytes=16 << 20)
    row_flops = SLOWER * 2 * half * slots * local_vecs * orbs * orbs

    def call(kernel, name, scalars, arrays, outs, scratch, flops):
        return pl.pallas_call(
            kernel,
            name=name,
            out_shape=outs,
            in_specs=[SMEM] * len(scalars) + [VMEM] * len(arrays),
            out_specs=(VMEM,) * len(outs),
            scratch_shapes=scratch,
            compiler_params=params,
            cost_estimate=pl.CostEstimate(
                flops=flops, bytes_accessed=flops // 128, transcendentals=0
            ),
        )(*scalars, *arrays)

    def step_call(kernel, name, scalars, arrays, flops):
        return call(kernel, name, scalars, arrays, (state, end, end), [ext], flops)

    def exchange(ends):
        return swap_chips(ends[0]), swap_cores(ends[1])

    def scalars(value):
        return pltpu.with_memory_space_constraint(value, pltpu.SMEM)

    ints = scalars(jnp.stack([core, chip, col, row * blocks_dev]).astype(jnp.int32))
    shift, halfwidth = scalars(shift), scalars(halfwidth)

    def stays(value):
        return pltpu.with_memory_space_constraint(value, pltpu.HBM)

    own, give = pl.pallas_call(
        cut_kernel,
        name="cut",
        out_shape=(state, state),
        in_specs=[SMEM, HBM, HBM],
        out_specs=(VMEM, VMEM),
        scratch_shapes=[
            pltpu.SMEM(block_sizes.shape, jnp.int32),
            pltpu.VMEM(trial_vectors.shape, BF16),
            pltpu.SemaphoreType.DMA((2,)),
        ],
        compiler_params=params,
    )(ints, stays(block_sizes), stays(trial_vectors))
    got, ints = lax.optimization_barrier((swap_cores(give), ints))
    matrix = vmem((half, *hamiltonian_blocks.shape[1:]), BF16)
    ham, ovl, index, signs, place, scal = pl.pallas_call(
        functools.partial(load_kernel, total_blocks),
        name="load",
        out_shape=(
            matrix,
            matrix,
            pltpu.SMEM((half, slots), jnp.int32),
            pltpu.SMEM((half, slots), F32),
            pltpu.SMEM((3 + half,), jnp.int32),
            pltpu.SMEM((2,), F32),
        ),
        in_specs=[SMEM] * 3 + [HBM] * 5,
        out_specs=(VMEM, VMEM, SMEM, SMEM, SMEM, SMEM),
        scratch_shapes=[
            pltpu.SMEM(block_columns.shape, jnp.int32),
            pltpu.SMEM(block_phases.shape, jnp.int32),
            pltpu.SMEM(block_sizes.shape, jnp.int32),
            pltpu.SemaphoreType.DMA((2, half)),
            pltpu.SemaphoreType.DMA((3,)),
        ],
        compiler_params=params,
        cost_estimate=pl.CostEstimate(
            flops=0, bytes_accessed=4 * hamiltonian_blocks.size, transcendentals=0
        ),
    )(
        ints,
        shift,
        halfwidth,
        stays(block_columns),
        stays(block_phases),
        stays(block_sizes),
        stays(hamiltonian_blocks),
        stays(correlation_offset),
    )
    current = [jnp.where(core == 0, own, got), jnp.where(core == 0, got, own)]
    spare = half - HALF_BAND
    ends = [
        (
            lax.dynamic_slice_in_dim(value, spare * core, HALF_BAND, 0),
            lax.dynamic_slice_in_dim(value, spare * (1 - core), HALF_BAND, 0),
        )
        for value in current
    ]
    table = (place, index, signs)
    scaled, term, previous = [None] * CORES, [None] * CORES, list(current)
    halo = [exchange(ends[g]) for g in range(CORES)]
    for degree in range(DEGREE):
        for g in range(CORES):
            if g > 0:
                current[g], scaled[0] = lax.optimization_barrier((current[g], scaled[0]))
            scaled[g], *ends = step_call(
                scaled_kernel,
                "scaled",
                (*table, scal),
                (current[g], *halo[g], ham, ovl),
                2 * row_flops,
            )
            halo[g] = exchange(ends)
        for g in range(CORES):
            term[g], *ends = step_call(
                term_kernel, "term", table, (scaled[g], *halo[g], ovl), row_flops
            )
            halo[g] = exchange(ends)
        for g in range(CORES):
            first = degree == 0
            arrays = (term[g], *halo[g], scaled[g]) + (() if first else (previous[g],)) + (ovl,)
            updated, *ends = step_call(
                functools.partial(update_kernel, first),
                "update",
                table,
                arrays,
                row_flops,
            )
            halo[g] = exchange(ends)
            previous[g], current[g] = current[g], updated

    y_others = [from_chip(value, step) for step in range(1, chips) for value in current]
    image = jax.ShapeDtypeStruct((2, local_vecs, half * orbs), BF16)
    (ready,) = call(
        images_kernel,
        "images",
        table,
        (current[0], *halo[0], ham, ovl),
        (image,),
        [ext],
        2 * row_flops,
    )
    payload = jax.ShapeDtypeStruct((size + DIAGONAL_ROWS, vecs), BF16)
    keep, send = call(
        functools.partial(gram_kernel, chips),
        "gram",
        table,
        (current[1], *halo[1], ham, ovl, ready, current[0], *y_others),
        (payload, payload),
        [ext, pltpu.VMEM(image.shape, BF16), pltpu.VMEM((2, *payload.shape), BF16)],
        3 * row_flops,
    )

    def add(left, right):
        return call(add_kernel, "add", (), (left, right), (payload,), [], row_flops // 8)[0]

    summed = add(keep, swap_cores(send))
    if num_rows & (num_rows - 1):
        every = lax.all_gather(summed, "row")
        summed = every[0]
        for r in range(1, num_rows):
            summed = add(summed, every[r])
    else:
        bit = 1
        while bit < num_rows:
            other = lax.ppermute(summed, "row", [(r, r ^ bit) for r in range(num_rows)])
            summed = add(summed, other)
            bit *= 2
    mine = [summed] + [from_chip(summed, step) for step in range(1, chips)]
    theirs = [swap_cores(value) for value in mine]
    y_theirs = [swap_cores(value) for value in (*current, *y_others)]
    basis, reduced = call(
        functools.partial(finish_kernel, chips, 0.5 / (total_blocks * orbs)),
        "finish",
        (place,),
        (*mine, *theirs, *current, *y_others, *y_theirs),
        (
            jax.ShapeDtypeStruct((local_vecs, blocks_dev * orbs), BF16),
            jax.ShapeDtypeStruct((local_vecs, size), F32),
        ),
        [
            pltpu.VMEM((2, size, size), F32),
            pltpu.VMEM((size, size), F32),
            pltpu.VMEM((size, size), F32),
        ],
        10 * row_flops,
    )
    return basis, reduced.T


def solution(mesh):
    return jax.shard_map(
        local,
        mesh=mesh,
        in_specs=(
            P("col", ("pool", "row")),
            P(("pool", "row"), None, None, None),
            P(("pool", "row"), None, None, None),
            P(("pool", "row"), None),
            P(("pool", "row"), None),
            P(("pool", "row")),
            P("pool"),
            P("pool"),
        ),
        out_specs=(P("col", ("pool", "row")), P("pool", "col")),
        check_vma=False,
    )
```

```python
import functools

import jax
import jax.numpy as jnp
from jax import lax
from jax.experimental import pallas as pl
from jax.experimental.pallas import tpu as pltpu
from jax.sharding import PartitionSpec as P

HALF_BAND = 5
DEGREE = 4
CORES = 2
PANEL = 32
SLOWER = 24
SUBLANES = 8
DIAGONAL_ROWS = 16

BF16 = jnp.bfloat16
F32 = jnp.float32
NT = (((1,), (1,)), ((), ()))
TN = (((0,), (0,)), ((), ()))

SMEM = pl.BlockSpec(memory_space=pltpu.SMEM)
VMEM = pl.BlockSpec(memory_space=pltpu.VMEM)
HBM = pl.BlockSpec(memory_space=pltpu.HBM)


def vmem(shape, dtype):
    return pltpu.VMEM(shape, dtype)


def fill_ext(core, own, intra, inter, ext):
    half = own.shape[0]
    ext[HALF_BAND : HALF_BAND + half] = own[...]
    ext[pl.ds((half + HALF_BAND) * (1 - core), HALF_BAND)] = intra[...]
    ext[pl.ds((half + HALF_BAND) * core, HALF_BAND)] = inter[...]


def picked(table, ext, row):
    index, signs = table
    slots = index.shape[1]
    return jnp.concatenate(
        [ext[index[row, s]] * signs[row, s].astype(BF16) for s in range(slots)], axis=1
    )


def row_matrix(blocks, row):
    return jnp.concatenate([blocks[row, s] for s in range(blocks.shape[1])], axis=1)


def send_ends(core, full, intra_out, inter_out):
    spare = full.shape[0] - HALF_BAND
    intra_out[...] = full[pl.ds(spare * (1 - core), HALF_BAND)]
    inter_out[...] = full[pl.ds(spare * core, HALF_BAND)]


def image_of(table, ext, matrices, row):
    matrix = jnp.concatenate([row_matrix(blocks, row) for blocks in matrices], axis=0)
    return lax.dot_general(matrix, picked(table, ext, row), NT, preferred_element_type=F32)


def both_rows(table, ext, ham, ovl, row):
    orbs = ham.shape[2]
    image = image_of(table, ext, (ham, ovl), row)
    return image[:orbs].T, image[orbs:].T


def one_row(table, ext, ovl, row):
    return image_of(table, ext, (ovl,), row).T


def cut_kernel(ints, sizes, trial, own, near, give, far, across, sizes_here, here, masked, sems):
    copies = [
        pltpu.make_async_copy(sizes, sizes_here, sems.at[0]),
        pltpu.make_async_copy(trial, here, sems.at[1]),
    ]
    for copy in copies:
        copy.start()
    for copy in copies:
        copy.wait()
    half, _, orbs = own.shape
    core = ints[0]
    lane = lax.broadcasted_iota(jnp.int32, own.shape[1:], 1)
    for row in range(2 * half):
        values = here[:, row * orbs : (row + 1) * orbs].astype(F32)
        masked[row] = jnp.where(lane < sizes_here[row], values, 0.0).astype(BF16)
    spare = half - HALF_BAND
    last = 2 * half - HALF_BAND
    own[...] = masked[pl.ds(half * core, half)]
    near[...] = masked[pl.ds(half - HALF_BAND * core, HALF_BAND)]
    give[...] = masked[pl.ds(spare * (1 - core), half + HALF_BAND)]
    far[...] = masked[pl.ds(last * (1 - core), HALF_BAND)]
    across[...] = masked[pl.ds(last * core, HALF_BAND)]


def load_kernel(total, ints, shift, width, columns, phases, sizes, ham, ovl, *rest):
    ham_out, ovl_out, index, signs, place, scal, columns_here, phases_here, sizes_here = rest[:9]
    sems, more_sems = rest[9:]
    half, slots = index.shape
    first = ints[0] * half
    small = [
        pltpu.make_async_copy(source, target, more_sems.at[i])
        for i, (source, target) in enumerate(
            ((columns, columns_here), (phases, phases_here), (sizes, sizes_here))
        )
    ]
    large = [
        pltpu.make_async_copy(source.at[first + row], target.at[row], sems.at[matrix, row])
        for row in range(half)
        for matrix, (source, target) in enumerate(((ham, ham_out), (ovl, ovl_out)))
    ]
    for copy in small + large:
        copy.start()
    scal[0] = shift[0]
    scal[1] = width[0]
    for i in range(3):
        place[i] = ints[i]
    for copy in small:
        copy.wait()
    start = ints[3] + first

    def fill(row, _):
        place[3 + row] = sizes_here[first + row]
        for slot in range(slots):
            away = columns_here[first + row, slot] - (start + row) + HALF_BAND
            away = jnp.where(away < 0, away + total, away)
            away = jnp.where(away >= total, away - total, away)
            index[row, slot] = row + away
            signs[row, slot] = (1 - 2 * phases_here[first + row, slot]).astype(F32)
        return 0

    lax.fori_loop(0, half, fill, 0)
    for copy in large:
        copy.wait()


def scaled_kernel(
    ints, index, signs, scal, own, inter, intra, ham, ovl, out, inter_out, intra_out, ext
):
    core = ints[0]
    fill_ext(core, own, intra, inter, ext)
    inv = 1.0 / (jnp.zeros(own.shape[1:], F32) + scal[1])
    for row in range(own.shape[0]):
        image_h, image_e = both_rows((index, signs), ext, ham, ovl, row)
        mine = own[row].astype(F32)
        out[row] = ((image_h - scal[0] * (mine + image_e)) * inv).astype(BF16)
    send_ends(core, out, intra_out, inter_out)


def term_kernel(ints, index, signs, own, inter, intra, ovl, out, inter_out, intra_out, ext):
    core = ints[0]
    fill_ext(core, own, intra, inter, ext)
    for row in range(own.shape[0]):
        out[row] = (-one_row((index, signs), ext, ovl, row)).astype(BF16)
    send_ends(core, out, intra_out, inter_out)


def update_kernel(first, ints, index, signs, own, inter, intra, scaled, *rest):
    if first:
        ovl, out, inter_out, intra_out, ext = rest
    else:
        previous, ovl, out, inter_out, intra_out, ext = rest
    core = ints[0]
    half = own.shape[0]
    fill_ext(core, own, intra, inter, ext)
    lane = lax.broadcasted_iota(jnp.int32, own.shape[1:], 1)
    for row in range(half):
        image = one_row((index, signs), ext, ovl, row)
        filtered = scaled[row].astype(F32) + own[row].astype(F32) - image
        if not first:
            filtered = 2.0 * filtered - previous[row].astype(F32)
        out[row] = jnp.where(lane < ints[3 + row], filtered, 0.0).astype(BF16)
    send_ends(core, out, intra_out, inter_out)


def images_kernel(ints, index, signs, own, inter, intra, ham, ovl, y_other, out, ext):
    del y_other
    core = ints[0]
    fill_ext(core, own, intra, inter, ext)
    half, _, orbs = own.shape
    for row in range(half):
        image_h, image_e = both_rows((index, signs), ext, ham, ovl, row)
        at = slice(row * orbs, (row + 1) * orbs)
        out[0, :, at] = (own[row].astype(F32) + image_e).astype(BF16)
        out[1, :, at] = image_h.astype(BF16)


def gram_kernel(chips, ints, *refs):
    images, groups = refs[:CORES], refs[CORES : CORES + CORES * chips]
    keep, send, both = refs[CORES + CORES * chips :]
    core, chip = ints[0], ints[1]
    half, local_vecs, _ = groups[0].shape
    vecs = CORES * local_vecs
    flat = jnp.concatenate(
        [jnp.concatenate([group[row] for row in range(half)], axis=1) for group in groups], axis=0
    )
    eye = lax.broadcasted_iota(jnp.int32, (vecs, vecs), 0) == lax.broadcasted_iota(
        jnp.int32, (vecs, vecs), 1
    )
    for matrix in range(2):
        mine = jnp.concatenate([image[matrix] for image in images], axis=0)
        pair = lax.dot_general(mine, flat, NT, preferred_element_type=F32)
        for step in range(chips):
            where = pl.multiple_of(lax.rem(chip + step, chips) * vecs, vecs)
            block = pair[:, step * vecs : (step + 1) * vecs]
            both[matrix, pl.ds(where, vecs), :] = block.astype(BF16)
        diagonal = jnp.sum(jnp.where(eye, pair[:, :vecs], 0.0), axis=0, keepdims=True)
        both[matrix, chips * vecs :, :] = diagonal_parts(diagonal)
    keep[...] = both[core]
    send[...] = both[1 - core]


def diagonal_parts(diagonal):
    high, middle, low = (part.astype(F32) for part in split3(diagonal))
    rows = lax.broadcasted_iota(jnp.int32, (DIAGONAL_ROWS, diagonal.shape[1]), 0)
    parts = jnp.where(rows == 0, high, jnp.where(rows == 1, middle, jnp.where(rows == 2, low, 0.0)))
    return parts.astype(BF16)


def diagonal_of(payload):
    parts = payload[payload.shape[0] - DIAGONAL_ROWS :, :].astype(F32)
    return parts[0:1] + (parts[1:2] + parts[2:3])


def add_kernel(left, right, out):
    body = left.shape[0] - DIAGONAL_ROWS
    out[:body] = (left[:body, :].astype(F32) + right[:body, :].astype(F32)).astype(BF16)
    out[body:] = diagonal_parts(diagonal_of(left) + diagonal_of(right))


def split3(value):
    high = value.astype(BF16)
    rest = value - high.astype(F32)
    middle = rest.astype(BF16)
    low = (rest - middle.astype(F32)).astype(BF16)
    return high, middle, low


def panel_inverse(block):
    lane = lax.broadcasted_iota(jnp.int32, (PANEL, 128), 1)
    rows = lax.broadcasted_iota(jnp.int32, (PANEL, 128), 0)
    work = jnp.where(lane < PANEL, block, jnp.where(lax.rem(lane, PANEL) == rows, 1.0, 0.0))
    count = PANEL // SUBLANES
    pieces = [work[v * SUBLANES : (v + 1) * SUBLANES] for v in range(count)]
    sub = lax.broadcasted_iota(jnp.int32, (SUBLANES, 128), 0)

    def spread(value, k):
        return jnp.broadcast_to(value[k % SUBLANES : k % SUBLANES + 1], (SUBLANES, 128))

    pivots = [jnp.ones((SUBLANES, 128), F32) for _ in range(count)]
    for start, group in ((0, 16), (16, 16)):
        columns = {
            k: {
                v: jnp.broadcast_to(pieces[v][:, k : k + 1], (SUBLANES, 128))
                for v in range(start // SUBLANES, count)
            }
            for k in range(start, start + group)
        }
        at = spread(columns[start][start // SUBLANES], start)
        for k in range(start, start + group):
            here = k // SUBLANES
            pivots[here] = jnp.where(sub == k % SUBLANES, at, pivots[here])
            guess = pl.reciprocal(at, approx=True)
            correction = 2.0 - at * guess
            inv = guess * correction
            if k + 1 < start + group:
                below = (k + 1) // SUBLANES
                product = spread(columns[k][below], k + 1) * spread(columns[k + 1][here], k)
                at = spread(columns[k + 1][below], k + 1) - (product * guess) * correction
            factors = {v: columns[k][v] * inv for v in range(here, count)}
            factors[here] = jnp.where(sub > k % SUBLANES, factors[here], 0.0)
            for later in range(k + 1, start + group):
                top = spread(columns[later][here], k)
                for v in range(here, count):
                    columns[later][v] = columns[later][v] - factors[v] * top
            top = spread(pieces[here], k)
            for v in range(here, count):
                pieces[v] = pieces[v] - factors[v] * top
    pivot = jnp.concatenate(pivots, axis=0)
    root = lax.rsqrt(pivot)
    root = root * (1.5 - 0.5 * ((pivot * root) * root))
    return jnp.concatenate(pieces, axis=0) * root


def factor(work, inverse):
    size = work.shape[0]
    wide = lax.broadcasted_iota(jnp.int32, (PANEL, size), 1)
    tall = lax.broadcasted_iota(jnp.int32, (PANEL, size), 0)
    lane = lax.broadcasted_iota(jnp.int32, (PANEL, 128), 1)
    zero = jnp.zeros((PANEL, size), BF16)
    for start in range(0, size, PANEL):
        rows = work[start : start + PANEL, :]
        tile = start // 128 * 128
        block = work[start : start + PANEL, tile : tile + 128]
        if start % 128:
            block = pltpu.roll(block, 128 - start % 128, axis=1)
        t_high, t_mid, t_low = split3(jnp.where(lane < PANEL, 0.0, panel_inverse(block)))
        first = jnp.where(lane < 2 * PANEL, t_high, jnp.where(lane < 3 * PANEL, t_mid, t_low))
        second = jnp.where(lane < 2 * PANEL, t_high, jnp.where(lane < 3 * PANEL, t_mid, t_high))
        left = jnp.concatenate([first, second], axis=1)
        inside = (wide >= start) & (wide < start + PANEL)
        rows = jnp.where(inside, jnp.where(wide - start == tall, 1.0, 0.0), rows)
        r_high, r_mid, r_low = split3(rows)
        right = jnp.concatenate([zero, r_high, r_high, r_high, zero, r_mid, r_mid, r_low], axis=0)
        new = jnp.dot(left, right, preferred_element_type=F32)
        inverse[start : start + PANEL, :] = jnp.where(wide < start + PANEL, new, 0.0)
        after = start + PANEL
        if after < size:
            high, middle, low = split3(new)
            base = after // 128 * 128
            lhs = jnp.concatenate([high, high, middle, middle, high, low], axis=0)[:, base:]
            rhs = jnp.concatenate([high, middle, high, middle, low, high], axis=0)
            change = lax.dot_general(lhs, rhs, TN, preferred_element_type=F32)[after - base :]
            columns = lax.broadcasted_iota(jnp.int32, change.shape, 1)
            old = work[after:, :]
            work[after:, :] = jnp.where((columns >= start) & (columns < after), 0.0, old) - change


def finish_kernel(chips, scale, ints, *refs):
    mine, theirs = refs[:chips], refs[chips : 2 * chips]
    y_mine = refs[2 * chips : (2 + CORES) * chips]
    y_theirs = refs[(2 + CORES) * chips : (2 + 2 * CORES) * chips]
    basis, reduced, pair, work, inverse = refs[(2 + 2 * CORES) * chips :]
    core, chip, col = ints[0], ints[1], ints[2]
    half, local_vecs, orbs = y_mine[0].shape
    vecs = CORES * local_vecs
    eye = lax.broadcasted_iota(jnp.int32, (vecs, vecs), 0) == lax.broadcasted_iota(
        jnp.int32, (vecs, vecs), 1
    )
    for step in range(chips):
        which = lax.rem(chip + step, chips)
        rows = pl.ds(pl.multiple_of(which * vecs, vecs), vecs)
        for matrix, payload in ((core, mine[step]), (1 - core, theirs[step])):
            diagonal = diagonal_of(payload)
            for k in range(chips):
                block = payload[k * vecs : (k + 1) * vecs, :].astype(F32)
                block = jnp.where(eye & (which == k), diagonal, block)
                pair[matrix, rows, k * vecs : (k + 1) * vecs] = block
    work[...] = (pair[0] + pair[0].T) * scale
    factor(work, inverse)
    start = pl.multiple_of(col * local_vecs, local_vecs)
    own_rows = inverse[pl.ds(start, local_vecs), :]
    gram_h = (pair[1] + pair[1].T) * scale
    half_way = jnp.dot(
        own_rows, gram_h, precision=lax.Precision.HIGHEST, preferred_element_type=F32
    )
    reduced[...] = lax.dot_general(
        half_way, inverse[...], NT, precision=lax.Precision.HIGHEST, preferred_element_type=F32
    )
    rotation = own_rows.astype(BF16)
    turned = []
    for step in range(chips):
        which = lax.rem(chip + step, chips)
        part = rotation[:, :vecs]
        for k in range(1, chips):
            part = jnp.where(which == k, rotation[:, k * vecs : (k + 1) * vecs], part)
        turned.append(part)
    turned = jnp.concatenate(turned, axis=1)
    for which, group in ((core, y_mine), (1 - core, y_theirs)):
        for row in range(half):
            everything = jnp.concatenate([vectors[row] for vectors in group], axis=0)
            result = jnp.dot(turned, everything, preferred_element_type=F32).astype(BF16)
            at = pl.multiple_of((which * half + row) * orbs, orbs)
            basis[:, pl.ds(at, orbs)] = result


def local(
    trial_vectors,
    hamiltonian_blocks,
    correlation_offset,
    block_columns,
    block_phases,
    block_sizes,
    shift,
    halfwidth,
):
    blocks_dev, slots = block_columns.shape
    orbs = hamiltonian_blocks.shape[2]
    num_rows, num_cols = lax.axis_size("row"), lax.axis_size("col")
    total_blocks = blocks_dev * num_rows
    half = blocks_dev // CORES
    chips = num_cols // CORES
    local_vecs = trial_vectors.shape[0]
    vecs = local_vecs * CORES
    size = local_vecs * num_cols
    row, col = lax.axis_index("row"), lax.axis_index("col")
    core, chip = lax.rem(col, CORES), lax.div(col, CORES)

    def swap_cores(value):
        return lax.ppermute(value, "col", [(c, c ^ 1) for c in range(num_cols)])

    def swap_chips(value):
        pairs = []
        for r in range(num_rows):
            for x in range(chips):
                upper = r * num_cols + x * CORES + 1
                lower = (r + 1) % num_rows * num_cols + x * CORES
                pairs += [(upper, lower), (lower, upper)]
        return lax.ppermute(value, ("row", "col"), pairs)

    def next_chips(value):
        pairs = []
        for r in range(num_rows):
            for c in range(num_cols):
                to = (r + 1 if c % CORES == 0 else r - 1) % num_rows
                pairs.append((r * num_cols + c, to * num_cols + c))
        return lax.ppermute(value, ("row", "col"), pairs)

    def from_chip(value, step):
        pairs = [((c + step * CORES) % num_cols, c) for c in range(num_cols)]
        return lax.ppermute(value, "col", pairs)

    state = jax.ShapeDtypeStruct((half, local_vecs, orbs), BF16)
    end = jax.ShapeDtypeStruct((HALF_BAND, local_vecs, orbs), BF16)
    ext = pltpu.VMEM((half + 2 * HALF_BAND, local_vecs, orbs), BF16)
    params = pltpu.CompilerParams(vmem_limit_bytes=16 << 20)
    row_flops = SLOWER * 2 * half * slots * local_vecs * orbs * orbs

    def call(kernel, name, scalars, arrays, outs, scratch, flops):
        return pl.pallas_call(
            kernel,
            name=name,
            out_shape=outs,
            in_specs=[SMEM] * len(scalars) + [VMEM] * len(arrays),
            out_specs=(VMEM,) * len(outs),
            scratch_shapes=scratch,
            compiler_params=params,
            cost_estimate=pl.CostEstimate(
                flops=flops, bytes_accessed=flops // 128, transcendentals=0
            ),
        )(*scalars, *arrays)

    def step_call(kernel, name, scalars, arrays, flops):
        return call(kernel, name, scalars, arrays, (state, end, end), [ext], flops)

    def exchange(ends):
        return swap_chips(ends[0]), swap_cores(ends[1])

    def scalars(value):
        return pltpu.with_memory_space_constraint(value, pltpu.SMEM)

    ints = scalars(jnp.stack([core, chip, col, row * blocks_dev]).astype(jnp.int32))
    shift, halfwidth = scalars(shift), scalars(halfwidth)

    def stays(value):
        return pltpu.with_memory_space_constraint(value, pltpu.HBM)

    more = jax.ShapeDtypeStruct((half + HALF_BAND, local_vecs, orbs), BF16)
    own, near, give, far, across = pl.pallas_call(
        cut_kernel,
        name="cut",
        out_shape=(state, end, more, end, end),
        in_specs=[SMEM, HBM, HBM],
        out_specs=(VMEM,) * 5,
        scratch_shapes=[
            pltpu.SMEM(block_sizes.shape, jnp.int32),
            pltpu.VMEM(trial_vectors.shape, BF16),
            pltpu.VMEM((blocks_dev, local_vecs, orbs), BF16),
            pltpu.SemaphoreType.DMA((2,)),
        ],
        compiler_params=params,
    )(ints, stays(block_sizes), stays(trial_vectors))
    far, across = next_chips(far), swap_chips(across)
    got = swap_cores(give)
    matrix = vmem((half, *hamiltonian_blocks.shape[1:]), BF16)
    ham, ovl, index, signs, place, scal = pl.pallas_call(
        functools.partial(load_kernel, total_blocks),
        name="load",
        out_shape=(
            matrix,
            matrix,
            pltpu.SMEM((half, slots), jnp.int32),
            pltpu.SMEM((half, slots), F32),
            pltpu.SMEM((3 + half,), jnp.int32),
            pltpu.SMEM((2,), F32),
        ),
        in_specs=[SMEM] * 3 + [HBM] * 5,
        out_specs=(VMEM, VMEM, SMEM, SMEM, SMEM, SMEM),
        scratch_shapes=[
            pltpu.SMEM(block_columns.shape, jnp.int32),
            pltpu.SMEM(block_phases.shape, jnp.int32),
            pltpu.SMEM(block_sizes.shape, jnp.int32),
            pltpu.SemaphoreType.DMA((2, half)),
            pltpu.SemaphoreType.DMA((3,)),
        ],
        compiler_params=params,
        cost_estimate=pl.CostEstimate(
            flops=0, bytes_accessed=4 * hamiltonian_blocks.size, transcendentals=0
        ),
    )(
        ints,
        shift,
        halfwidth,
        stays(block_columns),
        stays(block_phases),
        stays(block_sizes),
        stays(hamiltonian_blocks),
        stays(correlation_offset),
    )
    got_own = lax.dynamic_slice_in_dim(got, HALF_BAND * core, half, 0)
    got_near = lax.dynamic_slice_in_dim(got, half * (1 - core), HALF_BAND, 0)

    def by_group(mine, other):
        return [jnp.where(core == 0, mine, other), jnp.where(core == 0, other, mine)]

    current = by_group(own, got_own)
    halo = list(zip(by_group(far, across), by_group(near, got_near)))
    table = (place, index, signs)
    scaled, term, previous = [None] * CORES, [None] * CORES, list(current)
    for degree in range(DEGREE):
        for g in range(CORES):
            if g > 0:
                current[g], scaled[0] = lax.optimization_barrier((current[g], scaled[0]))
            scaled[g], *ends = step_call(
                scaled_kernel,
                "scaled",
                (*table, scal),
                (current[g], *halo[g], ham, ovl),
                2 * row_flops,
            )
            halo[g] = exchange(ends)
        for g in range(CORES):
            term[g], *ends = step_call(
                term_kernel, "term", table, (scaled[g], *halo[g], ovl), row_flops
            )
            halo[g] = exchange(ends)
        for g in range(CORES):
            first = degree == 0
            arrays = (term[g], *halo[g], scaled[g]) + (() if first else (previous[g],)) + (ovl,)
            updated, *ends = step_call(
                functools.partial(update_kernel, first),
                "update",
                table,
                arrays,
                row_flops,
            )
            halo[g] = exchange(ends)
            previous[g], current[g] = current[g], updated

    y_others = [from_chip(value, step) for step in range(1, chips) for value in current]
    image = jax.ShapeDtypeStruct((2, local_vecs, half * orbs), BF16)
    images = []
    for g, vectors in enumerate(current):
        if g > 0:
            vectors, images[0] = lax.optimization_barrier((vectors, images[0]))
        images += call(
            images_kernel,
            "images",
            table,
            (vectors, *halo[g], ham, ovl, y_others[0]),
            (image,),
            [ext],
            2 * row_flops,
        )
    payload = jax.ShapeDtypeStruct((size + DIAGONAL_ROWS, vecs), BF16)
    keep, send = call(
        functools.partial(gram_kernel, chips),
        "gram",
        (place,),
        (*images, *current, *y_others),
        (payload, payload),
        [pltpu.VMEM((2, *payload.shape), BF16)],
        row_flops,
    )

    def add(left, right):
        return call(add_kernel, "add", (), (left, right), (payload,), [], row_flops // 8)[0]

    summed = add(keep, swap_cores(send))
    if num_rows & (num_rows - 1):
        every = lax.all_gather(summed, "row")
        summed = every[0]
        for r in range(1, num_rows):
            summed = add(summed, every[r])
    else:
        bit = 1
        while bit < num_rows:
            other = lax.ppermute(summed, "row", [(r, r ^ bit) for r in range(num_rows)])
            summed = add(summed, other)
            bit *= 2
    mine = [summed] + [from_chip(summed, step) for step in range(1, chips)]
    theirs = [swap_cores(value) for value in mine]
    y_theirs = [swap_cores(value) for value in (*current, *y_others)]
    basis, reduced = call(
        functools.partial(finish_kernel, chips, 0.5 / (total_blocks * orbs)),
        "finish",
        (place,),
        (*mine, *theirs, *current, *y_others, *y_theirs),
        (
            jax.ShapeDtypeStruct((local_vecs, blocks_dev * orbs), BF16),
            jax.ShapeDtypeStruct((local_vecs, size), F32),
        ),
        [
            pltpu.VMEM((2, size, size), F32),
            pltpu.VMEM((size, size), F32),
            pltpu.VMEM((size, size), F32),
        ],
        10 * row_flops,
    )
    return basis, reduced.T


def solution(mesh):
    return jax.shard_map(
        local,
        mesh=mesh,
        in_specs=(
            P("col", ("pool", "row")),
            P(("pool", "row"), None, None, None),
            P(("pool", "row"), None, None, None),
            P(("pool", "row"), None),
            P(("pool", "row"), None),
            P(("pool", "row")),
            P("pool"),
            P("pool"),
        ),
        out_specs=(P("col", ("pool", "row")), P("pool", "col")),
        check_vma=False,
    )
```

```python
import functools

import jax
import jax.numpy as jnp
from jax import lax
from jax.experimental import pallas as pl
from jax.experimental.pallas import tpu as pltpu
from jax.sharding import PartitionSpec as P

HALF_BAND = 5
DEGREE = 4
CORES = 2
PANEL = 32
SLOWER = 24
SUBLANES = 8
DIAGONAL_ROWS = 16
DEVICE_ROW = 3

BF16 = jnp.bfloat16
F32 = jnp.float32
NT = (((1,), (1,)), ((), ()))
TN = (((0,), (0,)), ((), ()))

SMEM = pl.BlockSpec(memory_space=pltpu.SMEM)
VMEM = pl.BlockSpec(memory_space=pltpu.VMEM)
HBM = pl.BlockSpec(memory_space=pltpu.HBM)


def vmem(shape, dtype):
    return pltpu.VMEM(shape, dtype)


def fill_ext(core, own, intra, inter, ext):
    half = own.shape[0]
    ext[HALF_BAND : HALF_BAND + half] = own[...]
    ext[pl.ds((half + HALF_BAND) * (1 - core), HALF_BAND)] = intra[...]
    ext[pl.ds((half + HALF_BAND) * core, HALF_BAND)] = inter[...]


def picked(table, ext, row):
    index, signs = table
    slots = index.shape[1]
    return jnp.concatenate(
        [ext[index[row, s]] * signs[row, s].astype(BF16) for s in range(slots)], axis=1
    )


def row_matrix(blocks, row):
    return jnp.concatenate([blocks[row, s] for s in range(blocks.shape[1])], axis=1)


def send_ends(core, full, intra_out, inter_out):
    spare = full.shape[0] - HALF_BAND
    intra_out[...] = full[pl.ds(spare * (1 - core), HALF_BAND)]
    inter_out[...] = full[pl.ds(spare * core, HALF_BAND)]


def image_of(table, ext, matrices, row):
    matrix = jnp.concatenate([row_matrix(blocks, row) for blocks in matrices], axis=0)
    return lax.dot_general(matrix, picked(table, ext, row), NT, preferred_element_type=F32)


def both_rows(table, ext, ham, ovl, row):
    orbs = ham.shape[2]
    image = image_of(table, ext, (ham, ovl), row)
    return image[:orbs].T, image[orbs:].T


def one_row(table, ext, ovl, row):
    return image_of(table, ext, (ovl,), row).T


def cut_kernel(ints, sizes, trial, own, near, give, far, across, sizes_here, here, masked, sems):
    copies = [
        pltpu.make_async_copy(sizes, sizes_here, sems.at[0]),
        pltpu.make_async_copy(trial, here, sems.at[1]),
    ]
    for copy in copies:
        copy.start()
    for copy in copies:
        copy.wait()
    half, _, orbs = own.shape
    core = ints[0]
    lane = lax.broadcasted_iota(jnp.int32, own.shape[1:], 1)
    for row in range(2 * half):
        values = here[:, row * orbs : (row + 1) * orbs].astype(F32)
        masked[row] = jnp.where(lane < sizes_here[row], values, 0.0).astype(BF16)
    spare = half - HALF_BAND
    last = 2 * half - HALF_BAND
    own[...] = masked[pl.ds(half * core, half)]
    near[...] = masked[pl.ds(half - HALF_BAND * core, HALF_BAND)]
    give[...] = masked[pl.ds(spare * (1 - core), half + HALF_BAND)]
    far[...] = masked[pl.ds(last * (1 - core), HALF_BAND)]
    across[...] = masked[pl.ds(last * core, HALF_BAND)]


def load_kernel(total, ints, shift, width, columns, phases, sizes, ham, ovl, *rest):
    ham_out, ovl_out, index, signs, place, scal, columns_here, phases_here, sizes_here = rest[:9]
    sems, more_sems = rest[9:]
    half, slots = index.shape
    first = ints[0] * half
    small = [
        pltpu.make_async_copy(source, target, more_sems.at[i])
        for i, (source, target) in enumerate(
            ((columns, columns_here), (phases, phases_here), (sizes, sizes_here))
        )
    ]
    large = [
        pltpu.make_async_copy(source.at[first + row], target.at[row], sems.at[matrix, row])
        for row in range(half)
        for matrix, (source, target) in enumerate(((ham, ham_out), (ovl, ovl_out)))
    ]
    for copy in small + large:
        copy.start()
    scal[0] = shift[0]
    scal[1] = width[0]
    for i in range(3):
        place[i] = ints[i]
    place[DEVICE_ROW] = ints[4]
    for copy in small:
        copy.wait()
    start = ints[3] + first

    def fill(row, _):
        place[4 + row] = sizes_here[first + row]
        for slot in range(slots):
            away = columns_here[first + row, slot] - (start + row) + HALF_BAND
            away = jnp.where(away < 0, away + total, away)
            away = jnp.where(away >= total, away - total, away)
            index[row, slot] = row + away
            signs[row, slot] = (1 - 2 * phases_here[first + row, slot]).astype(F32)
        return 0

    lax.fori_loop(0, half, fill, 0)
    for copy in large:
        copy.wait()


def scaled_kernel(
    ints, index, signs, scal, own, inter, intra, ham, ovl, out, inter_out, intra_out, ext
):
    core = ints[0]
    fill_ext(core, own, intra, inter, ext)
    inv = 1.0 / (jnp.zeros(own.shape[1:], F32) + scal[1])
    for row in range(own.shape[0]):
        image_h, image_e = both_rows((index, signs), ext, ham, ovl, row)
        mine = own[row].astype(F32)
        out[row] = ((image_h - scal[0] * (mine + image_e)) * inv).astype(BF16)
    send_ends(core, out, intra_out, inter_out)


def term_kernel(ints, index, signs, own, inter, intra, ovl, out, inter_out, intra_out, ext):
    core = ints[0]
    fill_ext(core, own, intra, inter, ext)
    for row in range(own.shape[0]):
        out[row] = (-one_row((index, signs), ext, ovl, row)).astype(BF16)
    send_ends(core, out, intra_out, inter_out)


def update_kernel(first, ints, index, signs, own, inter, intra, scaled, *rest):
    if first:
        ovl, out, inter_out, intra_out, ext = rest
    else:
        previous, ovl, out, inter_out, intra_out, ext = rest
    core = ints[0]
    half = own.shape[0]
    fill_ext(core, own, intra, inter, ext)
    lane = lax.broadcasted_iota(jnp.int32, own.shape[1:], 1)
    for row in range(half):
        image = one_row((index, signs), ext, ovl, row)
        filtered = scaled[row].astype(F32) + own[row].astype(F32) - image
        if not first:
            filtered = 2.0 * filtered - previous[row].astype(F32)
        out[row] = jnp.where(lane < ints[4 + row], filtered, 0.0).astype(BF16)
    send_ends(core, out, intra_out, inter_out)


def images_kernel(ints, index, signs, own, inter, intra, ham, ovl, y_other, out, ext):
    del y_other
    core = ints[0]
    fill_ext(core, own, intra, inter, ext)
    half, _, orbs = own.shape
    for row in range(half):
        image_h, image_e = both_rows((index, signs), ext, ham, ovl, row)
        at = slice(row * orbs, (row + 1) * orbs)
        out[0, :, at] = (own[row].astype(F32) + image_e).astype(BF16)
        out[1, :, at] = image_h.astype(BF16)


def gram_kernel(chips, ints, *refs):
    images, groups = refs[:CORES], refs[CORES : CORES + CORES * chips]
    keep, send, both = refs[CORES + CORES * chips :]
    core, chip = ints[0], ints[1]
    half, local_vecs, _ = groups[0].shape
    vecs = CORES * local_vecs
    flat = jnp.concatenate(
        [jnp.concatenate([group[row] for row in range(half)], axis=1) for group in groups], axis=0
    )
    eye = lax.broadcasted_iota(jnp.int32, (vecs, vecs), 0) == lax.broadcasted_iota(
        jnp.int32, (vecs, vecs), 1
    )
    for matrix in range(2):
        mine = jnp.concatenate([image[matrix] for image in images], axis=0)
        pair = lax.dot_general(mine, flat, NT, preferred_element_type=F32)
        for step in range(chips):
            where = pl.multiple_of(lax.rem(chip + step, chips) * vecs, vecs)
            block = pair[:, step * vecs : (step + 1) * vecs]
            both[matrix, pl.ds(where, vecs), :] = block.astype(BF16)
        diagonal = jnp.sum(jnp.where(eye, pair[:, :vecs], 0.0), axis=0, keepdims=True)
        both[matrix, chips * vecs :, :] = diagonal_parts(diagonal)
    keep[...] = both[core]
    send[...] = both[1 - core]


def diagonal_parts(diagonal):
    high, middle, low = (part.astype(F32) for part in split3(diagonal))
    rows = lax.broadcasted_iota(jnp.int32, (DIAGONAL_ROWS, diagonal.shape[1]), 0)
    parts = jnp.where(rows == 0, high, jnp.where(rows == 1, middle, jnp.where(rows == 2, low, 0.0)))
    return parts.astype(BF16)


def diagonal_of(payload):
    parts = payload[payload.shape[0] - DIAGONAL_ROWS :, :].astype(F32)
    return parts[0:1] + (parts[1:2] + parts[2:3])


def add_kernel(left, right, out):
    body = left.shape[0] - DIAGONAL_ROWS
    out[:body] = (left[:body, :].astype(F32) + right[:body, :].astype(F32)).astype(BF16)
    out[body:] = diagonal_parts(diagonal_of(left) + diagonal_of(right))


def sum_kernel(ints, *refs):
    *payloads, out, held = refs
    count = len(payloads)
    for step, payload in enumerate(payloads):
        held[lax.rem(ints[DEVICE_ROW] + count - step, count)] = payload[...]
    body = out.shape[0] - DIAGONAL_ROWS
    total = held[0, :body, :].astype(F32)
    diagonal = diagonal_of(held.at[0])
    for r in range(1, count):
        total = total + held[r, :body, :].astype(F32)
        diagonal = diagonal + diagonal_of(held.at[r])
    out[:body] = total.astype(BF16)
    out[body:] = diagonal_parts(diagonal)


def split3(value):
    high = value.astype(BF16)
    rest = value - high.astype(F32)
    middle = rest.astype(BF16)
    low = (rest - middle.astype(F32)).astype(BF16)
    return high, middle, low


def panel_inverse(block):
    lane = lax.broadcasted_iota(jnp.int32, (PANEL, 128), 1)
    rows = lax.broadcasted_iota(jnp.int32, (PANEL, 128), 0)
    work = jnp.where(lane < PANEL, block, jnp.where(lax.rem(lane, PANEL) == rows, 1.0, 0.0))
    count = PANEL // SUBLANES
    pieces = [work[v * SUBLANES : (v + 1) * SUBLANES] for v in range(count)]
    sub = lax.broadcasted_iota(jnp.int32, (SUBLANES, 128), 0)

    def spread(value, k):
        return jnp.broadcast_to(value[k % SUBLANES : k % SUBLANES + 1], (SUBLANES, 128))

    pivots = [jnp.ones((SUBLANES, 128), F32) for _ in range(count)]
    for start, group in ((0, 16), (16, 16)):
        columns = {
            k: {
                v: jnp.broadcast_to(pieces[v][:, k : k + 1], (SUBLANES, 128))
                for v in range(start // SUBLANES, count)
            }
            for k in range(start, start + group)
        }
        at = spread(columns[start][start // SUBLANES], start)
        for k in range(start, start + group):
            here = k // SUBLANES
            pivots[here] = jnp.where(sub == k % SUBLANES, at, pivots[here])
            guess = pl.reciprocal(at, approx=True)
            correction = 2.0 - at * guess
            inv = guess * correction
            if k + 1 < start + group:
                below = (k + 1) // SUBLANES
                product = spread(columns[k][below], k + 1) * spread(columns[k + 1][here], k)
                at = spread(columns[k + 1][below], k + 1) - (product * guess) * correction
            factors = {v: columns[k][v] * inv for v in range(here, count)}
            factors[here] = jnp.where(sub > k % SUBLANES, factors[here], 0.0)
            for later in range(k + 1, start + group):
                top = spread(columns[later][here], k)
                for v in range(here, count):
                    columns[later][v] = columns[later][v] - factors[v] * top
            top = spread(pieces[here], k)
            for v in range(here, count):
                pieces[v] = pieces[v] - factors[v] * top
    pivot = jnp.concatenate(pivots, axis=0)
    root = lax.rsqrt(pivot)
    root = root * (1.5 - 0.5 * ((pivot * root) * root))
    return jnp.concatenate(pieces, axis=0) * root


def factor(work, inverse):
    size = work.shape[0]
    wide = lax.broadcasted_iota(jnp.int32, (PANEL, size), 1)
    tall = lax.broadcasted_iota(jnp.int32, (PANEL, size), 0)
    lane = lax.broadcasted_iota(jnp.int32, (PANEL, 128), 1)
    zero = jnp.zeros((PANEL, size), BF16)
    for start in range(0, size, PANEL):
        rows = work[start : start + PANEL, :]
        tile = start // 128 * 128
        block = work[start : start + PANEL, tile : tile + 128]
        if start % 128:
            block = pltpu.roll(block, 128 - start % 128, axis=1)
        t_high, t_mid, t_low = split3(jnp.where(lane < PANEL, 0.0, panel_inverse(block)))
        first = jnp.where(lane < 2 * PANEL, t_high, jnp.where(lane < 3 * PANEL, t_mid, t_low))
        second = jnp.where(lane < 2 * PANEL, t_high, jnp.where(lane < 3 * PANEL, t_mid, t_high))
        left = jnp.concatenate([first, second], axis=1)
        inside = (wide >= start) & (wide < start + PANEL)
        rows = jnp.where(inside, jnp.where(wide - start == tall, 1.0, 0.0), rows)
        r_high, r_mid, r_low = split3(rows)
        right = jnp.concatenate([zero, r_high, r_high, r_high, zero, r_mid, r_mid, r_low], axis=0)
        new = jnp.dot(left, right, preferred_element_type=F32)
        inverse[start : start + PANEL, :] = jnp.where(wide < start + PANEL, new, 0.0)
        after = start + PANEL
        if after < size:
            high, middle, low = split3(new)
            base = after // 128 * 128
            lhs = jnp.concatenate([high, high, middle, middle, high, low], axis=0)[:, base:]
            rhs = jnp.concatenate([high, middle, high, middle, low, high], axis=0)
            change = lax.dot_general(lhs, rhs, TN, preferred_element_type=F32)[after - base :]
            columns = lax.broadcasted_iota(jnp.int32, change.shape, 1)
            old = work[after:, :]
            work[after:, :] = jnp.where((columns >= start) & (columns < after), 0.0, old) - change


def finish_kernel(chips, scale, ints, *refs):
    mine, theirs = refs[:chips], refs[chips : 2 * chips]
    y_mine = refs[2 * chips : (2 + CORES) * chips]
    y_theirs = refs[(2 + CORES) * chips : (2 + 2 * CORES) * chips]
    basis, reduced, pair, work, inverse = refs[(2 + 2 * CORES) * chips :]
    core, chip, col = ints[0], ints[1], ints[2]
    half, local_vecs, orbs = y_mine[0].shape
    vecs = CORES * local_vecs
    eye = lax.broadcasted_iota(jnp.int32, (vecs, vecs), 0) == lax.broadcasted_iota(
        jnp.int32, (vecs, vecs), 1
    )
    for step in range(chips):
        which = lax.rem(chip + step, chips)
        rows = pl.ds(pl.multiple_of(which * vecs, vecs), vecs)
        for matrix, payload in ((core, mine[step]), (1 - core, theirs[step])):
            diagonal = diagonal_of(payload)
            for k in range(chips):
                block = payload[k * vecs : (k + 1) * vecs, :].astype(F32)
                block = jnp.where(eye & (which == k), diagonal, block)
                pair[matrix, rows, k * vecs : (k + 1) * vecs] = block
    work[...] = (pair[0] + pair[0].T) * scale
    factor(work, inverse)
    start = pl.multiple_of(col * local_vecs, local_vecs)
    own_rows = inverse[pl.ds(start, local_vecs), :]
    gram_h = (pair[1] + pair[1].T) * scale
    half_way = jnp.dot(
        own_rows, gram_h, precision=lax.Precision.HIGHEST, preferred_element_type=F32
    )
    reduced[...] = lax.dot_general(
        half_way, inverse[...], NT, precision=lax.Precision.HIGHEST, preferred_element_type=F32
    )
    rotation = own_rows.astype(BF16)
    turned = []
    for step in range(chips):
        which = lax.rem(chip + step, chips)
        part = rotation[:, :vecs]
        for k in range(1, chips):
            part = jnp.where(which == k, rotation[:, k * vecs : (k + 1) * vecs], part)
        turned.append(part)
    turned = jnp.concatenate(turned, axis=1)
    for which, group in ((core, y_mine), (1 - core, y_theirs)):
        for row in range(half):
            everything = jnp.concatenate([vectors[row] for vectors in group], axis=0)
            result = jnp.dot(turned, everything, preferred_element_type=F32).astype(BF16)
            at = pl.multiple_of((which * half + row) * orbs, orbs)
            basis[:, pl.ds(at, orbs)] = result


def local(
    trial_vectors,
    hamiltonian_blocks,
    correlation_offset,
    block_columns,
    block_phases,
    block_sizes,
    shift,
    halfwidth,
):
    blocks_dev, slots = block_columns.shape
    orbs = hamiltonian_blocks.shape[2]
    num_rows, num_cols = lax.axis_size("row"), lax.axis_size("col")
    total_blocks = blocks_dev * num_rows
    half = blocks_dev // CORES
    chips = num_cols // CORES
    local_vecs = trial_vectors.shape[0]
    vecs = local_vecs * CORES
    size = local_vecs * num_cols
    row, col = lax.axis_index("row"), lax.axis_index("col")
    core, chip = lax.rem(col, CORES), lax.div(col, CORES)

    def swap_cores(value):
        return lax.ppermute(value, "col", [(c, c ^ 1) for c in range(num_cols)])

    def swap_chips(value):
        pairs = []
        for r in range(num_rows):
            for x in range(chips):
                upper = r * num_cols + x * CORES + 1
                lower = (r + 1) % num_rows * num_cols + x * CORES
                pairs += [(upper, lower), (lower, upper)]
        return lax.ppermute(value, ("row", "col"), pairs)

    def next_chips(value):
        pairs = []
        for r in range(num_rows):
            for c in range(num_cols):
                to = (r + 1 if c % CORES == 0 else r - 1) % num_rows
                pairs.append((r * num_cols + c, to * num_cols + c))
        return lax.ppermute(value, ("row", "col"), pairs)

    def from_chip(value, step):
        pairs = [((c + step * CORES) % num_cols, c) for c in range(num_cols)]
        return lax.ppermute(value, "col", pairs)

    state = jax.ShapeDtypeStruct((half, local_vecs, orbs), BF16)
    end = jax.ShapeDtypeStruct((HALF_BAND, local_vecs, orbs), BF16)
    ext = pltpu.VMEM((half + 2 * HALF_BAND, local_vecs, orbs), BF16)
    params = pltpu.CompilerParams(vmem_limit_bytes=16 << 20)
    row_flops = SLOWER * 2 * half * slots * local_vecs * orbs * orbs

    def call(kernel, name, scalars, arrays, outs, scratch, flops):
        return pl.pallas_call(
            kernel,
            name=name,
            out_shape=outs,
            in_specs=[SMEM] * len(scalars) + [VMEM] * len(arrays),
            out_specs=(VMEM,) * len(outs),
            scratch_shapes=scratch,
            compiler_params=params,
            cost_estimate=pl.CostEstimate(
                flops=flops, bytes_accessed=flops // 128, transcendentals=0
            ),
        )(*scalars, *arrays)

    def step_call(kernel, name, scalars, arrays, flops):
        return call(kernel, name, scalars, arrays, (state, end, end), [ext], flops)

    def exchange(ends):
        return swap_chips(ends[0]), swap_cores(ends[1])

    def scalars(value):
        return pltpu.with_memory_space_constraint(value, pltpu.SMEM)

    ints = scalars(jnp.stack([core, chip, col, row * blocks_dev, row]).astype(jnp.int32))
    shift, halfwidth = scalars(shift), scalars(halfwidth)

    def stays(value):
        return pltpu.with_memory_space_constraint(value, pltpu.HBM)

    more = jax.ShapeDtypeStruct((half + HALF_BAND, local_vecs, orbs), BF16)
    own, near, give, far, across = pl.pallas_call(
        cut_kernel,
        name="cut",
        out_shape=(state, end, more, end, end),
        in_specs=[SMEM, HBM, HBM],
        out_specs=(VMEM,) * 5,
        scratch_shapes=[
            pltpu.SMEM(block_sizes.shape, jnp.int32),
            pltpu.VMEM(trial_vectors.shape, BF16),
            pltpu.VMEM((blocks_dev, local_vecs, orbs), BF16),
            pltpu.SemaphoreType.DMA((2,)),
        ],
        compiler_params=params,
    )(ints, stays(block_sizes), stays(trial_vectors))
    far, across = next_chips(far), swap_chips(across)
    got = swap_cores(give)
    matrix = vmem((half, *hamiltonian_blocks.shape[1:]), BF16)
    ham, ovl, index, signs, place, scal = pl.pallas_call(
        functools.partial(load_kernel, total_blocks),
        name="load",
        out_shape=(
            matrix,
            matrix,
            pltpu.SMEM((half, slots), jnp.int32),
            pltpu.SMEM((half, slots), F32),
            pltpu.SMEM((4 + half,), jnp.int32),
            pltpu.SMEM((2,), F32),
        ),
        in_specs=[SMEM] * 3 + [HBM] * 5,
        out_specs=(VMEM, VMEM, SMEM, SMEM, SMEM, SMEM),
        scratch_shapes=[
            pltpu.SMEM(block_columns.shape, jnp.int32),
            pltpu.SMEM(block_phases.shape, jnp.int32),
            pltpu.SMEM(block_sizes.shape, jnp.int32),
            pltpu.SemaphoreType.DMA((2, half)),
            pltpu.SemaphoreType.DMA((3,)),
        ],
        compiler_params=params,
        cost_estimate=pl.CostEstimate(
            flops=0, bytes_accessed=4 * hamiltonian_blocks.size, transcendentals=0
        ),
    )(
        ints,
        shift,
        halfwidth,
        stays(block_columns),
        stays(block_phases),
        stays(block_sizes),
        stays(hamiltonian_blocks),
        stays(correlation_offset),
    )
    got_own = lax.dynamic_slice_in_dim(got, HALF_BAND * core, half, 0)
    got_near = lax.dynamic_slice_in_dim(got, half * (1 - core), HALF_BAND, 0)

    def by_group(mine, other):
        return [jnp.where(core == 0, mine, other), jnp.where(core == 0, other, mine)]

    current = by_group(own, got_own)
    halo = list(zip(by_group(far, across), by_group(near, got_near)))
    table = (place, index, signs)
    scaled, term, previous = [None] * CORES, [None] * CORES, list(current)
    for degree in range(DEGREE):
        for g in range(CORES):
            if g > 0:
                current[g], scaled[0] = lax.optimization_barrier((current[g], scaled[0]))
            scaled[g], *ends = step_call(
                scaled_kernel,
                "scaled",
                (*table, scal),
                (current[g], *halo[g], ham, ovl),
                2 * row_flops,
            )
            halo[g] = exchange(ends)
        for g in range(CORES):
            term[g], *ends = step_call(
                term_kernel, "term", table, (scaled[g], *halo[g], ovl), row_flops
            )
            halo[g] = exchange(ends)
        for g in range(CORES):
            first = degree == 0
            arrays = (term[g], *halo[g], scaled[g]) + (() if first else (previous[g],)) + (ovl,)
            updated, *ends = step_call(
                functools.partial(update_kernel, first),
                "update",
                table,
                arrays,
                row_flops,
            )
            halo[g] = exchange(ends)
            previous[g], current[g] = current[g], updated

    y_others = [from_chip(value, step) for step in range(1, chips) for value in current]
    image = jax.ShapeDtypeStruct((2, local_vecs, half * orbs), BF16)
    images = []
    for g, vectors in enumerate(current):
        if g > 0:
            vectors, images[0] = lax.optimization_barrier((vectors, images[0]))
        images += call(
            images_kernel,
            "images",
            table,
            (vectors, *halo[g], ham, ovl, y_others[0]),
            (image,),
            [ext],
            2 * row_flops,
        )
    payload = jax.ShapeDtypeStruct((size + DIAGONAL_ROWS, vecs), BF16)
    keep, send = call(
        functools.partial(gram_kernel, chips),
        "gram",
        (place,),
        (*images, *current, *y_others),
        (payload, payload),
        [pltpu.VMEM((2, *payload.shape), BF16)],
        row_flops,
    )

    def add(left, right):
        return call(add_kernel, "add", (), (left, right), (payload,), [], row_flops // 8)[0]

    summed = add(keep, swap_cores(send))
    if num_rows <= 4:
        others = [
            lax.ppermute(summed, "row", [(r, (r + step) % num_rows) for r in range(num_rows)])
            for step in range(1, num_rows)
        ]
        (summed,) = call(
            sum_kernel,
            "sum",
            (place,),
            (summed, *others),
            (payload,),
            [pltpu.VMEM((num_rows, *payload.shape), BF16)],
            row_flops // 8,
        )
    elif num_rows & (num_rows - 1):
        every = lax.all_gather(summed, "row")
        summed = every[0]
        for r in range(1, num_rows):
            summed = add(summed, every[r])
    else:
        bit = 1
        while bit < num_rows:
            other = lax.ppermute(summed, "row", [(r, r ^ bit) for r in range(num_rows)])
            summed = add(summed, other)
            bit *= 2
    mine = [summed] + [from_chip(summed, step) for step in range(1, chips)]
    theirs = [swap_cores(value) for value in mine]
    y_theirs = [swap_cores(value) for value in (*current, *y_others)]
    basis, reduced = call(
        functools.partial(finish_kernel, chips, 0.5 / (total_blocks * orbs)),
        "finish",
        (place,),
        (*mine, *theirs, *current, *y_others, *y_theirs),
        (
            jax.ShapeDtypeStruct((local_vecs, blocks_dev * orbs), BF16),
            jax.ShapeDtypeStruct((local_vecs, size), F32),
        ),
        [
            pltpu.VMEM((2, size, size), F32),
            pltpu.VMEM((size, size), F32),
            pltpu.VMEM((size, size), F32),
        ],
        10 * row_flops,
    )
    return basis, reduced.T


def solution(mesh):
    return jax.shard_map(
        local,
        mesh=mesh,
        in_specs=(
            P("col", ("pool", "row")),
            P(("pool", "row"), None, None, None),
            P(("pool", "row"), None, None, None),
            P(("pool", "row"), None),
            P(("pool", "row"), None),
            P(("pool", "row")),
            P("pool"),
            P("pool"),
        ),
        out_specs=(P("col", ("pool", "row")), P("pool", "col")),
        check_vma=False,
    )
```

```python
import functools

import jax
import jax.numpy as jnp
from jax import lax
from jax.experimental import pallas as pl
from jax.experimental.pallas import tpu as pltpu
from jax.sharding import PartitionSpec as P

HALF_BAND = 5
DEGREE = 4
CORES = 2
PANEL = 32
SLOWER = 24
SUBLANES = 8
DIAGONAL_ROWS = 16
DEVICE_ROW = 3

BF16 = jnp.bfloat16
F32 = jnp.float32
NT = (((1,), (1,)), ((), ()))
TN = (((0,), (0,)), ((), ()))

SMEM = pl.BlockSpec(memory_space=pltpu.SMEM)
VMEM = pl.BlockSpec(memory_space=pltpu.VMEM)
HBM = pl.BlockSpec(memory_space=pltpu.HBM)


def vmem(shape, dtype):
    return pltpu.VMEM(shape, dtype)


def fill_ext(core, own, intra, inter, ext):
    half = own.shape[0]
    ext[HALF_BAND : HALF_BAND + half] = own[...]
    ext[pl.ds((half + HALF_BAND) * (1 - core), HALF_BAND)] = intra[...]
    ext[pl.ds((half + HALF_BAND) * core, HALF_BAND)] = inter[...]


def picked(table, ext, row):
    index, signs = table
    slots = index.shape[1]
    return jnp.concatenate(
        [ext[index[row, s]] * signs[row, s].astype(BF16) for s in range(slots)], axis=1
    )


def row_matrix(blocks, row):
    return jnp.concatenate([blocks[row, s] for s in range(blocks.shape[1])], axis=1)


def send_ends(core, full, intra_out, inter_out):
    spare = full.shape[0] - HALF_BAND
    intra_out[...] = full[pl.ds(spare * (1 - core), HALF_BAND)]
    inter_out[...] = full[pl.ds(spare * core, HALF_BAND)]


def image_of(table, ext, matrices, row):
    matrix = jnp.concatenate([row_matrix(blocks, row) for blocks in matrices], axis=0)
    return lax.dot_general(matrix, picked(table, ext, row), NT, preferred_element_type=F32)


def both_rows(table, ext, ham, ovl, row):
    orbs = ham.shape[2]
    image = image_of(table, ext, (ham, ovl), row)
    return image[:orbs].T, image[orbs:].T


def one_row(table, ext, ovl, row):
    return image_of(table, ext, (ovl,), row).T


def cut_kernel(ints, sizes, trial, own, near, give, far, across, sizes_here, here, masked, sems):
    copies = [
        pltpu.make_async_copy(sizes, sizes_here, sems.at[0]),
        pltpu.make_async_copy(trial, here, sems.at[1]),
    ]
    for copy in copies:
        copy.start()
    for copy in copies:
        copy.wait()
    half, _, orbs = own.shape
    core = ints[0]
    lane = lax.broadcasted_iota(jnp.int32, own.shape[1:], 1)
    for row in range(2 * half):
        values = here[:, row * orbs : (row + 1) * orbs].astype(F32)
        masked[row] = jnp.where(lane < sizes_here[row], values, 0.0).astype(BF16)
    spare = half - HALF_BAND
    last = 2 * half - HALF_BAND
    own[...] = masked[pl.ds(half * core, half)]
    near[...] = masked[pl.ds(half - HALF_BAND * core, HALF_BAND)]
    give[...] = masked[pl.ds(spare * (1 - core), half + HALF_BAND)]
    far[...] = masked[pl.ds(last * (1 - core), HALF_BAND)]
    across[...] = masked[pl.ds(last * core, HALF_BAND)]


def load_kernel(total, ints, shift, width, columns, phases, sizes, ham, ovl, *rest):
    ham_out, ovl_out, index, signs, place, scal, columns_here, phases_here, sizes_here = rest[:9]
    sems, more_sems = rest[9:]
    half, slots = index.shape
    first = ints[0] * half
    small = [
        pltpu.make_async_copy(source, target, more_sems.at[i])
        for i, (source, target) in enumerate(
            ((columns, columns_here), (phases, phases_here), (sizes, sizes_here))
        )
    ]
    large = [
        pltpu.make_async_copy(source.at[first + row], target.at[row], sems.at[matrix, row])
        for row in range(half)
        for matrix, (source, target) in enumerate(((ham, ham_out), (ovl, ovl_out)))
    ]
    for copy in small + large:
        copy.start()
    scal[0] = shift[0]
    scal[1] = width[0]
    for i in range(3):
        place[i] = ints[i]
    place[DEVICE_ROW] = ints[4]
    for copy in small:
        copy.wait()
    start = ints[3] + first

    def fill(row, _):
        place[4 + row] = sizes_here[first + row]
        for slot in range(slots):
            away = columns_here[first + row, slot] - (start + row) + HALF_BAND
            away = jnp.where(away < 0, away + total, away)
            away = jnp.where(away >= total, away - total, away)
            index[row, slot] = row + away
            signs[row, slot] = (1 - 2 * phases_here[first + row, slot]).astype(F32)
        return 0

    lax.fori_loop(0, half, fill, 0)
    for copy in large:
        copy.wait()


def scaled_kernel(
    ints, index, signs, scal, own, inter, intra, ham, ovl, out, inter_out, intra_out, ext
):
    core = ints[0]
    fill_ext(core, own, intra, inter, ext)
    inv = 1.0 / (jnp.zeros(own.shape[1:], F32) + scal[1])
    for row in range(own.shape[0]):
        image_h, image_e = both_rows((index, signs), ext, ham, ovl, row)
        mine = own[row].astype(F32)
        out[row] = ((image_h - scal[0] * (mine + image_e)) * inv).astype(BF16)
    send_ends(core, out, intra_out, inter_out)


def term_kernel(ints, index, signs, own, inter, intra, ovl, out, inter_out, intra_out, ext):
    core = ints[0]
    fill_ext(core, own, intra, inter, ext)
    for row in range(own.shape[0]):
        out[row] = (-one_row((index, signs), ext, ovl, row)).astype(BF16)
    send_ends(core, out, intra_out, inter_out)


def update_kernel(first, ints, index, signs, own, inter, intra, scaled, *rest):
    if first:
        ovl, out, inter_out, intra_out, ext = rest
    else:
        previous, ovl, out, inter_out, intra_out, ext = rest
    core = ints[0]
    half = own.shape[0]
    fill_ext(core, own, intra, inter, ext)
    lane = lax.broadcasted_iota(jnp.int32, own.shape[1:], 1)
    for row in range(half):
        image = one_row((index, signs), ext, ovl, row)
        filtered = scaled[row].astype(F32) + own[row].astype(F32) - image
        if not first:
            filtered = 2.0 * filtered - previous[row].astype(F32)
        out[row] = jnp.where(lane < ints[4 + row], filtered, 0.0).astype(BF16)
    send_ends(core, out, intra_out, inter_out)


def images_kernel(ints, index, signs, own, inter, intra, ham, ovl, y_other, out, ext):
    del y_other
    core = ints[0]
    fill_ext(core, own, intra, inter, ext)
    half, _, orbs = own.shape
    for row in range(half):
        image_h, image_e = both_rows((index, signs), ext, ham, ovl, row)
        at = slice(row * orbs, (row + 1) * orbs)
        out[0, :, at] = (own[row].astype(F32) + image_e).astype(BF16)
        out[1, :, at] = image_h.astype(BF16)


def gram_kernel(chips, ints, *refs):
    images, groups = refs[:CORES], refs[CORES : CORES + CORES * chips]
    keep, send, both = refs[CORES + CORES * chips :]
    core, chip = ints[0], ints[1]
    half, local_vecs, _ = groups[0].shape
    vecs = CORES * local_vecs
    flat = jnp.concatenate(
        [jnp.concatenate([group[row] for row in range(half)], axis=1) for group in groups], axis=0
    )
    eye = lax.broadcasted_iota(jnp.int32, (vecs, vecs), 0) == lax.broadcasted_iota(
        jnp.int32, (vecs, vecs), 1
    )
    for matrix in range(2):
        mine = jnp.concatenate([image[matrix] for image in images], axis=0)
        pair = lax.dot_general(mine, flat, NT, preferred_element_type=F32)
        both[matrix, : vecs // 2, :] = packed(pair[:, :vecs]).astype(BF16)
        for step in range(1, chips):
            block = pair[:, step * vecs : (step + 1) * vecs]
            both[matrix, (2 * step - 1) * vecs // 2 : (2 * step + 1) * vecs // 2, :] = block.astype(BF16)
        diagonal = jnp.sum(jnp.where(eye, pair[:, :vecs], 0.0), axis=0, keepdims=True)
        both[matrix, (2 * chips - 1) * vecs // 2 :, :] = diagonal_parts(diagonal)
    keep[...] = both[core]
    send[...] = both[1 - core]


def packed(block):
    half = block.shape[0] // 2
    block = 0.5 * (block + block.T)
    top, bottom = block[:half], block[half:]
    bottom = jnp.concatenate([bottom[:, half:], bottom[:, :half]], axis=1)
    row = lax.broadcasted_iota(jnp.int32, top.shape, 0)
    lane = lax.broadcasted_iota(jnp.int32, top.shape, 1)
    return jnp.where((lane < half) & (lane > row), bottom, top)


def unpacked(block):
    half = block.shape[0]
    turned = block.T
    row = lax.broadcasted_iota(jnp.int32, (half, half), 0)
    lane = lax.broadcasted_iota(jnp.int32, (half, half), 1)
    square, beside = block[:, :half], block[:, half:]
    first = jnp.where(lane < row, square, turned[:half])
    last = jnp.where(lane > row, square, turned[:half])
    return jnp.concatenate(
        [
            jnp.concatenate([first, beside], axis=1),
            jnp.concatenate([turned[half:], last], axis=1),
        ],
        axis=0,
    )


def diagonal_parts(diagonal):
    high, middle, low = (part.astype(F32) for part in split3(diagonal))
    rows = lax.broadcasted_iota(jnp.int32, (DIAGONAL_ROWS, diagonal.shape[1]), 0)
    parts = jnp.where(rows == 0, high, jnp.where(rows == 1, middle, jnp.where(rows == 2, low, 0.0)))
    return parts.astype(BF16)


def diagonal_of(payload):
    parts = payload[payload.shape[0] - DIAGONAL_ROWS :, :].astype(F32)
    return parts[0:1] + (parts[1:2] + parts[2:3])


def add_kernel(left, right, out):
    body = left.shape[0] - DIAGONAL_ROWS
    out[:body] = (left[:body, :].astype(F32) + right[:body, :].astype(F32)).astype(BF16)
    out[body:] = diagonal_parts(diagonal_of(left) + diagonal_of(right))


def sum_kernel(ints, *refs):
    *payloads, out, held = refs
    count = len(payloads)
    for step, payload in enumerate(payloads):
        held[lax.rem(ints[DEVICE_ROW] + count - step, count)] = payload[...]
    body = out.shape[0] - DIAGONAL_ROWS
    total = held[0, :body, :].astype(F32)
    diagonal = diagonal_of(held.at[0])
    for r in range(1, count):
        total = total + held[r, :body, :].astype(F32)
        diagonal = diagonal + diagonal_of(held.at[r])
    out[:body] = total.astype(BF16)
    out[body:] = diagonal_parts(diagonal)


def split3(value):
    high = value.astype(BF16)
    rest = value - high.astype(F32)
    middle = rest.astype(BF16)
    low = (rest - middle.astype(F32)).astype(BF16)
    return high, middle, low


def panel_inverse(block):
    lane = lax.broadcasted_iota(jnp.int32, (PANEL, 128), 1)
    rows = lax.broadcasted_iota(jnp.int32, (PANEL, 128), 0)
    work = jnp.where(lane < PANEL, block, jnp.where(lax.rem(lane, PANEL) == rows, 1.0, 0.0))
    count = PANEL // SUBLANES
    pieces = [work[v * SUBLANES : (v + 1) * SUBLANES] for v in range(count)]
    sub = lax.broadcasted_iota(jnp.int32, (SUBLANES, 128), 0)

    def spread(value, k):
        return jnp.broadcast_to(value[k % SUBLANES : k % SUBLANES + 1], (SUBLANES, 128))

    pivots = [jnp.ones((SUBLANES, 128), F32) for _ in range(count)]
    for start, group in ((0, 16), (16, 16)):
        columns = {
            k: {
                v: jnp.broadcast_to(pieces[v][:, k : k + 1], (SUBLANES, 128))
                for v in range(start // SUBLANES, count)
            }
            for k in range(start, start + group)
        }
        at = spread(columns[start][start // SUBLANES], start)
        for k in range(start, start + group):
            here = k // SUBLANES
            pivots[here] = jnp.where(sub == k % SUBLANES, at, pivots[here])
            guess = pl.reciprocal(at, approx=True)
            correction = 2.0 - at * guess
            inv = guess * correction
            if k + 1 < start + group:
                below = (k + 1) // SUBLANES
                product = spread(columns[k][below], k + 1) * spread(columns[k + 1][here], k)
                at = spread(columns[k + 1][below], k + 1) - (product * guess) * correction
            factors = {v: columns[k][v] * inv for v in range(here, count)}
            factors[here] = jnp.where(sub > k % SUBLANES, factors[here], 0.0)
            for later in range(k + 1, start + group):
                top = spread(columns[later][here], k)
                for v in range(here, count):
                    columns[later][v] = columns[later][v] - factors[v] * top
            top = spread(pieces[here], k)
            for v in range(here, count):
                pieces[v] = pieces[v] - factors[v] * top
    pivot = jnp.concatenate(pivots, axis=0)
    root = lax.rsqrt(pivot)
    root = root * (1.5 - 0.5 * ((pivot * root) * root))
    return jnp.concatenate(pieces, axis=0) * root


def factor(work, inverse):
    size = work.shape[0]
    wide = lax.broadcasted_iota(jnp.int32, (PANEL, size), 1)
    tall = lax.broadcasted_iota(jnp.int32, (PANEL, size), 0)
    lane = lax.broadcasted_iota(jnp.int32, (PANEL, 128), 1)
    zero = jnp.zeros((PANEL, size), BF16)
    for start in range(0, size, PANEL):
        rows = work[start : start + PANEL, :]
        tile = start // 128 * 128
        block = work[start : start + PANEL, tile : tile + 128]
        if start % 128:
            block = pltpu.roll(block, 128 - start % 128, axis=1)
        t_high, t_mid, t_low = split3(jnp.where(lane < PANEL, 0.0, panel_inverse(block)))
        first = jnp.where(lane < 2 * PANEL, t_high, jnp.where(lane < 3 * PANEL, t_mid, t_low))
        second = jnp.where(lane < 2 * PANEL, t_high, jnp.where(lane < 3 * PANEL, t_mid, t_high))
        left = jnp.concatenate([first, second], axis=1)
        inside = (wide >= start) & (wide < start + PANEL)
        rows = jnp.where(inside, jnp.where(wide - start == tall, 1.0, 0.0), rows)
        r_high, r_mid, r_low = split3(rows)
        right = jnp.concatenate([zero, r_high, r_high, r_high, zero, r_mid, r_mid, r_low], axis=0)
        new = jnp.dot(left, right, preferred_element_type=F32)
        inverse[start : start + PANEL, :] = jnp.where(wide < start + PANEL, new, 0.0)
        after = start + PANEL
        if after < size:
            high, middle, low = split3(new)
            base = after // 128 * 128
            lhs = jnp.concatenate([high, high, middle, middle, high, low], axis=0)[:, base:]
            rhs = jnp.concatenate([high, middle, high, middle, low, high], axis=0)
            change = lax.dot_general(lhs, rhs, TN, preferred_element_type=F32)[after - base :]
            columns = lax.broadcasted_iota(jnp.int32, change.shape, 1)
            old = work[after:, :]
            work[after:, :] = jnp.where((columns >= start) & (columns < after), 0.0, old) - change


def finish_kernel(chips, scale, ints, *refs):
    mine, theirs = refs[:chips], refs[chips : 2 * chips]
    y_mine = refs[2 * chips : (2 + CORES) * chips]
    y_theirs = refs[(2 + CORES) * chips : (2 + 2 * CORES) * chips]
    basis, reduced, pair, work, inverse = refs[(2 + 2 * CORES) * chips :]
    core, chip, col = ints[0], ints[1], ints[2]
    half, local_vecs, orbs = y_mine[0].shape
    vecs = CORES * local_vecs
    eye = lax.broadcasted_iota(jnp.int32, (vecs, vecs), 0) == lax.broadcasted_iota(
        jnp.int32, (vecs, vecs), 1
    )
    for step in range(chips):
        which = lax.rem(chip + step, chips)
        rows = pl.ds(pl.multiple_of(which * vecs, vecs), vecs)
        for matrix, payload in ((core, mine[step]), (1 - core, theirs[step])):
            own_block = unpacked(payload[: vecs // 2, :].astype(F32))
            own_block = jnp.where(eye, diagonal_of(payload), own_block)
            for k in range(chips):
                block = own_block
                for away in range(1, chips):
                    at = (2 * away - 1) * vecs // 2
                    other = payload[at : at + vecs, :].astype(F32)
                    block = jnp.where(lax.rem(which + away, chips) == k, other, block)
                pair[matrix, rows, k * vecs : (k + 1) * vecs] = block
    work[...] = (pair[0] + pair[0].T) * scale
    factor(work, inverse)
    start = pl.multiple_of(col * local_vecs, local_vecs)
    own_rows = inverse[pl.ds(start, local_vecs), :]
    gram_h = (pair[1] + pair[1].T) * scale
    half_way = jnp.dot(
        own_rows, gram_h, precision=lax.Precision.HIGHEST, preferred_element_type=F32
    )
    reduced[...] = lax.dot_general(
        half_way, inverse[...], NT, precision=lax.Precision.HIGHEST, preferred_element_type=F32
    )
    rotation = own_rows.astype(BF16)
    turned = []
    for step in range(chips):
        which = lax.rem(chip + step, chips)
        part = rotation[:, :vecs]
        for k in range(1, chips):
            part = jnp.where(which == k, rotation[:, k * vecs : (k + 1) * vecs], part)
        turned.append(part)
    turned = jnp.concatenate(turned, axis=1)
    for which, group in ((core, y_mine), (1 - core, y_theirs)):
        for row in range(half):
            everything = jnp.concatenate([vectors[row] for vectors in group], axis=0)
            result = jnp.dot(turned, everything, preferred_element_type=F32).astype(BF16)
            at = pl.multiple_of((which * half + row) * orbs, orbs)
            basis[:, pl.ds(at, orbs)] = result


def local(
    trial_vectors,
    hamiltonian_blocks,
    correlation_offset,
    block_columns,
    block_phases,
    block_sizes,
    shift,
    halfwidth,
):
    blocks_dev, slots = block_columns.shape
    orbs = hamiltonian_blocks.shape[2]
    num_rows, num_cols = lax.axis_size("row"), lax.axis_size("col")
    total_blocks = blocks_dev * num_rows
    half = blocks_dev // CORES
    chips = num_cols // CORES
    local_vecs = trial_vectors.shape[0]
    vecs = local_vecs * CORES
    size = local_vecs * num_cols
    row, col = lax.axis_index("row"), lax.axis_index("col")
    core, chip = lax.rem(col, CORES), lax.div(col, CORES)

    def swap_cores(value):
        return lax.ppermute(value, "col", [(c, c ^ 1) for c in range(num_cols)])

    def swap_chips(value):
        pairs = []
        for r in range(num_rows):
            for x in range(chips):
                upper = r * num_cols + x * CORES + 1
                lower = (r + 1) % num_rows * num_cols + x * CORES
                pairs += [(upper, lower), (lower, upper)]
        return lax.ppermute(value, ("row", "col"), pairs)

    def next_chips(value):
        pairs = []
        for r in range(num_rows):
            for c in range(num_cols):
                to = (r + 1 if c % CORES == 0 else r - 1) % num_rows
                pairs.append((r * num_cols + c, to * num_cols + c))
        return lax.ppermute(value, ("row", "col"), pairs)

    def from_chip(value, step):
        pairs = [((c + step * CORES) % num_cols, c) for c in range(num_cols)]
        return lax.ppermute(value, "col", pairs)

    state = jax.ShapeDtypeStruct((half, local_vecs, orbs), BF16)
    end = jax.ShapeDtypeStruct((HALF_BAND, local_vecs, orbs), BF16)
    ext = pltpu.VMEM((half + 2 * HALF_BAND, local_vecs, orbs), BF16)
    params = pltpu.CompilerParams(vmem_limit_bytes=16 << 20)
    row_flops = SLOWER * 2 * half * slots * local_vecs * orbs * orbs

    def call(kernel, name, scalars, arrays, outs, scratch, flops):
        return pl.pallas_call(
            kernel,
            name=name,
            out_shape=outs,
            in_specs=[SMEM] * len(scalars) + [VMEM] * len(arrays),
            out_specs=(VMEM,) * len(outs),
            scratch_shapes=scratch,
            compiler_params=params,
            cost_estimate=pl.CostEstimate(
                flops=flops, bytes_accessed=flops // 128, transcendentals=0
            ),
        )(*scalars, *arrays)

    def step_call(kernel, name, scalars, arrays, flops):
        return call(kernel, name, scalars, arrays, (state, end, end), [ext], flops)

    def exchange(ends):
        return swap_chips(ends[0]), swap_cores(ends[1])

    def scalars(value):
        return pltpu.with_memory_space_constraint(value, pltpu.SMEM)

    ints = scalars(jnp.stack([core, chip, col, row * blocks_dev, row]).astype(jnp.int32))
    shift, halfwidth = scalars(shift), scalars(halfwidth)

    def stays(value):
        return pltpu.with_memory_space_constraint(value, pltpu.HBM)

    more = jax.ShapeDtypeStruct((half + HALF_BAND, local_vecs, orbs), BF16)
    own, near, give, far, across = pl.pallas_call(
        cut_kernel,
        name="cut",
        out_shape=(state, end, more, end, end),
        in_specs=[SMEM, HBM, HBM],
        out_specs=(VMEM,) * 5,
        scratch_shapes=[
            pltpu.SMEM(block_sizes.shape, jnp.int32),
            pltpu.VMEM(trial_vectors.shape, BF16),
            pltpu.VMEM((blocks_dev, local_vecs, orbs), BF16),
            pltpu.SemaphoreType.DMA((2,)),
        ],
        compiler_params=params,
    )(ints, stays(block_sizes), stays(trial_vectors))
    far, across = next_chips(far), swap_chips(across)
    got = swap_cores(give)
    matrix = vmem((half, *hamiltonian_blocks.shape[1:]), BF16)
    ham, ovl, index, signs, place, scal = pl.pallas_call(
        functools.partial(load_kernel, total_blocks),
        name="load",
        out_shape=(
            matrix,
            matrix,
            pltpu.SMEM((half, slots), jnp.int32),
            pltpu.SMEM((half, slots), F32),
            pltpu.SMEM((4 + half,), jnp.int32),
            pltpu.SMEM((2,), F32),
        ),
        in_specs=[SMEM] * 3 + [HBM] * 5,
        out_specs=(VMEM, VMEM, SMEM, SMEM, SMEM, SMEM),
        scratch_shapes=[
            pltpu.SMEM(block_columns.shape, jnp.int32),
            pltpu.SMEM(block_phases.shape, jnp.int32),
            pltpu.SMEM(block_sizes.shape, jnp.int32),
            pltpu.SemaphoreType.DMA((2, half)),
            pltpu.SemaphoreType.DMA((3,)),
        ],
        compiler_params=params,
        cost_estimate=pl.CostEstimate(
            flops=0, bytes_accessed=4 * hamiltonian_blocks.size, transcendentals=0
        ),
    )(
        ints,
        shift,
        halfwidth,
        stays(block_columns),
        stays(block_phases),
        stays(block_sizes),
        stays(hamiltonian_blocks),
        stays(correlation_offset),
    )
    got_own = lax.dynamic_slice_in_dim(got, HALF_BAND * core, half, 0)
    got_near = lax.dynamic_slice_in_dim(got, half * (1 - core), HALF_BAND, 0)

    def by_group(mine, other):
        return [jnp.where(core == 0, mine, other), jnp.where(core == 0, other, mine)]

    current = by_group(own, got_own)
    halo = list(zip(by_group(far, across), by_group(near, got_near)))
    table = (place, index, signs)
    scaled, term, previous = [None] * CORES, [None] * CORES, list(current)
    for degree in range(DEGREE):
        for g in range(CORES):
            if g > 0:
                current[g], scaled[0] = lax.optimization_barrier((current[g], scaled[0]))
            scaled[g], *ends = step_call(
                scaled_kernel,
                "scaled",
                (*table, scal),
                (current[g], *halo[g], ham, ovl),
                2 * row_flops,
            )
            halo[g] = exchange(ends)
        for g in range(CORES):
            term[g], *ends = step_call(
                term_kernel, "term", table, (scaled[g], *halo[g], ovl), row_flops
            )
            halo[g] = exchange(ends)
        for g in range(CORES):
            first = degree == 0
            arrays = (term[g], *halo[g], scaled[g]) + (() if first else (previous[g],)) + (ovl,)
            updated, *ends = step_call(
                functools.partial(update_kernel, first),
                "update",
                table,
                arrays,
                row_flops,
            )
            halo[g] = exchange(ends)
            previous[g], current[g] = current[g], updated

    y_others = [from_chip(value, step) for step in range(1, chips) for value in current]
    image = jax.ShapeDtypeStruct((2, local_vecs, half * orbs), BF16)
    images = []
    for g, vectors in enumerate(current):
        if g > 0:
            vectors, images[0] = lax.optimization_barrier((vectors, images[0]))
        images += call(
            images_kernel,
            "images",
            table,
            (vectors, *halo[g], ham, ovl, y_others[0]),
            (image,),
            [ext],
            2 * row_flops,
        )
    payload = jax.ShapeDtypeStruct((size - vecs // 2 + DIAGONAL_ROWS, vecs), BF16)
    keep, send = call(
        functools.partial(gram_kernel, chips),
        "gram",
        (place,),
        (*images, *current, *y_others),
        (payload, payload),
        [pltpu.VMEM((2, *payload.shape), BF16)],
        row_flops,
    )

    def add(left, right):
        return call(add_kernel, "add", (), (left, right), (payload,), [], row_flops // 8)[0]

    summed = add(keep, swap_cores(send))
    if num_rows <= 4:
        others = [
            lax.ppermute(summed, "row", [(r, (r + step) % num_rows) for r in range(num_rows)])
            for step in range(1, num_rows)
        ]
        (summed,) = call(
            sum_kernel,
            "sum",
            (place,),
            (summed, *others),
            (payload,),
            [pltpu.VMEM((num_rows, *payload.shape), BF16)],
            row_flops // 8,
        )
    elif num_rows & (num_rows - 1):
        every = lax.all_gather(summed, "row")
        summed = every[0]
        for r in range(1, num_rows):
            summed = add(summed, every[r])
    else:
        bit = 1
        while bit < num_rows:
            other = lax.ppermute(summed, "row", [(r, r ^ bit) for r in range(num_rows)])
            summed = add(summed, other)
            bit *= 2
    mine = [summed] + [from_chip(summed, step) for step in range(1, chips)]
    theirs = [swap_cores(value) for value in mine]
    y_theirs = [swap_cores(value) for value in (*current, *y_others)]
    basis, reduced = call(
        functools.partial(finish_kernel, chips, 0.5 / (total_blocks * orbs)),
        "finish",
        (place,),
        (*mine, *theirs, *current, *y_others, *y_theirs),
        (
            jax.ShapeDtypeStruct((local_vecs, blocks_dev * orbs), BF16),
            jax.ShapeDtypeStruct((local_vecs, size), F32),
        ),
        [
            pltpu.VMEM((2, size, size), F32),
            pltpu.VMEM((size, size), F32),
            pltpu.VMEM((size, size), F32),
        ],
        10 * row_flops,
    )
    return basis, reduced.T


def solution(mesh):
    return jax.shard_map(
        local,
        mesh=mesh,
        in_specs=(
            P("col", ("pool", "row")),
            P(("pool", "row"), None, None, None),
            P(("pool", "row"), None, None, None),
            P(("pool", "row"), None),
            P(("pool", "row"), None),
            P(("pool", "row")),
            P("pool"),
            P("pool"),
        ),
        out_specs=(P("col", ("pool", "row")), P("pool", "col")),
        check_vma=False,
    )
```

```python
import functools

import jax
import jax.numpy as jnp
from jax import lax
from jax.experimental import pallas as pl
from jax.experimental.pallas import tpu as pltpu
from jax.sharding import PartitionSpec as P

HALF_BAND = 5
DEGREE = 4
CORES = 2
PANEL = 32
SLOWER = 24
SUBLANES = 8
DIAGONAL_ROWS = 16
DEVICE_ROW = 3

BF16 = jnp.bfloat16
F32 = jnp.float32
NT = (((1,), (1,)), ((), ()))
TN = (((0,), (0,)), ((), ()))

SMEM = pl.BlockSpec(memory_space=pltpu.SMEM)
VMEM = pl.BlockSpec(memory_space=pltpu.VMEM)
HBM = pl.BlockSpec(memory_space=pltpu.HBM)


def vmem(shape, dtype):
    return pltpu.VMEM(shape, dtype)


def fill_ext(core, own, intra, inter, ext):
    half = own.shape[0]
    ext[HALF_BAND : HALF_BAND + half] = own[...]
    ext[pl.ds((half + HALF_BAND) * (1 - core), HALF_BAND)] = intra[...]
    ext[pl.ds((half + HALF_BAND) * core, HALF_BAND)] = inter[...]


def picked(table, ext, row):
    index, signs = table
    slots = index.shape[1]
    return jnp.concatenate(
        [ext[index[row, s]] * signs[row, s].astype(BF16) for s in range(slots)], axis=1
    )


def row_matrix(blocks, row):
    return jnp.concatenate([blocks[row, s] for s in range(blocks.shape[1])], axis=1)


def send_ends(core, full, intra_out, inter_out):
    spare = full.shape[0] - HALF_BAND
    intra_out[...] = full[pl.ds(spare * (1 - core), HALF_BAND)]
    inter_out[...] = full[pl.ds(spare * core, HALF_BAND)]


def image_of(table, ext, matrices, row):
    matrix = jnp.concatenate([row_matrix(blocks, row) for blocks in matrices], axis=0)
    return lax.dot_general(matrix, picked(table, ext, row), NT, preferred_element_type=F32)


def both_rows(table, ext, ham, ovl, row):
    orbs = ham.shape[2]
    image = image_of(table, ext, (ham, ovl), row)
    return image[:orbs].T, image[orbs:].T


def one_row(table, ext, ovl, row):
    return image_of(table, ext, (ovl,), row).T


def cut_kernel(ints, sizes, trial, own, near, give, far, across, sizes_here, here, masked, sems):
    copies = [
        pltpu.make_async_copy(sizes, sizes_here, sems.at[0]),
        pltpu.make_async_copy(trial, here, sems.at[1]),
    ]
    for copy in copies:
        copy.start()
    for copy in copies:
        copy.wait()
    half, _, orbs = own.shape
    core = ints[0]
    lane = lax.broadcasted_iota(jnp.int32, own.shape[1:], 1)
    for row in range(2 * half):
        values = here[:, row * orbs : (row + 1) * orbs].astype(F32)
        masked[row] = jnp.where(lane < sizes_here[row], values, 0.0).astype(BF16)
    spare = half - HALF_BAND
    last = 2 * half - HALF_BAND
    own[...] = masked[pl.ds(half * core, half)]
    near[...] = masked[pl.ds(half - HALF_BAND * core, HALF_BAND)]
    give[...] = masked[pl.ds(spare * (1 - core), half + HALF_BAND)]
    far[...] = masked[pl.ds(last * (1 - core), HALF_BAND)]
    across[...] = masked[pl.ds(last * core, HALF_BAND)]


def load_kernel(total, ints, shift, width, columns, phases, sizes, ham, ovl, *rest):
    ham_out, ovl_out, index, signs, place, scal, columns_here, phases_here, sizes_here = rest[:9]
    sems, more_sems = rest[9:]
    half, slots = index.shape
    first = ints[0] * half
    small = [
        pltpu.make_async_copy(source, target, more_sems.at[i])
        for i, (source, target) in enumerate(
            ((columns, columns_here), (phases, phases_here), (sizes, sizes_here))
        )
    ]
    large = [
        pltpu.make_async_copy(source.at[first + row], target.at[row], sems.at[matrix, row])
        for row in range(half)
        for matrix, (source, target) in enumerate(((ham, ham_out), (ovl, ovl_out)))
    ]
    for copy in small + large:
        copy.start()
    scal[0] = shift[0]
    scal[1] = width[0]
    for i in range(3):
        place[i] = ints[i]
    place[DEVICE_ROW] = ints[4]
    for copy in small:
        copy.wait()
    start = ints[3] + first

    def fill(row, _):
        place[4 + row] = sizes_here[first + row]
        for slot in range(slots):
            away = columns_here[first + row, slot] - (start + row) + HALF_BAND
            away = jnp.where(away < 0, away + total, away)
            away = jnp.where(away >= total, away - total, away)
            index[row, slot] = row + away
            signs[row, slot] = (1 - 2 * phases_here[first + row, slot]).astype(F32)
        return 0

    lax.fori_loop(0, half, fill, 0)
    for copy in large:
        copy.wait()


def scaled_kernel(
    ints, index, signs, scal, own, inter, intra, ham, ovl, out, inter_out, intra_out, ext
):
    core = ints[0]
    fill_ext(core, own, intra, inter, ext)
    inv = 1.0 / (jnp.zeros(own.shape[1:], F32) + scal[1])
    for row in range(own.shape[0]):
        image_h, image_e = both_rows((index, signs), ext, ham, ovl, row)
        mine = own[row].astype(F32)
        out[row] = ((image_h - scal[0] * (mine + image_e)) * inv).astype(BF16)
    send_ends(core, out, intra_out, inter_out)


def term_kernel(ints, index, signs, own, inter, intra, ovl, out, inter_out, intra_out, ext):
    core = ints[0]
    fill_ext(core, own, intra, inter, ext)
    for row in range(own.shape[0]):
        out[row] = (-one_row((index, signs), ext, ovl, row)).astype(BF16)
    send_ends(core, out, intra_out, inter_out)


def update_kernel(first, ints, index, signs, own, inter, intra, scaled, *rest):
    if first:
        ovl, out, inter_out, intra_out, ext = rest
    else:
        previous, ovl, out, inter_out, intra_out, ext = rest
    core = ints[0]
    half = own.shape[0]
    fill_ext(core, own, intra, inter, ext)
    lane = lax.broadcasted_iota(jnp.int32, own.shape[1:], 1)
    for row in range(half):
        image = one_row((index, signs), ext, ovl, row)
        filtered = scaled[row].astype(F32) + own[row].astype(F32) - image
        if not first:
            filtered = 2.0 * filtered - previous[row].astype(F32)
        out[row] = jnp.where(lane < ints[4 + row], filtered, 0.0).astype(BF16)
    send_ends(core, out, intra_out, inter_out)


def images_kernel(ints, index, signs, own, inter, intra, ham, ovl, y_other, out, ext):
    del y_other
    core = ints[0]
    fill_ext(core, own, intra, inter, ext)
    half, _, orbs = own.shape
    for row in range(half):
        image_h, image_e = both_rows((index, signs), ext, ham, ovl, row)
        at = slice(row * orbs, (row + 1) * orbs)
        out[0, :, at] = (own[row].astype(F32) + image_e).astype(BF16)
        out[1, :, at] = image_h.astype(BF16)


def gram_kernel(chips, ints, *refs):
    images, groups = refs[:CORES], refs[CORES : CORES + CORES * chips]
    keep, send, both = refs[CORES + CORES * chips :]
    core, chip = ints[0], ints[1]
    half, local_vecs, _ = groups[0].shape
    vecs = CORES * local_vecs
    flat = jnp.concatenate(
        [jnp.concatenate([group[row] for row in range(half)], axis=1) for group in groups], axis=0
    )
    eye = lax.broadcasted_iota(jnp.int32, (vecs, vecs), 0) == lax.broadcasted_iota(
        jnp.int32, (vecs, vecs), 1
    )
    for matrix in range(2):
        mine = jnp.concatenate([image[matrix] for image in images], axis=0)
        pair = lax.dot_general(mine, flat, NT, preferred_element_type=F32)
        both[matrix, : vecs // 2, :] = packed(pair[:, :vecs]).astype(BF16)
        for step in range(1, chips):
            block = pair[:, step * vecs : (step + 1) * vecs]
            both[matrix, (2 * step - 1) * vecs // 2 : (2 * step + 1) * vecs // 2, :] = block.astype(BF16)
        diagonal = jnp.sum(jnp.where(eye, pair[:, :vecs], 0.0), axis=0, keepdims=True)
        both[matrix, (2 * chips - 1) * vecs // 2 :, :] = diagonal_parts(diagonal)
    keep[...] = both[core]
    send[...] = both[1 - core]


def packed(block):
    half = block.shape[0] // 2
    block = 0.5 * (block + block.T)
    top, bottom = block[:half], block[half:]
    bottom = jnp.concatenate([bottom[:, half:], bottom[:, :half]], axis=1)
    row = lax.broadcasted_iota(jnp.int32, top.shape, 0)
    lane = lax.broadcasted_iota(jnp.int32, top.shape, 1)
    return jnp.where((lane < half) & (lane > row), bottom, top)


def unpacked(block):
    half = block.shape[0]
    turned = block.T
    row = lax.broadcasted_iota(jnp.int32, (half, half), 0)
    lane = lax.broadcasted_iota(jnp.int32, (half, half), 1)
    square, beside = block[:, :half], block[:, half:]
    first = jnp.where(lane < row, square, turned[:half])
    last = jnp.where(lane > row, square, turned[:half])
    return jnp.concatenate(
        [
            jnp.concatenate([first, beside], axis=1),
            jnp.concatenate([turned[half:], last], axis=1),
        ],
        axis=0,
    )


def diagonal_parts(diagonal):
    high, middle, low = (part.astype(F32) for part in split3(diagonal))
    rows = lax.broadcasted_iota(jnp.int32, (DIAGONAL_ROWS, diagonal.shape[1]), 0)
    parts = jnp.where(rows == 0, high, jnp.where(rows == 1, middle, jnp.where(rows == 2, low, 0.0)))
    return parts.astype(BF16)


def diagonal_of(payload):
    parts = payload[payload.shape[0] - DIAGONAL_ROWS :, :].astype(F32)
    return parts[0:1] + (parts[1:2] + parts[2:3])


def add_kernel(left, right, out):
    body = left.shape[0] - DIAGONAL_ROWS
    out[:body] = (left[:body, :].astype(F32) + right[:body, :].astype(F32)).astype(BF16)
    out[body:] = diagonal_parts(diagonal_of(left) + diagonal_of(right))


def sum_kernel(ints, *refs):
    *payloads, out, held = refs
    count = len(payloads)
    for step, payload in enumerate(payloads):
        held[lax.bitwise_xor(ints[DEVICE_ROW], jnp.int32(step))] = payload[...]
    body = out.shape[0] - DIAGONAL_ROWS
    total = held[0, :body, :].astype(F32)
    diagonal = diagonal_of(held.at[0])
    for r in range(1, count):
        total = total + held[r, :body, :].astype(F32)
        diagonal = diagonal + diagonal_of(held.at[r])
    out[:body] = total.astype(BF16)
    out[body:] = diagonal_parts(diagonal)


def split3(value):
    high = value.astype(BF16)
    rest = value - high.astype(F32)
    middle = rest.astype(BF16)
    low = (rest - middle.astype(F32)).astype(BF16)
    return high, middle, low


def three_terms(left, right, axis):
    (high, middle, _), (other, little, _) = split3(left), split3(right)
    return (
        jnp.concatenate([high, high, middle], axis=1),
        jnp.concatenate([other, little, other], axis=axis),
    )


def panel_inverse(block):
    lane = lax.broadcasted_iota(jnp.int32, (PANEL, 128), 1)
    rows = lax.broadcasted_iota(jnp.int32, (PANEL, 128), 0)
    work = jnp.where(lane < PANEL, block, jnp.where(lax.rem(lane, PANEL) == rows, 1.0, 0.0))
    count = PANEL // SUBLANES
    pieces = [work[v * SUBLANES : (v + 1) * SUBLANES] for v in range(count)]
    sub = lax.broadcasted_iota(jnp.int32, (SUBLANES, 128), 0)

    def spread(value, k):
        return jnp.broadcast_to(value[k % SUBLANES : k % SUBLANES + 1], (SUBLANES, 128))

    pivots = [jnp.ones((SUBLANES, 128), F32) for _ in range(count)]
    for start, group in ((0, 8), (8, 8), (16, 16)):
        columns = {
            k: {
                v: jnp.broadcast_to(pieces[v][:, k : k + 1], (SUBLANES, 128))
                for v in range(start // SUBLANES, count)
            }
            for k in range(start, start + group)
        }
        at = spread(columns[start][start // SUBLANES], start)
        for k in range(start, start + group):
            here = k // SUBLANES
            pivots[here] = jnp.where(sub == k % SUBLANES, at, pivots[here])
            guess = pl.reciprocal(at, approx=True)
            correction = 2.0 - at * guess
            inv = guess * correction
            if k + 1 < start + group:
                below = (k + 1) // SUBLANES
                product = spread(columns[k][below], k + 1) * spread(columns[k + 1][here], k)
                at = spread(columns[k + 1][below], k + 1) - (product * guess) * correction
            factors = {v: columns[k][v] * inv for v in range(here, count)}
            factors[here] = jnp.where(sub > k % SUBLANES, factors[here], 0.0)
            for later in range(k + 1, start + group):
                top = spread(columns[later][here], k)
                for v in range(here, count):
                    columns[later][v] = columns[later][v] - factors[v] * top
            top = spread(pieces[here], k)
            for v in range(here, count):
                pieces[v] = pieces[v] - factors[v] * top
    pivot = jnp.concatenate(pivots, axis=0)
    root = lax.rsqrt(pivot)
    root = root * (1.5 - 0.5 * ((pivot * root) * root))
    return jnp.concatenate(pieces, axis=0) * root


def factor(work, inverse):
    size = work.shape[0]
    wide = lax.broadcasted_iota(jnp.int32, (PANEL, size), 1)
    tall = lax.broadcasted_iota(jnp.int32, (PANEL, size), 0)
    lane = lax.broadcasted_iota(jnp.int32, (PANEL, 128), 1)
    zero = jnp.zeros((PANEL, size), BF16)
    for start in range(0, size, PANEL):
        rows = work[start : start + PANEL, :]
        tile = start // 128 * 128
        block = work[start : start + PANEL, tile : tile + 128]
        if start % 128:
            block = pltpu.roll(block, 128 - start % 128, axis=1)
        t_high, t_mid, t_low = split3(jnp.where(lane < PANEL, 0.0, panel_inverse(block)))
        first = jnp.where(lane < 2 * PANEL, t_high, jnp.where(lane < 3 * PANEL, t_mid, t_low))
        second = jnp.where(lane < 2 * PANEL, t_high, jnp.where(lane < 3 * PANEL, t_mid, t_high))
        left = jnp.concatenate([first, second], axis=1)
        inside = (wide >= start) & (wide < start + PANEL)
        rows = jnp.where(inside, jnp.where(wide - start == tall, 1.0, 0.0), rows)
        r_high, r_mid, r_low = split3(rows)
        right = jnp.concatenate([zero, r_high, r_high, r_high, zero, r_mid, r_mid, r_low], axis=0)
        new = jnp.dot(left, right, preferred_element_type=F32)
        inverse[start : start + PANEL, :] = jnp.where(wide < start + PANEL, new, 0.0)
        after = start + PANEL
        if after < size:
            high, middle, low = split3(new)
            base = after // 128 * 128
            lhs = jnp.concatenate([high, high, middle, middle, high, low], axis=0)[:, base:]
            rhs = jnp.concatenate([high, middle, high, middle, low, high], axis=0)
            change = lax.dot_general(lhs, rhs, TN, preferred_element_type=F32)[after - base :]
            columns = lax.broadcasted_iota(jnp.int32, change.shape, 1)
            old = work[after:, :]
            work[after:, :] = jnp.where((columns >= start) & (columns < after), 0.0, old) - change


def finish_kernel(chips, scale, ints, *refs):
    mine, theirs = refs[:chips], refs[chips : 2 * chips]
    y_mine = refs[2 * chips : (2 + CORES) * chips]
    y_theirs = refs[(2 + CORES) * chips : (2 + 2 * CORES) * chips]
    basis, reduced, pair, work, inverse = refs[(2 + 2 * CORES) * chips :]
    core, chip, col = ints[0], ints[1], ints[2]
    half, local_vecs, orbs = y_mine[0].shape
    vecs = CORES * local_vecs
    eye = lax.broadcasted_iota(jnp.int32, (vecs, vecs), 0) == lax.broadcasted_iota(
        jnp.int32, (vecs, vecs), 1
    )
    for step in range(chips):
        which = lax.rem(chip + step, chips)
        rows = pl.ds(pl.multiple_of(which * vecs, vecs), vecs)
        for matrix, payload in ((core, mine[step]), (1 - core, theirs[step])):
            own_block = unpacked(payload[: vecs // 2, :].astype(F32))
            own_block = jnp.where(eye, diagonal_of(payload), own_block)
            for k in range(chips):
                block = own_block
                for away in range(1, chips):
                    at = (2 * away - 1) * vecs // 2
                    other = payload[at : at + vecs, :].astype(F32)
                    block = jnp.where(lax.rem(which + away, chips) == k, other, block)
                pair[matrix, rows, k * vecs : (k + 1) * vecs] = block
    work[...] = (pair[0] + pair[0].T) * scale
    factor(work, inverse)
    start = pl.multiple_of(col * local_vecs, local_vecs)
    own_rows = inverse[pl.ds(start, local_vecs), :]
    gram_h = (pair[1] + pair[1].T) * scale
    half_way = jnp.dot(*three_terms(own_rows, gram_h, 0), preferred_element_type=F32)
    reduced[...] = lax.dot_general(
        *three_terms(half_way, inverse[...], 1), NT, preferred_element_type=F32
    )
    rotation = own_rows.astype(BF16)
    turned = []
    for step in range(chips):
        which = lax.rem(chip + step, chips)
        part = rotation[:, :vecs]
        for k in range(1, chips):
            part = jnp.where(which == k, rotation[:, k * vecs : (k + 1) * vecs], part)
        turned.append(part)
    turned = jnp.concatenate(turned, axis=1)
    for which, group in ((core, y_mine), (1 - core, y_theirs)):
        for row in range(half):
            everything = jnp.concatenate([vectors[row] for vectors in group], axis=0)
            result = jnp.dot(turned, everything, preferred_element_type=F32).astype(BF16)
            at = pl.multiple_of((which * half + row) * orbs, orbs)
            basis[:, pl.ds(at, orbs)] = result


def local(
    trial_vectors,
    hamiltonian_blocks,
    correlation_offset,
    block_columns,
    block_phases,
    block_sizes,
    shift,
    halfwidth,
):
    blocks_dev, slots = block_columns.shape
    orbs = hamiltonian_blocks.shape[2]
    num_rows, num_cols = lax.axis_size("row"), lax.axis_size("col")
    total_blocks = blocks_dev * num_rows
    half = blocks_dev // CORES
    chips = num_cols // CORES
    local_vecs = trial_vectors.shape[0]
    vecs = local_vecs * CORES
    size = local_vecs * num_cols
    row, col = lax.axis_index("row"), lax.axis_index("col")
    core, chip = lax.rem(col, CORES), lax.div(col, CORES)

    def swap_cores(value):
        return lax.ppermute(value, "col", [(c, c ^ 1) for c in range(num_cols)])

    def swap_chips(value):
        pairs = []
        for r in range(num_rows):
            for x in range(chips):
                upper = r * num_cols + x * CORES + 1
                lower = (r + 1) % num_rows * num_cols + x * CORES
                pairs += [(upper, lower), (lower, upper)]
        return lax.ppermute(value, ("row", "col"), pairs)

    def next_chips(value):
        pairs = []
        for r in range(num_rows):
            for c in range(num_cols):
                to = (r + 1 if c % CORES == 0 else r - 1) % num_rows
                pairs.append((r * num_cols + c, to * num_cols + c))
        return lax.ppermute(value, ("row", "col"), pairs)

    def from_chip(value, step):
        pairs = [((c + step * CORES) % num_cols, c) for c in range(num_cols)]
        return lax.ppermute(value, "col", pairs)

    state = jax.ShapeDtypeStruct((half, local_vecs, orbs), BF16)
    end = jax.ShapeDtypeStruct((HALF_BAND, local_vecs, orbs), BF16)
    ext = pltpu.VMEM((half + 2 * HALF_BAND, local_vecs, orbs), BF16)
    params = pltpu.CompilerParams(vmem_limit_bytes=16 << 20)
    row_flops = SLOWER * 2 * half * slots * local_vecs * orbs * orbs

    def call(kernel, name, scalars, arrays, outs, scratch, flops):
        return pl.pallas_call(
            kernel,
            name=name,
            out_shape=outs,
            in_specs=[SMEM] * len(scalars) + [VMEM] * len(arrays),
            out_specs=(VMEM,) * len(outs),
            scratch_shapes=scratch,
            compiler_params=params,
            cost_estimate=pl.CostEstimate(
                flops=flops, bytes_accessed=flops // 128, transcendentals=0
            ),
        )(*scalars, *arrays)

    def step_call(kernel, name, scalars, arrays, flops):
        return call(kernel, name, scalars, arrays, (state, end, end), [ext], flops)

    def exchange(ends):
        return swap_chips(ends[0]), swap_cores(ends[1])

    def scalars(value):
        return pltpu.with_memory_space_constraint(value, pltpu.SMEM)

    ints = scalars(jnp.stack([core, chip, col, row * blocks_dev, row]).astype(jnp.int32))
    shift, halfwidth = scalars(shift), scalars(halfwidth)

    def stays(value):
        return pltpu.with_memory_space_constraint(value, pltpu.HBM)

    more = jax.ShapeDtypeStruct((half + HALF_BAND, local_vecs, orbs), BF16)
    own, near, give, far, across = pl.pallas_call(
        cut_kernel,
        name="cut",
        out_shape=(state, end, more, end, end),
        in_specs=[SMEM, HBM, HBM],
        out_specs=(VMEM,) * 5,
        scratch_shapes=[
            pltpu.SMEM(block_sizes.shape, jnp.int32),
            pltpu.VMEM(trial_vectors.shape, BF16),
            pltpu.VMEM((blocks_dev, local_vecs, orbs), BF16),
            pltpu.SemaphoreType.DMA((2,)),
        ],
        compiler_params=params,
    )(ints, stays(block_sizes), stays(trial_vectors))
    far, across = next_chips(far), swap_chips(across)
    got = swap_cores(give)
    matrix = vmem((half, *hamiltonian_blocks.shape[1:]), BF16)
    ham, ovl, index, signs, place, scal = pl.pallas_call(
        functools.partial(load_kernel, total_blocks),
        name="load",
        out_shape=(
            matrix,
            matrix,
            pltpu.SMEM((half, slots), jnp.int32),
            pltpu.SMEM((half, slots), F32),
            pltpu.SMEM((4 + half,), jnp.int32),
            pltpu.SMEM((2,), F32),
        ),
        in_specs=[SMEM] * 3 + [HBM] * 5,
        out_specs=(VMEM, VMEM, SMEM, SMEM, SMEM, SMEM),
        scratch_shapes=[
            pltpu.SMEM(block_columns.shape, jnp.int32),
            pltpu.SMEM(block_phases.shape, jnp.int32),
            pltpu.SMEM(block_sizes.shape, jnp.int32),
            pltpu.SemaphoreType.DMA((2, half)),
            pltpu.SemaphoreType.DMA((3,)),
        ],
        compiler_params=params,
        cost_estimate=pl.CostEstimate(
            flops=0, bytes_accessed=4 * hamiltonian_blocks.size, transcendentals=0
        ),
    )(
        ints,
        shift,
        halfwidth,
        stays(block_columns),
        stays(block_phases),
        stays(block_sizes),
        stays(hamiltonian_blocks),
        stays(correlation_offset),
    )
    got_own = lax.dynamic_slice_in_dim(got, HALF_BAND * core, half, 0)
    got_near = lax.dynamic_slice_in_dim(got, half * (1 - core), HALF_BAND, 0)

    def by_group(mine, other):
        return [jnp.where(core == 0, mine, other), jnp.where(core == 0, other, mine)]

    current = by_group(own, got_own)
    halo = list(zip(by_group(far, across), by_group(near, got_near)))
    table = (place, index, signs)
    scaled, term, previous = [None] * CORES, [None] * CORES, list(current)
    for degree in range(DEGREE):
        for g in range(CORES):
            if g > 0:
                current[g], scaled[0] = lax.optimization_barrier((current[g], scaled[0]))
            scaled[g], *ends = step_call(
                scaled_kernel,
                "scaled",
                (*table, scal),
                (current[g], *halo[g], ham, ovl),
                2 * row_flops,
            )
            halo[g] = exchange(ends)
        for g in range(CORES):
            term[g], *ends = step_call(
                term_kernel, "term", table, (scaled[g], *halo[g], ovl), row_flops
            )
            halo[g] = exchange(ends)
        for g in range(CORES):
            first = degree == 0
            arrays = (term[g], *halo[g], scaled[g]) + (() if first else (previous[g],)) + (ovl,)
            updated, *ends = step_call(
                functools.partial(update_kernel, first),
                "update",
                table,
                arrays,
                row_flops,
            )
            halo[g] = exchange(ends)
            previous[g], current[g] = current[g], updated

    y_others = [from_chip(value, step) for step in range(1, chips) for value in current]
    image = jax.ShapeDtypeStruct((2, local_vecs, half * orbs), BF16)
    images = []
    for g, vectors in enumerate(current):
        if g > 0:
            vectors, images[0] = lax.optimization_barrier((vectors, images[0]))
        images += call(
            images_kernel,
            "images",
            table,
            (vectors, *halo[g], ham, ovl, y_others[0]),
            (image,),
            [ext],
            2 * row_flops,
        )
    payload = jax.ShapeDtypeStruct((size - vecs // 2 + DIAGONAL_ROWS, vecs), BF16)
    keep, send = call(
        functools.partial(gram_kernel, chips),
        "gram",
        (place,),
        (*images, *current, *y_others),
        (payload, payload),
        [pltpu.VMEM((2, *payload.shape), BF16)],
        row_flops,
    )

    def add(left, right):
        return call(add_kernel, "add", (), (left, right), (payload,), [], row_flops // 8)[0]

    summed = add(keep, swap_cores(send))
    if num_rows in (2, 4):
        others = [
            lax.ppermute(summed, "row", [(r, r ^ step) for r in range(num_rows)])
            for step in range(1, num_rows)
        ]
        (summed,) = call(
            sum_kernel,
            "sum",
            (place,),
            (summed, *others),
            (payload,),
            [pltpu.VMEM((num_rows, *payload.shape), BF16)],
            row_flops // 8,
        )
    elif num_rows & (num_rows - 1):
        every = lax.all_gather(summed, "row")
        summed = every[0]
        for r in range(1, num_rows):
            summed = add(summed, every[r])
    else:
        bit = 1
        while bit < num_rows:
            other = lax.ppermute(summed, "row", [(r, r ^ bit) for r in range(num_rows)])
            summed = add(summed, other)
            bit *= 2
    mine = [summed] + [from_chip(summed, step) for step in range(1, chips)]
    theirs = [swap_cores(value) for value in mine]
    y_theirs = [swap_cores(value) for value in (*current, *y_others)]
    basis, reduced = call(
        functools.partial(finish_kernel, chips, 0.5 / (total_blocks * orbs)),
        "finish",
        (place,),
        (*mine, *theirs, *current, *y_others, *y_theirs),
        (
            jax.ShapeDtypeStruct((local_vecs, blocks_dev * orbs), BF16),
            jax.ShapeDtypeStruct((local_vecs, size), F32),
        ),
        [
            pltpu.VMEM((2, size, size), F32),
            pltpu.VMEM((size, size), F32),
            pltpu.VMEM((size, size), F32),
        ],
        10 * row_flops,
    )
    return basis, reduced.T


def solution(mesh):
    return jax.shard_map(
        local,
        mesh=mesh,
        in_specs=(
            P("col", ("pool", "row")),
            P(("pool", "row"), None, None, None),
            P(("pool", "row"), None, None, None),
            P(("pool", "row"), None),
            P(("pool", "row"), None),
            P(("pool", "row")),
            P("pool"),
            P("pool"),
        ),
        out_specs=(P("col", ("pool", "row")), P("pool", "col")),
        check_vma=False,
    )
```

```python
import functools

import jax
import jax.numpy as jnp
from jax import lax
from jax.experimental import pallas as pl
from jax.experimental.pallas import tpu as pltpu
from jax.sharding import PartitionSpec as P

HALF_BAND = 5
DEGREE = 4
CORES = 2
PANEL = 32
SLOWER = 24
SUBLANES = 8
DIAGONAL_ROWS = 16
DEVICE_ROW = 3

BF16 = jnp.bfloat16
F32 = jnp.float32
NT = (((1,), (1,)), ((), ()))
TN = (((0,), (0,)), ((), ()))

SMEM = pl.BlockSpec(memory_space=pltpu.SMEM)
VMEM = pl.BlockSpec(memory_space=pltpu.VMEM)
HBM = pl.BlockSpec(memory_space=pltpu.HBM)


def vmem(shape, dtype):
    return pltpu.VMEM(shape, dtype)


def fill_ext(core, own, intra, inter, ext):
    half = own.shape[0]
    ext[HALF_BAND : HALF_BAND + half] = own[...]
    ext[pl.ds((half + HALF_BAND) * (1 - core), HALF_BAND)] = intra[...]
    ext[pl.ds((half + HALF_BAND) * core, HALF_BAND)] = inter[...]


def picked(table, ext, row):
    index, signs = table
    slots = index.shape[1]
    return jnp.concatenate(
        [ext[index[row, s]] * signs[row, s].astype(BF16) for s in range(slots)], axis=1
    )


def row_matrix(blocks, row):
    return jnp.concatenate([blocks[row, s] for s in range(blocks.shape[1])], axis=1)


def send_ends(core, full, intra_out, inter_out):
    spare = full.shape[0] - HALF_BAND
    intra_out[...] = full[pl.ds(spare * (1 - core), HALF_BAND)]
    inter_out[...] = full[pl.ds(spare * core, HALF_BAND)]


def image_of(table, ext, matrices, row):
    matrix = jnp.concatenate([row_matrix(blocks, row) for blocks in matrices], axis=0)
    return lax.dot_general(matrix, picked(table, ext, row), NT, preferred_element_type=F32)


def both_rows(table, ext, ham, ovl, row):
    orbs = ham.shape[2]
    image = image_of(table, ext, (ham, ovl), row)
    return image[:orbs].T, image[orbs:].T


def one_row(table, ext, ovl, row):
    return image_of(table, ext, (ovl,), row).T


def cut_kernel(ints, sizes, trial, own, near, give, far, across, sizes_here, here, masked, sems):
    copies = [
        pltpu.make_async_copy(sizes, sizes_here, sems.at[0]),
        pltpu.make_async_copy(trial, here, sems.at[1]),
    ]
    for copy in copies:
        copy.start()
    for copy in copies:
        copy.wait()
    half, _, orbs = own.shape
    core = ints[0]
    lane = lax.broadcasted_iota(jnp.int32, own.shape[1:], 1)
    for row in range(2 * half):
        values = here[:, row * orbs : (row + 1) * orbs].astype(F32)
        masked[row] = jnp.where(lane < sizes_here[row], values, 0.0).astype(BF16)
    spare = half - HALF_BAND
    last = 2 * half - HALF_BAND
    own[...] = masked[pl.ds(half * core, half)]
    near[...] = masked[pl.ds(half - HALF_BAND * core, HALF_BAND)]
    give[...] = masked[pl.ds(spare * (1 - core), half + HALF_BAND)]
    far[...] = masked[pl.ds(last * (1 - core), HALF_BAND)]
    across[...] = masked[pl.ds(last * core, HALF_BAND)]


def load_kernel(total, ints, shift, width, columns, phases, sizes, ham, ovl, *rest):
    ham_out, ovl_out, index, signs, place, scal, columns_here, phases_here, sizes_here = rest[:9]
    sems, more_sems = rest[9:]
    half, slots = index.shape
    first = ints[0] * half
    small = [
        pltpu.make_async_copy(source, target, more_sems.at[i])
        for i, (source, target) in enumerate(
            ((columns, columns_here), (phases, phases_here), (sizes, sizes_here))
        )
    ]
    large = [
        pltpu.make_async_copy(source.at[first + row], target.at[row], sems.at[matrix, row])
        for row in range(half)
        for matrix, (source, target) in enumerate(((ham, ham_out), (ovl, ovl_out)))
    ]
    for copy in small + large:
        copy.start()
    scal[0] = shift[0]
    scal[1] = width[0]
    for i in range(3):
        place[i] = ints[i]
    place[DEVICE_ROW] = ints[4]
    for copy in small:
        copy.wait()
    start = ints[3] + first

    def fill(row, _):
        place[4 + row] = sizes_here[first + row]
        for slot in range(slots):
            away = columns_here[first + row, slot] - (start + row) + HALF_BAND
            away = jnp.where(away < 0, away + total, away)
            away = jnp.where(away >= total, away - total, away)
            index[row, slot] = row + away
            signs[row, slot] = (1 - 2 * phases_here[first + row, slot]).astype(F32)
        return 0

    lax.fori_loop(0, half, fill, 0)
    for copy in large:
        copy.wait()


def scaled_kernel(
    ints, index, signs, scal, own, inter, intra, ham, ovl, out, inter_out, intra_out, ext
):
    core = ints[0]
    fill_ext(core, own, intra, inter, ext)
    inv = 1.0 / (jnp.zeros(own.shape[1:], F32) + scal[1])
    for row in range(own.shape[0]):
        image_h, image_e = both_rows((index, signs), ext, ham, ovl, row)
        mine = own[row].astype(F32)
        out[row] = ((image_h - scal[0] * (mine + image_e)) * inv).astype(BF16)
    send_ends(core, out, intra_out, inter_out)


def term_kernel(ints, index, signs, own, inter, intra, ovl, out, inter_out, intra_out, ext):
    core = ints[0]
    fill_ext(core, own, intra, inter, ext)
    for row in range(own.shape[0]):
        out[row] = (-one_row((index, signs), ext, ovl, row)).astype(BF16)
    send_ends(core, out, intra_out, inter_out)


def update_kernel(first, ints, index, signs, own, inter, intra, scaled, *rest):
    if first:
        ovl, out, inter_out, intra_out, ext = rest
    else:
        previous, ovl, out, inter_out, intra_out, ext = rest
    core = ints[0]
    half = own.shape[0]
    fill_ext(core, own, intra, inter, ext)
    lane = lax.broadcasted_iota(jnp.int32, own.shape[1:], 1)
    for row in range(half):
        image = one_row((index, signs), ext, ovl, row)
        filtered = scaled[row].astype(F32) + own[row].astype(F32) - image
        if not first:
            filtered = 2.0 * filtered - previous[row].astype(F32)
        out[row] = jnp.where(lane < ints[4 + row], filtered, 0.0).astype(BF16)
    send_ends(core, out, intra_out, inter_out)


def images_kernel(ints, index, signs, own, inter, intra, ham, ovl, y_other, out, ext):
    del y_other
    core = ints[0]
    fill_ext(core, own, intra, inter, ext)
    half, _, orbs = own.shape
    for row in range(half):
        image_h, image_e = both_rows((index, signs), ext, ham, ovl, row)
        at = slice(row * orbs, (row + 1) * orbs)
        out[0, :, at] = (own[row].astype(F32) + image_e).astype(BF16)
        out[1, :, at] = image_h.astype(BF16)


def gram_kernel(chips, ints, *refs):
    images, groups = refs[:CORES], refs[CORES : CORES + CORES * chips]
    keep, send, both = refs[CORES + CORES * chips :]
    core, chip = ints[0], ints[1]
    half, local_vecs, _ = groups[0].shape
    vecs = CORES * local_vecs
    flat = jnp.concatenate(
        [jnp.concatenate([group[row] for row in range(half)], axis=1) for group in groups], axis=0
    )
    eye = lax.broadcasted_iota(jnp.int32, (vecs, vecs), 0) == lax.broadcasted_iota(
        jnp.int32, (vecs, vecs), 1
    )
    for matrix in range(2):
        mine = jnp.concatenate([image[matrix] for image in images], axis=0)
        pair = lax.dot_general(mine, flat, NT, preferred_element_type=F32)
        both[matrix, : vecs // 2, :] = packed(pair[:, :vecs]).astype(BF16)
        for step in range(1, chips):
            block = pair[:, step * vecs : (step + 1) * vecs]
            both[matrix, (2 * step - 1) * vecs // 2 : (2 * step + 1) * vecs // 2, :] = block.astype(BF16)
        diagonal = jnp.sum(jnp.where(eye, pair[:, :vecs], 0.0), axis=0, keepdims=True)
        both[matrix, (2 * chips - 1) * vecs // 2 :, :] = diagonal_parts(diagonal)
    keep[...] = both[core]
    send[...] = both[1 - core]


def packed(block):
    half = block.shape[0] // 2
    block = 0.5 * (block + block.T)
    top, bottom = block[:half], block[half:]
    bottom = jnp.concatenate([bottom[:, half:], bottom[:, :half]], axis=1)
    row = lax.broadcasted_iota(jnp.int32, top.shape, 0)
    lane = lax.broadcasted_iota(jnp.int32, top.shape, 1)
    return jnp.where((lane < half) & (lane > row), bottom, top)


def unpacked(block):
    half = block.shape[0]
    turned = block.T
    row = lax.broadcasted_iota(jnp.int32, (half, half), 0)
    lane = lax.broadcasted_iota(jnp.int32, (half, half), 1)
    square, beside = block[:, :half], block[:, half:]
    first = jnp.where(lane < row, square, turned[:half])
    last = jnp.where(lane > row, square, turned[:half])
    return jnp.concatenate(
        [
            jnp.concatenate([first, beside], axis=1),
            jnp.concatenate([turned[half:], last], axis=1),
        ],
        axis=0,
    )


def diagonal_parts(diagonal):
    high, middle, low = (part.astype(F32) for part in split3(diagonal))
    rows = lax.broadcasted_iota(jnp.int32, (DIAGONAL_ROWS, diagonal.shape[1]), 0)
    parts = jnp.where(rows == 0, high, jnp.where(rows == 1, middle, jnp.where(rows == 2, low, 0.0)))
    return parts.astype(BF16)


def diagonal_of(payload):
    parts = payload[payload.shape[0] - DIAGONAL_ROWS :, :].astype(F32)
    return parts[0:1] + (parts[1:2] + parts[2:3])


def add_kernel(left, right, out):
    body = left.shape[0] - DIAGONAL_ROWS
    out[:body] = (left[:body, :].astype(F32) + right[:body, :].astype(F32)).astype(BF16)
    out[body:] = diagonal_parts(diagonal_of(left) + diagonal_of(right))


def sum_kernel(ints, *refs):
    *payloads, out, held = refs
    count = len(payloads)
    for step, payload in enumerate(payloads):
        held[lax.bitwise_xor(ints[DEVICE_ROW], jnp.int32(step))] = payload[...]
    body = out.shape[0] - DIAGONAL_ROWS
    total = held[0, :body, :].astype(F32)
    diagonal = diagonal_of(held.at[0])
    for r in range(1, count):
        total = total + held[r, :body, :].astype(F32)
        diagonal = diagonal + diagonal_of(held.at[r])
    out[:body] = total.astype(BF16)
    out[body:] = diagonal_parts(diagonal)


def split3(value):
    high = value.astype(BF16)
    rest = value - high.astype(F32)
    middle = rest.astype(BF16)
    low = (rest - middle.astype(F32)).astype(BF16)
    return high, middle, low


def three_terms(left, right, axis):
    (high, middle, _), (other, little, _) = split3(left), split3(right)
    return (
        jnp.concatenate([high, high, middle], axis=1),
        jnp.concatenate([other, little, other], axis=axis),
    )


def panel_inverse(block):
    lane = lax.broadcasted_iota(jnp.int32, (PANEL, 128), 1)
    rows = lax.broadcasted_iota(jnp.int32, (PANEL, 128), 0)
    work = jnp.where(lane < PANEL, block, jnp.where(lax.rem(lane, PANEL) == rows, 1.0, 0.0))
    count = PANEL // SUBLANES
    pieces = [work[v * SUBLANES : (v + 1) * SUBLANES] for v in range(count)]
    sub = lax.broadcasted_iota(jnp.int32, (SUBLANES, 128), 0)

    def spread(value, k):
        return jnp.broadcast_to(value[k % SUBLANES : k % SUBLANES + 1], (SUBLANES, 128))

    pivots = [jnp.ones((SUBLANES, 128), F32) for _ in range(count)]
    for start, group in ((0, 16), (16, 16)):
        columns = {
            k: {
                v: jnp.broadcast_to(pieces[v][:, k : k + 1], (SUBLANES, 128))
                for v in range(start // SUBLANES, count)
            }
            for k in range(start, start + group)
        }
        at = spread(columns[start][start // SUBLANES], start)
        for k in range(start, start + group):
            here = k // SUBLANES
            pivots[here] = jnp.where(sub == k % SUBLANES, at, pivots[here])
            guess = pl.reciprocal(at, approx=True)
            correction = 2.0 - at * guess
            inv = guess * correction
            if k + 1 < start + group:
                below = (k + 1) // SUBLANES
                product = spread(columns[k][below], k + 1) * spread(columns[k + 1][here], k)
                at = spread(columns[k + 1][below], k + 1) - (product * guess) * correction
            factors = {v: columns[k][v] * inv for v in range(here, count)}
            factors[here] = jnp.where(sub > k % SUBLANES, factors[here], 0.0)
            for later in range(k + 1, start + group):
                top = spread(columns[later][here], k)
                for v in range(here, count):
                    columns[later][v] = columns[later][v] - factors[v] * top
            top = spread(pieces[here], k)
            for v in range(here, count):
                pieces[v] = pieces[v] - factors[v] * top
    pivot = jnp.concatenate(pivots, axis=0)
    root = lax.rsqrt(pivot)
    root = root * (1.5 - 0.5 * ((pivot * root) * root))
    return jnp.concatenate(pieces, axis=0) * root


def factor(work, inverse):
    size = work.shape[0]
    wide = lax.broadcasted_iota(jnp.int32, (PANEL, size), 1)
    tall = lax.broadcasted_iota(jnp.int32, (PANEL, size), 0)
    lane = lax.broadcasted_iota(jnp.int32, (PANEL, 128), 1)
    zero = jnp.zeros((PANEL, size), BF16)
    for start in range(0, size, PANEL):
        rows = work[start : start + PANEL, :]
        tile = start // 128 * 128
        block = work[start : start + PANEL, tile : tile + 128]
        if start % 128:
            block = pltpu.roll(block, 128 - start % 128, axis=1)
        t_high, t_mid, t_low = split3(jnp.where(lane < PANEL, 0.0, panel_inverse(block)))
        first = jnp.where(lane < 2 * PANEL, t_high, jnp.where(lane < 3 * PANEL, t_mid, t_low))
        second = jnp.where(lane < 2 * PANEL, t_high, jnp.where(lane < 3 * PANEL, t_mid, t_high))
        left = jnp.concatenate([first, second], axis=1)
        inside = (wide >= start) & (wide < start + PANEL)
        rows = jnp.where(inside, jnp.where(wide - start == tall, 1.0, 0.0), rows)
        r_high, r_mid, r_low = split3(rows)
        right = jnp.concatenate([zero, r_high, r_high, r_high, zero, r_mid, r_mid, r_low], axis=0)
        new = jnp.dot(left, right, preferred_element_type=F32)
        inverse[start : start + PANEL, :] = jnp.where(wide < start + PANEL, new, 0.0)
        after = start + PANEL
        if after < size:
            high, middle, low = split3(new)
            base = after // 128 * 128
            lhs = jnp.concatenate([high, high, middle, middle, high, low], axis=0)[:, base:]
            rhs = jnp.concatenate([high, middle, high, middle, low, high], axis=0)
            change = lax.dot_general(lhs, rhs, TN, preferred_element_type=F32)[after - base :]
            columns = lax.broadcasted_iota(jnp.int32, change.shape, 1)
            old = work[after:, :]
            work[after:, :] = jnp.where((columns >= start) & (columns < after), 0.0, old) - change


def six_terms(left, right):
    (high, middle, low), (other, little, least) = split3(left), split3(right)
    return jnp.dot(
        jnp.concatenate([high, high, middle, middle, high, low], axis=1),
        jnp.concatenate([other, little, other, little, least, other], axis=0),
        preferred_element_type=F32,
    )


def factor_halves(gram, work, inverse):
    half = gram.shape[0] // 2
    first, last = slice(0, half), slice(half, 2 * half)
    work[0] = gram[first, first]
    factor(work.at[0], inverse.at[first, first])
    beside = six_terms(inverse[first, first], gram[first, last])
    turned = beside.T
    work[1] = gram[last, last] - six_terms(turned, beside)
    factor(work.at[1], inverse.at[last, last])
    inverse[last, first] = -six_terms(
        inverse[last, last], six_terms(turned, inverse[first, first])
    )
    inverse[first, last] = jnp.zeros((half, half), F32)


def finish_kernel(chips, scale, ints, *refs):
    mine, theirs = refs[:chips], refs[chips : 2 * chips]
    y_mine = refs[2 * chips : (2 + CORES) * chips]
    y_theirs = refs[(2 + CORES) * chips : (2 + 2 * CORES) * chips]
    basis, reduced, pair, work, inverse = refs[(2 + 2 * CORES) * chips :]
    core, chip, col = ints[0], ints[1], ints[2]
    half, local_vecs, orbs = y_mine[0].shape
    vecs = CORES * local_vecs
    eye = lax.broadcasted_iota(jnp.int32, (vecs, vecs), 0) == lax.broadcasted_iota(
        jnp.int32, (vecs, vecs), 1
    )
    for step in range(chips):
        which = lax.rem(chip + step, chips)
        rows = pl.ds(pl.multiple_of(which * vecs, vecs), vecs)
        for matrix, payload in ((core, mine[step]), (1 - core, theirs[step])):
            own_block = unpacked(payload[: vecs // 2, :].astype(F32))
            own_block = jnp.where(eye, diagonal_of(payload), own_block)
            for k in range(chips):
                block = own_block
                for away in range(1, chips):
                    at = (2 * away - 1) * vecs // 2
                    other = payload[at : at + vecs, :].astype(F32)
                    block = jnp.where(lax.rem(which + away, chips) == k, other, block)
                pair[matrix, rows, k * vecs : (k + 1) * vecs] = block
    factor_halves((pair[0] + pair[0].T) * scale, work, inverse)
    start = pl.multiple_of(col * local_vecs, local_vecs)
    own_rows = inverse[pl.ds(start, local_vecs), :]
    gram_h = (pair[1] + pair[1].T) * scale
    half_way = jnp.dot(*three_terms(own_rows, gram_h, 0), preferred_element_type=F32)
    reduced[...] = lax.dot_general(
        *three_terms(half_way, inverse[...], 1), NT, preferred_element_type=F32
    )
    rotation = own_rows.astype(BF16)
    turned = []
    for step in range(chips):
        which = lax.rem(chip + step, chips)
        part = rotation[:, :vecs]
        for k in range(1, chips):
            part = jnp.where(which == k, rotation[:, k * vecs : (k + 1) * vecs], part)
        turned.append(part)
    turned = jnp.concatenate(turned, axis=1)
    for which, group in ((core, y_mine), (1 - core, y_theirs)):
        for row in range(half):
            everything = jnp.concatenate([vectors[row] for vectors in group], axis=0)
            result = jnp.dot(turned, everything, preferred_element_type=F32).astype(BF16)
            at = pl.multiple_of((which * half + row) * orbs, orbs)
            basis[:, pl.ds(at, orbs)] = result


def local(
    trial_vectors,
    hamiltonian_blocks,
    correlation_offset,
    block_columns,
    block_phases,
    block_sizes,
    shift,
    halfwidth,
):
    blocks_dev, slots = block_columns.shape
    orbs = hamiltonian_blocks.shape[2]
    num_rows, num_cols = lax.axis_size("row"), lax.axis_size("col")
    total_blocks = blocks_dev * num_rows
    half = blocks_dev // CORES
    chips = num_cols // CORES
    local_vecs = trial_vectors.shape[0]
    vecs = local_vecs * CORES
    size = local_vecs * num_cols
    row, col = lax.axis_index("row"), lax.axis_index("col")
    core, chip = lax.rem(col, CORES), lax.div(col, CORES)

    def swap_cores(value):
        return lax.ppermute(value, "col", [(c, c ^ 1) for c in range(num_cols)])

    def swap_chips(value):
        pairs = []
        for r in range(num_rows):
            for x in range(chips):
                upper = r * num_cols + x * CORES + 1
                lower = (r + 1) % num_rows * num_cols + x * CORES
                pairs += [(upper, lower), (lower, upper)]
        return lax.ppermute(value, ("row", "col"), pairs)

    def next_chips(value):
        pairs = []
        for r in range(num_rows):
            for c in range(num_cols):
                to = (r + 1 if c % CORES == 0 else r - 1) % num_rows
                pairs.append((r * num_cols + c, to * num_cols + c))
        return lax.ppermute(value, ("row", "col"), pairs)

    def from_chip(value, step):
        pairs = [((c + step * CORES) % num_cols, c) for c in range(num_cols)]
        return lax.ppermute(value, "col", pairs)

    state = jax.ShapeDtypeStruct((half, local_vecs, orbs), BF16)
    end = jax.ShapeDtypeStruct((HALF_BAND, local_vecs, orbs), BF16)
    ext = pltpu.VMEM((half + 2 * HALF_BAND, local_vecs, orbs), BF16)
    params = pltpu.CompilerParams(vmem_limit_bytes=16 << 20)
    row_flops = SLOWER * 2 * half * slots * local_vecs * orbs * orbs

    def call(kernel, name, scalars, arrays, outs, scratch, flops):
        return pl.pallas_call(
            kernel,
            name=name,
            out_shape=outs,
            in_specs=[SMEM] * len(scalars) + [VMEM] * len(arrays),
            out_specs=(VMEM,) * len(outs),
            scratch_shapes=scratch,
            compiler_params=params,
            cost_estimate=pl.CostEstimate(
                flops=flops, bytes_accessed=flops // 128, transcendentals=0
            ),
        )(*scalars, *arrays)

    def step_call(kernel, name, scalars, arrays, flops):
        return call(kernel, name, scalars, arrays, (state, end, end), [ext], flops)

    def exchange(ends):
        return swap_chips(ends[0]), swap_cores(ends[1])

    def scalars(value):
        return pltpu.with_memory_space_constraint(value, pltpu.SMEM)

    ints = scalars(jnp.stack([core, chip, col, row * blocks_dev, row]).astype(jnp.int32))
    shift, halfwidth = scalars(shift), scalars(halfwidth)

    def stays(value):
        return pltpu.with_memory_space_constraint(value, pltpu.HBM)

    more = jax.ShapeDtypeStruct((half + HALF_BAND, local_vecs, orbs), BF16)
    own, near, give, far, across = pl.pallas_call(
        cut_kernel,
        name="cut",
        out_shape=(state, end, more, end, end),
        in_specs=[SMEM, HBM, HBM],
        out_specs=(VMEM,) * 5,
        scratch_shapes=[
            pltpu.SMEM(block_sizes.shape, jnp.int32),
            pltpu.VMEM(trial_vectors.shape, BF16),
            pltpu.VMEM((blocks_dev, local_vecs, orbs), BF16),
            pltpu.SemaphoreType.DMA((2,)),
        ],
        compiler_params=params,
    )(ints, stays(block_sizes), stays(trial_vectors))
    far, across = next_chips(far), swap_chips(across)
    got = swap_cores(give)
    matrix = vmem((half, *hamiltonian_blocks.shape[1:]), BF16)
    ham, ovl, index, signs, place, scal = pl.pallas_call(
        functools.partial(load_kernel, total_blocks),
        name="load",
        out_shape=(
            matrix,
            matrix,
            pltpu.SMEM((half, slots), jnp.int32),
            pltpu.SMEM((half, slots), F32),
            pltpu.SMEM((4 + half,), jnp.int32),
            pltpu.SMEM((2,), F32),
        ),
        in_specs=[SMEM] * 3 + [HBM] * 5,
        out_specs=(VMEM, VMEM, SMEM, SMEM, SMEM, SMEM),
        scratch_shapes=[
            pltpu.SMEM(block_columns.shape, jnp.int32),
            pltpu.SMEM(block_phases.shape, jnp.int32),
            pltpu.SMEM(block_sizes.shape, jnp.int32),
            pltpu.SemaphoreType.DMA((2, half)),
            pltpu.SemaphoreType.DMA((3,)),
        ],
        compiler_params=params,
        cost_estimate=pl.CostEstimate(
            flops=0, bytes_accessed=4 * hamiltonian_blocks.size, transcendentals=0
        ),
    )(
        ints,
        shift,
        halfwidth,
        stays(block_columns),
        stays(block_phases),
        stays(block_sizes),
        stays(hamiltonian_blocks),
        stays(correlation_offset),
    )
    got_own = lax.dynamic_slice_in_dim(got, HALF_BAND * core, half, 0)
    got_near = lax.dynamic_slice_in_dim(got, half * (1 - core), HALF_BAND, 0)

    def by_group(mine, other):
        return [jnp.where(core == 0, mine, other), jnp.where(core == 0, other, mine)]

    current = by_group(own, got_own)
    halo = list(zip(by_group(far, across), by_group(near, got_near)))
    table = (place, index, signs)
    scaled, term, previous = [None] * CORES, [None] * CORES, list(current)
    for degree in range(DEGREE):
        for g in range(CORES):
            if g > 0:
                current[g], scaled[0] = lax.optimization_barrier((current[g], scaled[0]))
            scaled[g], *ends = step_call(
                scaled_kernel,
                "scaled",
                (*table, scal),
                (current[g], *halo[g], ham, ovl),
                2 * row_flops,
            )
            halo[g] = exchange(ends)
        for g in range(CORES):
            term[g], *ends = step_call(
                term_kernel, "term", table, (scaled[g], *halo[g], ovl), row_flops
            )
            halo[g] = exchange(ends)
        for g in range(CORES):
            first = degree == 0
            arrays = (term[g], *halo[g], scaled[g]) + (() if first else (previous[g],)) + (ovl,)
            updated, *ends = step_call(
                functools.partial(update_kernel, first),
                "update",
                table,
                arrays,
                row_flops,
            )
            halo[g] = exchange(ends)
            previous[g], current[g] = current[g], updated

    y_others = [from_chip(value, step) for step in range(1, chips) for value in current]
    image = jax.ShapeDtypeStruct((2, local_vecs, half * orbs), BF16)
    images = []
    for g, vectors in enumerate(current):
        if g > 0:
            vectors, images[0] = lax.optimization_barrier((vectors, images[0]))
        images += call(
            images_kernel,
            "images",
            table,
            (vectors, *halo[g], ham, ovl, y_others[0]),
            (image,),
            [ext],
            2 * row_flops,
        )
    payload = jax.ShapeDtypeStruct((size - vecs // 2 + DIAGONAL_ROWS, vecs), BF16)
    keep, send = call(
        functools.partial(gram_kernel, chips),
        "gram",
        (place,),
        (*images, *current, *y_others),
        (payload, payload),
        [pltpu.VMEM((2, *payload.shape), BF16)],
        row_flops,
    )

    def add(left, right):
        return call(add_kernel, "add", (), (left, right), (payload,), [], row_flops // 8)[0]

    summed = add(keep, swap_cores(send))
    if num_rows in (2, 4):
        others = [
            lax.ppermute(summed, "row", [(r, r ^ step) for r in range(num_rows)])
            for step in range(1, num_rows)
        ]
        (summed,) = call(
            sum_kernel,
            "sum",
            (place,),
            (summed, *others),
            (payload,),
            [pltpu.VMEM((num_rows, *payload.shape), BF16)],
            row_flops // 8,
        )
    elif num_rows & (num_rows - 1):
        every = lax.all_gather(summed, "row")
        summed = every[0]
        for r in range(1, num_rows):
            summed = add(summed, every[r])
    else:
        bit = 1
        while bit < num_rows:
            other = lax.ppermute(summed, "row", [(r, r ^ bit) for r in range(num_rows)])
            summed = add(summed, other)
            bit *= 2
    mine = [summed] + [from_chip(summed, step) for step in range(1, chips)]
    theirs = [swap_cores(value) for value in mine]
    y_theirs = [swap_cores(value) for value in (*current, *y_others)]
    basis, reduced = call(
        functools.partial(finish_kernel, chips, 0.5 / (total_blocks * orbs)),
        "finish",
        (place,),
        (*mine, *theirs, *current, *y_others, *y_theirs),
        (
            jax.ShapeDtypeStruct((local_vecs, blocks_dev * orbs), BF16),
            jax.ShapeDtypeStruct((local_vecs, size), F32),
        ),
        [
            pltpu.VMEM((2, size, size), F32),
            pltpu.VMEM((2, size // 2, size // 2), F32),
            pltpu.VMEM((size, size), F32),
        ],
        10 * row_flops,
    )
    return basis, reduced.T


def solution(mesh):
    return jax.shard_map(
        local,
        mesh=mesh,
        in_specs=(
            P("col", ("pool", "row")),
            P(("pool", "row"), None, None, None),
            P(("pool", "row"), None, None, None),
            P(("pool", "row"), None),
            P(("pool", "row"), None),
            P(("pool", "row")),
            P("pool"),
            P("pool"),
        ),
        out_specs=(P("col", ("pool", "row")), P("pool", "col")),
        check_vma=False,
    )
```

```python
import functools

import jax
import jax.numpy as jnp
from jax import lax
from jax.experimental import pallas as pl
from jax.experimental.pallas import tpu as pltpu
from jax.sharding import PartitionSpec as P

HALF_BAND = 5
DEGREE = 4
CORES = 2
PANEL = 32
SLOWER = 24
SUBLANES = 8
DIAGONAL_ROWS = 16
DEVICE_ROW = 3

BF16 = jnp.bfloat16
F32 = jnp.float32
NT = (((1,), (1,)), ((), ()))
TN = (((0,), (0,)), ((), ()))

SMEM = pl.BlockSpec(memory_space=pltpu.SMEM)
VMEM = pl.BlockSpec(memory_space=pltpu.VMEM)
HBM = pl.BlockSpec(memory_space=pltpu.HBM)


def vmem(shape, dtype):
    return pltpu.VMEM(shape, dtype)


def fill_ext(core, own, intra, inter, ext):
    half = own.shape[0]
    ext[HALF_BAND : HALF_BAND + half] = own[...]
    ext[pl.ds((half + HALF_BAND) * (1 - core), HALF_BAND)] = intra[...]
    ext[pl.ds((half + HALF_BAND) * core, HALF_BAND)] = inter[...]


def picked(table, ext, row):
    index, signs = table
    slots = index.shape[1]
    return jnp.concatenate(
        [ext[index[row, s]] * signs[row, s].astype(BF16) for s in range(slots)], axis=1
    )


def row_matrix(blocks, row):
    return jnp.concatenate([blocks[row, s] for s in range(blocks.shape[1])], axis=1)


def send_ends(core, full, intra_out, inter_out):
    spare = full.shape[0] - HALF_BAND
    intra_out[...] = full[pl.ds(spare * (1 - core), HALF_BAND)]
    inter_out[...] = full[pl.ds(spare * core, HALF_BAND)]


def image_of(table, ext, matrices, row):
    matrix = jnp.concatenate([row_matrix(blocks, row) for blocks in matrices], axis=0)
    return lax.dot_general(matrix, picked(table, ext, row), NT, preferred_element_type=F32)


def both_rows(table, ext, ham, ovl, row):
    orbs = ham.shape[2]
    image = image_of(table, ext, (ham, ovl), row)
    return image[:orbs].T, image[orbs:].T


def one_row(table, ext, ovl, row):
    return image_of(table, ext, (ovl,), row).T


def cut_kernel(ints, sizes, trial, own, near, give, far, across, sizes_here, here, masked, sems):
    copies = [
        pltpu.make_async_copy(sizes, sizes_here, sems.at[0]),
        pltpu.make_async_copy(trial, here, sems.at[1]),
    ]
    for copy in copies:
        copy.start()
    for copy in copies:
        copy.wait()
    half, _, orbs = own.shape
    core = ints[0]
    lane = lax.broadcasted_iota(jnp.int32, own.shape[1:], 1)
    for row in range(2 * half):
        values = here[:, row * orbs : (row + 1) * orbs].astype(F32)
        masked[row] = jnp.where(lane < sizes_here[row], values, 0.0).astype(BF16)
    spare = half - HALF_BAND
    last = 2 * half - HALF_BAND
    own[...] = masked[pl.ds(half * core, half)]
    near[...] = masked[pl.ds(half - HALF_BAND * core, HALF_BAND)]
    give[...] = masked[pl.ds(spare * (1 - core), half + HALF_BAND)]
    far[...] = masked[pl.ds(last * (1 - core), HALF_BAND)]
    across[...] = masked[pl.ds(last * core, HALF_BAND)]


def load_kernel(total, ints, shift, width, columns, phases, sizes, ham, ovl, *rest):
    ham_out, ovl_out, index, signs, place, scal, columns_here, phases_here, sizes_here = rest[:9]
    sems, more_sems = rest[9:]
    half, slots = index.shape
    first = ints[0] * half
    small = [
        pltpu.make_async_copy(source, target, more_sems.at[i])
        for i, (source, target) in enumerate(
            ((columns, columns_here), (phases, phases_here), (sizes, sizes_here))
        )
    ]
    large = [
        pltpu.make_async_copy(source.at[first + row], target.at[row], sems.at[matrix, row])
        for row in range(half)
        for matrix, (source, target) in enumerate(((ham, ham_out), (ovl, ovl_out)))
    ]
    for copy in small + large:
        copy.start()
    scal[0] = shift[0]
    scal[1] = width[0]
    for i in range(3):
        place[i] = ints[i]
    place[DEVICE_ROW] = ints[4]
    for copy in small:
        copy.wait()
    start = ints[3] + first

    def fill(row, _):
        place[4 + row] = sizes_here[first + row]
        for slot in range(slots):
            away = columns_here[first + row, slot] - (start + row) + HALF_BAND
            away = jnp.where(away < 0, away + total, away)
            away = jnp.where(away >= total, away - total, away)
            index[row, slot] = row + away
            signs[row, slot] = (1 - 2 * phases_here[first + row, slot]).astype(F32)
        return 0

    lax.fori_loop(0, half, fill, 0)
    for copy in large:
        copy.wait()


def for_rows(count, step):
    def pair(i, carry):
        step(2 * i)
        step(2 * i + 1)
        return carry

    lax.fori_loop(0, count // 2, pair, 0)
    if count % 2:
        step(count - 1)


def scaled_kernel(
    ints, index, signs, scal, own, inter, intra, ham, ovl, out, inter_out, intra_out, ext
):
    core = ints[0]
    fill_ext(core, own, intra, inter, ext)
    inv = 1.0 / (jnp.zeros(own.shape[1:], F32) + scal[1])

    def step(row):
        image_h, image_e = both_rows((index, signs), ext, ham, ovl, row)
        mine = own[row].astype(F32)
        out[row] = ((image_h - scal[0] * (mine + image_e)) * inv).astype(BF16)

    for_rows(own.shape[0], step)
    send_ends(core, out, intra_out, inter_out)


def term_kernel(ints, index, signs, own, inter, intra, ovl, out, inter_out, intra_out, ext):
    core = ints[0]
    fill_ext(core, own, intra, inter, ext)

    def step(row):
        out[row] = (-one_row((index, signs), ext, ovl, row)).astype(BF16)

    for_rows(own.shape[0], step)
    send_ends(core, out, intra_out, inter_out)


def update_kernel(first, ints, index, signs, own, inter, intra, scaled, *rest):
    if first:
        ovl, out, inter_out, intra_out, ext = rest
    else:
        previous, ovl, out, inter_out, intra_out, ext = rest
    core = ints[0]
    half = own.shape[0]
    fill_ext(core, own, intra, inter, ext)
    lane = lax.broadcasted_iota(jnp.int32, own.shape[1:], 1)

    def step(row):
        image = one_row((index, signs), ext, ovl, row)
        filtered = scaled[row].astype(F32) + own[row].astype(F32) - image
        if not first:
            filtered = 2.0 * filtered - previous[row].astype(F32)
        out[row] = jnp.where(lane < ints[4 + row], filtered, 0.0).astype(BF16)

    for_rows(half, step)
    send_ends(core, out, intra_out, inter_out)


def images_kernel(ints, index, signs, own, inter, intra, ham, ovl, y_other, out, ext):
    del y_other
    core = ints[0]
    fill_ext(core, own, intra, inter, ext)
    half, _, orbs = own.shape
    for row in range(half):
        image_h, image_e = both_rows((index, signs), ext, ham, ovl, row)
        at = slice(row * orbs, (row + 1) * orbs)
        out[0, :, at] = (own[row].astype(F32) + image_e).astype(BF16)
        out[1, :, at] = image_h.astype(BF16)


def gram_kernel(chips, ints, *refs):
    images, groups = refs[:CORES], refs[CORES : CORES + CORES * chips]
    keep, send, both = refs[CORES + CORES * chips :]
    core, chip = ints[0], ints[1]
    half, local_vecs, _ = groups[0].shape
    vecs = CORES * local_vecs
    flat = jnp.concatenate(
        [jnp.concatenate([group[row] for row in range(half)], axis=1) for group in groups], axis=0
    )
    eye = lax.broadcasted_iota(jnp.int32, (vecs, vecs), 0) == lax.broadcasted_iota(
        jnp.int32, (vecs, vecs), 1
    )
    for matrix in range(2):
        mine = jnp.concatenate([image[matrix] for image in images], axis=0)
        pair = lax.dot_general(mine, flat, NT, preferred_element_type=F32)
        both[matrix, : vecs // 2, :] = packed(pair[:, :vecs]).astype(BF16)
        for step in range(1, chips):
            block = pair[:, step * vecs : (step + 1) * vecs]
            both[matrix, (2 * step - 1) * vecs // 2 : (2 * step + 1) * vecs // 2, :] = block.astype(BF16)
        diagonal = jnp.sum(jnp.where(eye, pair[:, :vecs], 0.0), axis=0, keepdims=True)
        both[matrix, (2 * chips - 1) * vecs // 2 :, :] = diagonal_parts(diagonal)
    keep[...] = both[core]
    send[...] = both[1 - core]


def packed(block):
    half = block.shape[0] // 2
    block = 0.5 * (block + block.T)
    top, bottom = block[:half], block[half:]
    bottom = jnp.concatenate([bottom[:, half:], bottom[:, :half]], axis=1)
    row = lax.broadcasted_iota(jnp.int32, top.shape, 0)
    lane = lax.broadcasted_iota(jnp.int32, top.shape, 1)
    return jnp.where((lane < half) & (lane > row), bottom, top)


def unpacked(block):
    half = block.shape[0]
    turned = block.T
    row = lax.broadcasted_iota(jnp.int32, (half, half), 0)
    lane = lax.broadcasted_iota(jnp.int32, (half, half), 1)
    square, beside = block[:, :half], block[:, half:]
    first = jnp.where(lane < row, square, turned[:half])
    last = jnp.where(lane > row, square, turned[:half])
    return jnp.concatenate(
        [
            jnp.concatenate([first, beside], axis=1),
            jnp.concatenate([turned[half:], last], axis=1),
        ],
        axis=0,
    )


def diagonal_parts(diagonal):
    high, middle, low = (part.astype(F32) for part in split3(diagonal))
    rows = lax.broadcasted_iota(jnp.int32, (DIAGONAL_ROWS, diagonal.shape[1]), 0)
    parts = jnp.where(rows == 0, high, jnp.where(rows == 1, middle, jnp.where(rows == 2, low, 0.0)))
    return parts.astype(BF16)


def diagonal_of(payload):
    parts = payload[payload.shape[0] - DIAGONAL_ROWS :, :].astype(F32)
    return parts[0:1] + (parts[1:2] + parts[2:3])


def add_kernel(left, right, out):
    body = left.shape[0] - DIAGONAL_ROWS
    out[:body] = (left[:body, :].astype(F32) + right[:body, :].astype(F32)).astype(BF16)
    out[body:] = diagonal_parts(diagonal_of(left) + diagonal_of(right))


def sum_kernel(ints, *refs):
    *payloads, out, held = refs
    count = len(payloads)
    for step, payload in enumerate(payloads):
        held[lax.bitwise_xor(ints[DEVICE_ROW], jnp.int32(step))] = payload[...]
    body = out.shape[0] - DIAGONAL_ROWS
    total = held[0, :body, :].astype(F32)
    diagonal = diagonal_of(held.at[0])
    for r in range(1, count):
        total = total + held[r, :body, :].astype(F32)
        diagonal = diagonal + diagonal_of(held.at[r])
    out[:body] = total.astype(BF16)
    out[body:] = diagonal_parts(diagonal)


def split3(value):
    high = value.astype(BF16)
    rest = value - high.astype(F32)
    middle = rest.astype(BF16)
    low = (rest - middle.astype(F32)).astype(BF16)
    return high, middle, low


def three_terms(left, right, axis):
    (high, middle, _), (other, little, _) = split3(left), split3(right)
    return (
        jnp.concatenate([high, high, middle], axis=1),
        jnp.concatenate([other, little, other], axis=axis),
    )


def panel_inverse(block):
    lane = lax.broadcasted_iota(jnp.int32, (PANEL, 128), 1)
    rows = lax.broadcasted_iota(jnp.int32, (PANEL, 128), 0)
    work = jnp.where(lane < PANEL, block, jnp.where(lax.rem(lane, PANEL) == rows, 1.0, 0.0))
    count = PANEL // SUBLANES
    pieces = [work[v * SUBLANES : (v + 1) * SUBLANES] for v in range(count)]
    sub = lax.broadcasted_iota(jnp.int32, (SUBLANES, 128), 0)

    def spread(value, k):
        return jnp.broadcast_to(value[k % SUBLANES : k % SUBLANES + 1], (SUBLANES, 128))

    pivots = [jnp.ones((SUBLANES, 128), F32) for _ in range(count)]
    for start, group in ((0, 16), (16, 16)):
        columns = {
            k: {
                v: jnp.broadcast_to(pieces[v][:, k : k + 1], (SUBLANES, 128))
                for v in range(start // SUBLANES, count)
            }
            for k in range(start, start + group)
        }
        at = spread(columns[start][start // SUBLANES], start)
        for k in range(start, start + group):
            here = k // SUBLANES
            pivots[here] = jnp.where(sub == k % SUBLANES, at, pivots[here])
            guess = pl.reciprocal(at, approx=True)
            correction = 2.0 - at * guess
            inv = guess * correction
            if k + 1 < start + group:
                below = (k + 1) // SUBLANES
                product = spread(columns[k][below], k + 1) * spread(columns[k + 1][here], k)
                at = spread(columns[k + 1][below], k + 1) - (product * guess) * correction
            factors = {v: columns[k][v] * inv for v in range(here, count)}
            factors[here] = jnp.where(sub > k % SUBLANES, factors[here], 0.0)
            for later in range(k + 1, start + group):
                top = spread(columns[later][here], k)
                for v in range(here, count):
                    columns[later][v] = columns[later][v] - factors[v] * top
            top = spread(pieces[here], k)
            for v in range(here, count):
                pieces[v] = pieces[v] - factors[v] * top
    pivot = jnp.concatenate(pivots, axis=0)
    root = lax.rsqrt(pivot)
    root = root * (1.5 - 0.5 * ((pivot * root) * root))
    return jnp.concatenate(pieces, axis=0) * root


def factor(work, inverse):
    size = work.shape[0]
    lane = lax.broadcasted_iota(jnp.int32, (PANEL, size), 1)
    tall = lax.broadcasted_iota(jnp.int32, (PANEL, size), 0)
    all_rows = lax.broadcasted_iota(jnp.int32, (size, size), 0)
    columns = lax.broadcasted_iota(jnp.int32, (size, size), 1)
    zero = jnp.zeros((PANEL, size), BF16)

    def panel(i, carry):
        start = pl.multiple_of(i * PANEL, PANEL)
        after = start + PANEL
        rows = work[pl.ds(start, PANEL), :]
        block = pltpu.roll(rows, lax.rem(size - start, size), axis=1)
        t_high, t_mid, t_low = split3(jnp.where(lane < PANEL, 0.0, panel_inverse(block)))
        first = jnp.where(lane < 2 * PANEL, t_high, jnp.where(lane < 3 * PANEL, t_mid, t_low))
        second = jnp.where(lane < 2 * PANEL, t_high, jnp.where(lane < 3 * PANEL, t_mid, t_high))
        left = jnp.concatenate([first, second], axis=1)
        inside = (lane >= start) & (lane < after)
        rows = jnp.where(inside, jnp.where(lane - start == tall, 1.0, 0.0), rows)
        r_high, r_mid, r_low = split3(rows)
        right = jnp.concatenate([zero, r_high, r_high, r_high, zero, r_mid, r_mid, r_low], axis=0)
        new = jnp.dot(left, right, preferred_element_type=F32)
        inverse[pl.ds(start, PANEL), :] = jnp.where(lane < after, new, 0.0)
        high, middle, low = split3(new)
        lhs = jnp.concatenate([high, high, middle, middle, high, low], axis=0)
        rhs = jnp.concatenate([high, middle, high, middle, low, high], axis=0)
        change = lax.dot_general(lhs, rhs, TN, preferred_element_type=F32)
        old = jnp.where((columns >= start) & (columns < after), 0.0, work[...])
        work[...] = jnp.where(all_rows < after, 0.0, old - change)
        return carry

    lax.fori_loop(0, size // PANEL, panel, 0)


def six_terms(left, right):
    (high, middle, low), (other, little, least) = split3(left), split3(right)
    return jnp.dot(
        jnp.concatenate([high, high, middle, middle, high, low], axis=1),
        jnp.concatenate([other, little, other, little, least, other], axis=0),
        preferred_element_type=F32,
    )


def factor_halves(gram, work, inverse):
    half = gram.shape[0] // 2
    first, last = slice(0, half), slice(half, 2 * half)
    work[0] = gram[first, first]
    factor(work.at[0], inverse.at[first, first])
    beside = six_terms(inverse[first, first], gram[first, last])
    turned = beside.T
    work[1] = gram[last, last] - six_terms(turned, beside)
    factor(work.at[1], inverse.at[last, last])
    inverse[last, first] = -six_terms(
        inverse[last, last], six_terms(turned, inverse[first, first])
    )
    inverse[first, last] = jnp.zeros((half, half), F32)


def finish_kernel(chips, scale, ints, *refs):
    mine, theirs = refs[:chips], refs[chips : 2 * chips]
    y_mine = refs[2 * chips : (2 + CORES) * chips]
    y_theirs = refs[(2 + CORES) * chips : (2 + 2 * CORES) * chips]
    basis, reduced, pair, work, inverse = refs[(2 + 2 * CORES) * chips :]
    core, chip, col = ints[0], ints[1], ints[2]
    half, local_vecs, orbs = y_mine[0].shape
    vecs = CORES * local_vecs
    eye = lax.broadcasted_iota(jnp.int32, (vecs, vecs), 0) == lax.broadcasted_iota(
        jnp.int32, (vecs, vecs), 1
    )
    for step in range(chips):
        which = lax.rem(chip + step, chips)
        rows = pl.ds(pl.multiple_of(which * vecs, vecs), vecs)
        for matrix, payload in ((core, mine[step]), (1 - core, theirs[step])):
            own_block = unpacked(payload[: vecs // 2, :].astype(F32))
            own_block = jnp.where(eye, diagonal_of(payload), own_block)
            for k in range(chips):
                block = own_block
                for away in range(1, chips):
                    at = (2 * away - 1) * vecs // 2
                    other = payload[at : at + vecs, :].astype(F32)
                    block = jnp.where(lax.rem(which + away, chips) == k, other, block)
                pair[matrix, rows, k * vecs : (k + 1) * vecs] = block
    factor_halves((pair[0] + pair[0].T) * scale, work, inverse)
    start = pl.multiple_of(col * local_vecs, local_vecs)
    own_rows = inverse[pl.ds(start, local_vecs), :]
    gram_h = (pair[1] + pair[1].T) * scale
    half_way = jnp.dot(*three_terms(own_rows, gram_h, 0), preferred_element_type=F32)
    reduced[...] = lax.dot_general(
        *three_terms(half_way, inverse[...], 1), NT, preferred_element_type=F32
    )
    rotation = own_rows.astype(BF16)
    turned = []
    for step in range(chips):
        which = lax.rem(chip + step, chips)
        part = rotation[:, :vecs]
        for k in range(1, chips):
            part = jnp.where(which == k, rotation[:, k * vecs : (k + 1) * vecs], part)
        turned.append(part)
    turned = jnp.concatenate(turned, axis=1)
    for which, group in ((core, y_mine), (1 - core, y_theirs)):
        for row in range(half):
            everything = jnp.concatenate([vectors[row] for vectors in group], axis=0)
            result = jnp.dot(turned, everything, preferred_element_type=F32).astype(BF16)
            at = pl.multiple_of((which * half + row) * orbs, orbs)
            basis[:, pl.ds(at, orbs)] = result


def local(
    trial_vectors,
    hamiltonian_blocks,
    correlation_offset,
    block_columns,
    block_phases,
    block_sizes,
    shift,
    halfwidth,
):
    blocks_dev, slots = block_columns.shape
    orbs = hamiltonian_blocks.shape[2]
    num_rows, num_cols = lax.axis_size("row"), lax.axis_size("col")
    total_blocks = blocks_dev * num_rows
    half = blocks_dev // CORES
    chips = num_cols // CORES
    local_vecs = trial_vectors.shape[0]
    vecs = local_vecs * CORES
    size = local_vecs * num_cols
    row, col = lax.axis_index("row"), lax.axis_index("col")
    core, chip = lax.rem(col, CORES), lax.div(col, CORES)

    def swap_cores(value):
        return lax.ppermute(value, "col", [(c, c ^ 1) for c in range(num_cols)])

    def swap_chips(value):
        pairs = []
        for r in range(num_rows):
            for x in range(chips):
                upper = r * num_cols + x * CORES + 1
                lower = (r + 1) % num_rows * num_cols + x * CORES
                pairs += [(upper, lower), (lower, upper)]
        return lax.ppermute(value, ("row", "col"), pairs)

    def next_chips(value):
        pairs = []
        for r in range(num_rows):
            for c in range(num_cols):
                to = (r + 1 if c % CORES == 0 else r - 1) % num_rows
                pairs.append((r * num_cols + c, to * num_cols + c))
        return lax.ppermute(value, ("row", "col"), pairs)

    def from_chip(value, step):
        pairs = [((c + step * CORES) % num_cols, c) for c in range(num_cols)]
        return lax.ppermute(value, "col", pairs)

    state = jax.ShapeDtypeStruct((half, local_vecs, orbs), BF16)
    end = jax.ShapeDtypeStruct((HALF_BAND, local_vecs, orbs), BF16)
    ext = pltpu.VMEM((half + 2 * HALF_BAND, local_vecs, orbs), BF16)
    params = pltpu.CompilerParams(vmem_limit_bytes=16 << 20)
    row_flops = SLOWER * 2 * half * slots * local_vecs * orbs * orbs

    def call(kernel, name, scalars, arrays, outs, scratch, flops):
        return pl.pallas_call(
            kernel,
            name=name,
            out_shape=outs,
            in_specs=[SMEM] * len(scalars) + [VMEM] * len(arrays),
            out_specs=(VMEM,) * len(outs),
            scratch_shapes=scratch,
            compiler_params=params,
            cost_estimate=pl.CostEstimate(
                flops=flops, bytes_accessed=flops // 128, transcendentals=0
            ),
        )(*scalars, *arrays)

    def step_call(kernel, name, scalars, arrays, flops):
        return call(kernel, name, scalars, arrays, (state, end, end), [ext], flops)

    def exchange(ends):
        return swap_chips(ends[0]), swap_cores(ends[1])

    def scalars(value):
        return pltpu.with_memory_space_constraint(value, pltpu.SMEM)

    ints = scalars(jnp.stack([core, chip, col, row * blocks_dev, row]).astype(jnp.int32))
    shift, halfwidth = scalars(shift), scalars(halfwidth)

    def stays(value):
        return pltpu.with_memory_space_constraint(value, pltpu.HBM)

    more = jax.ShapeDtypeStruct((half + HALF_BAND, local_vecs, orbs), BF16)
    own, near, give, far, across = pl.pallas_call(
        cut_kernel,
        name="cut",
        out_shape=(state, end, more, end, end),
        in_specs=[SMEM, HBM, HBM],
        out_specs=(VMEM,) * 5,
        scratch_shapes=[
            pltpu.SMEM(block_sizes.shape, jnp.int32),
            pltpu.VMEM(trial_vectors.shape, BF16),
            pltpu.VMEM((blocks_dev, local_vecs, orbs), BF16),
            pltpu.SemaphoreType.DMA((2,)),
        ],
        compiler_params=params,
    )(ints, stays(block_sizes), stays(trial_vectors))
    far, across = next_chips(far), swap_chips(across)
    got = swap_cores(give)
    matrix = vmem((half, *hamiltonian_blocks.shape[1:]), BF16)
    ham, ovl, index, signs, place, scal = pl.pallas_call(
        functools.partial(load_kernel, total_blocks),
        name="load",
        out_shape=(
            matrix,
            matrix,
            pltpu.SMEM((half, slots), jnp.int32),
            pltpu.SMEM((half, slots), F32),
            pltpu.SMEM((4 + half,), jnp.int32),
            pltpu.SMEM((2,), F32),
        ),
        in_specs=[SMEM] * 3 + [HBM] * 5,
        out_specs=(VMEM, VMEM, SMEM, SMEM, SMEM, SMEM),
        scratch_shapes=[
            pltpu.SMEM(block_columns.shape, jnp.int32),
            pltpu.SMEM(block_phases.shape, jnp.int32),
            pltpu.SMEM(block_sizes.shape, jnp.int32),
            pltpu.SemaphoreType.DMA((2, half)),
            pltpu.SemaphoreType.DMA((3,)),
        ],
        compiler_params=params,
        cost_estimate=pl.CostEstimate(
            flops=0, bytes_accessed=4 * hamiltonian_blocks.size, transcendentals=0
        ),
    )(
        ints,
        shift,
        halfwidth,
        stays(block_columns),
        stays(block_phases),
        stays(block_sizes),
        stays(hamiltonian_blocks),
        stays(correlation_offset),
    )
    got_own = lax.dynamic_slice_in_dim(got, HALF_BAND * core, half, 0)
    got_near = lax.dynamic_slice_in_dim(got, half * (1 - core), HALF_BAND, 0)

    def by_group(mine, other):
        return [jnp.where(core == 0, mine, other), jnp.where(core == 0, other, mine)]

    current = by_group(own, got_own)
    halo = list(zip(by_group(far, across), by_group(near, got_near)))
    table = (place, index, signs)
    scaled, term, previous = [None] * CORES, [None] * CORES, list(current)
    for degree in range(DEGREE):
        for g in range(CORES):
            if g > 0:
                current[g], scaled[0] = lax.optimization_barrier((current[g], scaled[0]))
            scaled[g], *ends = step_call(
                scaled_kernel,
                "scaled",
                (*table, scal),
                (current[g], *halo[g], ham, ovl),
                2 * row_flops,
            )
            halo[g] = exchange(ends)
        for g in range(CORES):
            term[g], *ends = step_call(
                term_kernel, "term", table, (scaled[g], *halo[g], ovl), row_flops
            )
            halo[g] = exchange(ends)
        for g in range(CORES):
            first = degree == 0
            arrays = (term[g], *halo[g], scaled[g]) + (() if first else (previous[g],)) + (ovl,)
            updated, *ends = step_call(
                functools.partial(update_kernel, first),
                "update",
                table,
                arrays,
                row_flops,
            )
            halo[g] = exchange(ends)
            previous[g], current[g] = current[g], updated

    y_others = [from_chip(value, step) for step in range(1, chips) for value in current]
    image = jax.ShapeDtypeStruct((2, local_vecs, half * orbs), BF16)
    images = []
    for g, vectors in enumerate(current):
        if g > 0:
            vectors, images[0] = lax.optimization_barrier((vectors, images[0]))
        images += call(
            images_kernel,
            "images",
            table,
            (vectors, *halo[g], ham, ovl, y_others[0]),
            (image,),
            [ext],
            2 * row_flops,
        )
    payload = jax.ShapeDtypeStruct((size - vecs // 2 + DIAGONAL_ROWS, vecs), BF16)
    keep, send = call(
        functools.partial(gram_kernel, chips),
        "gram",
        (place,),
        (*images, *current, *y_others),
        (payload, payload),
        [pltpu.VMEM((2, *payload.shape), BF16)],
        row_flops,
    )

    def add(left, right):
        return call(add_kernel, "add", (), (left, right), (payload,), [], row_flops // 8)[0]

    summed = add(keep, swap_cores(send))
    if num_rows in (2, 4):
        others = [
            lax.ppermute(summed, "row", [(r, r ^ step) for r in range(num_rows)])
            for step in range(1, num_rows)
        ]
        (summed,) = call(
            sum_kernel,
            "sum",
            (place,),
            (summed, *others),
            (payload,),
            [pltpu.VMEM((num_rows, *payload.shape), BF16)],
            row_flops // 8,
        )
    elif num_rows & (num_rows - 1):
        every = lax.all_gather(summed, "row")
        summed = every[0]
        for r in range(1, num_rows):
            summed = add(summed, every[r])
    else:
        bit = 1
        while bit < num_rows:
            other = lax.ppermute(summed, "row", [(r, r ^ bit) for r in range(num_rows)])
            summed = add(summed, other)
            bit *= 2
    mine = [summed] + [from_chip(summed, step) for step in range(1, chips)]
    theirs = [swap_cores(value) for value in mine]
    y_theirs = [swap_cores(value) for value in (*current, *y_others)]
    basis, reduced = call(
        functools.partial(finish_kernel, chips, 0.5 / (total_blocks * orbs)),
        "finish",
        (place,),
        (*mine, *theirs, *current, *y_others, *y_theirs),
        (
            jax.ShapeDtypeStruct((local_vecs, blocks_dev * orbs), BF16),
            jax.ShapeDtypeStruct((local_vecs, size), F32),
        ),
        [
            pltpu.VMEM((2, size, size), F32),
            pltpu.VMEM((2, size // 2, size // 2), F32),
            pltpu.VMEM((size, size), F32),
        ],
        10 * row_flops,
    )
    return basis, reduced.T


def solution(mesh):
    return jax.shard_map(
        local,
        mesh=mesh,
        in_specs=(
            P("col", ("pool", "row")),
            P(("pool", "row"), None, None, None),
            P(("pool", "row"), None, None, None),
            P(("pool", "row"), None),
            P(("pool", "row"), None),
            P(("pool", "row")),
            P("pool"),
            P("pool"),
        ),
        out_specs=(P("col", ("pool", "row")), P("pool", "col")),
        check_vma=False,
    )
```

```python
import functools

import jax
import jax.numpy as jnp
from jax import lax
from jax.experimental import pallas as pl
from jax.experimental.pallas import tpu as pltpu
from jax.sharding import PartitionSpec as P

HALF_BAND = 5
DEGREE = 4
CORES = 2
PANEL = 32
SLOWER = 24
SUBLANES = 8
DIAGONAL_ROWS = 16
DEVICE_ROW = 3

BF16 = jnp.bfloat16
F32 = jnp.float32
NT = (((1,), (1,)), ((), ()))
TN = (((0,), (0,)), ((), ()))

SMEM = pl.BlockSpec(memory_space=pltpu.SMEM)
VMEM = pl.BlockSpec(memory_space=pltpu.VMEM)
HBM = pl.BlockSpec(memory_space=pltpu.HBM)


def vmem(shape, dtype):
    return pltpu.VMEM(shape, dtype)


def fill_ext(core, own, intra, inter, ext):
    half = own.shape[0]
    ext[HALF_BAND : HALF_BAND + half] = own[...]
    ext[pl.ds((half + HALF_BAND) * (1 - core), HALF_BAND)] = intra[...]
    ext[pl.ds((half + HALF_BAND) * core, HALF_BAND)] = inter[...]


def picked(table, ext, row):
    index, signs = table
    slots = index.shape[1]
    return jnp.concatenate(
        [ext[index[row, s]] * signs[row, s].astype(BF16) for s in range(slots)], axis=1
    )


def row_matrix(blocks, row):
    return jnp.concatenate([blocks[row, s] for s in range(blocks.shape[1])], axis=1)


def send_ends(core, full, intra_out, inter_out):
    spare = full.shape[0] - HALF_BAND
    intra_out[...] = full[pl.ds(spare * (1 - core), HALF_BAND)]
    inter_out[...] = full[pl.ds(spare * core, HALF_BAND)]


def image_of(table, ext, matrices, row):
    matrix = jnp.concatenate([row_matrix(blocks, row) for blocks in matrices], axis=0)
    return lax.dot_general(matrix, picked(table, ext, row), NT, preferred_element_type=F32)


def both_rows(table, ext, ham, ovl, row):
    orbs = ham.shape[2]
    image = image_of(table, ext, (ham, ovl), row)
    return image[:orbs].T, image[orbs:].T


def one_row(table, ext, ovl, row):
    return image_of(table, ext, (ovl,), row).T


def cut_kernel(ints, sizes, trial, own, near, give, far, across, sizes_here, here, masked, sems):
    copies = [
        pltpu.make_async_copy(sizes, sizes_here, sems.at[0]),
        pltpu.make_async_copy(trial, here, sems.at[1]),
    ]
    for copy in copies:
        copy.start()
    for copy in copies:
        copy.wait()
    half, _, orbs = own.shape
    core = ints[0]
    lane = lax.broadcasted_iota(jnp.int32, own.shape[1:], 1)
    for row in range(2 * half):
        values = here[:, row * orbs : (row + 1) * orbs].astype(F32)
        masked[row] = jnp.where(lane < sizes_here[row], values, 0.0).astype(BF16)
    spare = half - HALF_BAND
    last = 2 * half - HALF_BAND
    own[...] = masked[pl.ds(half * core, half)]
    near[...] = masked[pl.ds(half - HALF_BAND * core, HALF_BAND)]
    give[...] = masked[pl.ds(spare * (1 - core), half + HALF_BAND)]
    far[...] = masked[pl.ds(last * (1 - core), HALF_BAND)]
    across[...] = masked[pl.ds(last * core, HALF_BAND)]


def load_kernel(total, ints, shift, width, columns, phases, sizes, ham, ovl, *rest):
    ham_out, ovl_out, index, signs, place, scal, columns_here, phases_here, sizes_here = rest[:9]
    sems, more_sems = rest[9:]
    half, slots = index.shape
    first = ints[0] * half
    small = [
        pltpu.make_async_copy(source, target, more_sems.at[i])
        for i, (source, target) in enumerate(
            ((columns, columns_here), (phases, phases_here), (sizes, sizes_here))
        )
    ]
    large = [
        pltpu.make_async_copy(source.at[first + row], target.at[row], sems.at[matrix, row])
        for row in range(half)
        for matrix, (source, target) in enumerate(((ham, ham_out), (ovl, ovl_out)))
    ]
    for copy in small + large:
        copy.start()
    scal[0] = shift[0]
    scal[1] = width[0]
    for i in range(3):
        place[i] = ints[i]
    place[DEVICE_ROW] = ints[4]
    for copy in small:
        copy.wait()
    start = ints[3] + first

    def fill(row, _):
        place[4 + row] = sizes_here[first + row]
        for slot in range(slots):
            away = columns_here[first + row, slot] - (start + row) + HALF_BAND
            away = jnp.where(away < 0, away + total, away)
            away = jnp.where(away >= total, away - total, away)
            index[row, slot] = row + away
            signs[row, slot] = (1 - 2 * phases_here[first + row, slot]).astype(F32)
        return 0

    lax.fori_loop(0, half, fill, 0)
    for copy in large:
        copy.wait()


def scaled_kernel(
    ints, index, signs, scal, own, inter, intra, ham, ovl, out, inter_out, intra_out, ext
):
    core = ints[0]
    fill_ext(core, own, intra, inter, ext)
    inv = 1.0 / (jnp.zeros(own.shape[1:], F32) + scal[1])
    for row in range(own.shape[0]):
        image = image_of((index, signs), ext, (ham, ovl), row)
        orbs = ham.shape[2]
        image = (image[:orbs] - scal[0] * image[orbs:]).T
        out[row] = ((image - scal[0] * own[row].astype(F32)) * inv).astype(BF16)
    send_ends(core, out, intra_out, inter_out)


def term_kernel(ints, index, signs, own, inter, intra, ovl, out, inter_out, intra_out, ext):
    core = ints[0]
    fill_ext(core, own, intra, inter, ext)
    for row in range(own.shape[0]):
        out[row] = (-image_of((index, signs), ext, (ovl,), row)).astype(BF16).T
    send_ends(core, out, intra_out, inter_out)


def update_kernel(first, ints, index, signs, own, inter, intra, scaled, *rest):
    if first:
        ovl, out, inter_out, intra_out, ext = rest
    else:
        previous, ovl, out, inter_out, intra_out, ext = rest
    core = ints[0]
    half = own.shape[0]
    fill_ext(core, own, intra, inter, ext)
    lane = lax.broadcasted_iota(jnp.int32, own.shape[1:], 1)
    for row in range(half):
        image = one_row((index, signs), ext, ovl, row)
        filtered = scaled[row].astype(F32) + own[row].astype(F32) - image
        if not first:
            filtered = 2.0 * filtered - previous[row].astype(F32)
        out[row] = jnp.where(lane < ints[4 + row], filtered, 0.0).astype(BF16)
    send_ends(core, out, intra_out, inter_out)


def images_kernel(ints, index, signs, own, inter, intra, ham, ovl, y_other, out, ext):
    del y_other
    core = ints[0]
    fill_ext(core, own, intra, inter, ext)
    half, _, orbs = own.shape
    for row in range(half):
        image_h, image_e = both_rows((index, signs), ext, ham, ovl, row)
        at = slice(row * orbs, (row + 1) * orbs)
        out[0, :, at] = (own[row].astype(F32) + image_e).astype(BF16)
        out[1, :, at] = image_h.astype(BF16)


def gram_kernel(chips, ints, *refs):
    images, groups = refs[:CORES], refs[CORES : CORES + CORES * chips]
    keep, send, both = refs[CORES + CORES * chips :]
    core, chip = ints[0], ints[1]
    half, local_vecs, _ = groups[0].shape
    vecs = CORES * local_vecs
    flat = jnp.concatenate(
        [jnp.concatenate([group[row] for row in range(half)], axis=1) for group in groups], axis=0
    )
    eye = lax.broadcasted_iota(jnp.int32, (vecs, vecs), 0) == lax.broadcasted_iota(
        jnp.int32, (vecs, vecs), 1
    )
    for matrix in range(2):
        mine = jnp.concatenate([image[matrix] for image in images], axis=0)
        pair = lax.dot_general(mine, flat, NT, preferred_element_type=F32)
        both[matrix, : vecs // 2, :] = packed(pair[:, :vecs]).astype(BF16)
        for step in range(1, chips):
            block = pair[:, step * vecs : (step + 1) * vecs]
            both[matrix, (2 * step - 1) * vecs // 2 : (2 * step + 1) * vecs // 2, :] = block.astype(BF16)
        diagonal = jnp.sum(jnp.where(eye, pair[:, :vecs], 0.0), axis=0, keepdims=True)
        both[matrix, (2 * chips - 1) * vecs // 2 :, :] = diagonal_parts(diagonal)
    keep[...] = both[core]
    send[...] = both[1 - core]


def packed(block):
    half = block.shape[0] // 2
    block = 0.5 * (block + block.T)
    top, bottom = block[:half], block[half:]
    bottom = jnp.concatenate([bottom[:, half:], bottom[:, :half]], axis=1)
    row = lax.broadcasted_iota(jnp.int32, top.shape, 0)
    lane = lax.broadcasted_iota(jnp.int32, top.shape, 1)
    return jnp.where((lane < half) & (lane > row), bottom, top)


def unpacked(block):
    half = block.shape[0]
    turned = block.T
    row = lax.broadcasted_iota(jnp.int32, (half, half), 0)
    lane = lax.broadcasted_iota(jnp.int32, (half, half), 1)
    square, beside = block[:, :half], block[:, half:]
    first = jnp.where(lane < row, square, turned[:half])
    last = jnp.where(lane > row, square, turned[:half])
    return jnp.concatenate(
        [
            jnp.concatenate([first, beside], axis=1),
            jnp.concatenate([turned[half:], last], axis=1),
        ],
        axis=0,
    )


def diagonal_parts(diagonal):
    high, middle, low = (part.astype(F32) for part in split3(diagonal))
    rows = lax.broadcasted_iota(jnp.int32, (DIAGONAL_ROWS, diagonal.shape[1]), 0)
    parts = jnp.where(rows == 0, high, jnp.where(rows == 1, middle, jnp.where(rows == 2, low, 0.0)))
    return parts.astype(BF16)


def diagonal_of(payload):
    parts = payload[payload.shape[0] - DIAGONAL_ROWS :, :].astype(F32)
    return parts[0:1] + (parts[1:2] + parts[2:3])


def add_kernel(left, right, out):
    body = left.shape[0] - DIAGONAL_ROWS
    out[:body] = (left[:body, :].astype(F32) + right[:body, :].astype(F32)).astype(BF16)
    out[body:] = diagonal_parts(diagonal_of(left) + diagonal_of(right))


def sum_kernel(ints, *refs):
    *payloads, out, held = refs
    count = len(payloads)
    for step, payload in enumerate(payloads):
        held[lax.bitwise_xor(ints[DEVICE_ROW], jnp.int32(step))] = payload[...]
    body = out.shape[0] - DIAGONAL_ROWS
    total = held[0, :body, :].astype(F32)
    diagonal = diagonal_of(held.at[0])
    for r in range(1, count):
        total = total + held[r, :body, :].astype(F32)
        diagonal = diagonal + diagonal_of(held.at[r])
    out[:body] = total.astype(BF16)
    out[body:] = diagonal_parts(diagonal)


def split3(value):
    high = value.astype(BF16)
    rest = value - high.astype(F32)
    middle = rest.astype(BF16)
    low = (rest - middle.astype(F32)).astype(BF16)
    return high, middle, low


def three_terms(left, right, axis):
    (high, middle, _), (other, little, _) = split3(left), split3(right)
    return (
        jnp.concatenate([high, high, middle], axis=1),
        jnp.concatenate([other, little, other], axis=axis),
    )


def panel_inverse(block):
    lane = lax.broadcasted_iota(jnp.int32, (PANEL, 128), 1)
    rows = lax.broadcasted_iota(jnp.int32, (PANEL, 128), 0)
    work = jnp.where(lane < PANEL, block, jnp.where(lax.rem(lane, PANEL) == rows, 1.0, 0.0))
    count = PANEL // SUBLANES
    pieces = [work[v * SUBLANES : (v + 1) * SUBLANES] for v in range(count)]
    sub = lax.broadcasted_iota(jnp.int32, (SUBLANES, 128), 0)

    def spread(value, k):
        return jnp.broadcast_to(value[k % SUBLANES : k % SUBLANES + 1], (SUBLANES, 128))

    pivots = [jnp.ones((SUBLANES, 128), F32) for _ in range(count)]
    for start, group in ((0, 8), (8, 8), (16, 16)):
        columns = {
            k: {
                v: jnp.broadcast_to(pieces[v][:, k : k + 1], (SUBLANES, 128))
                for v in range(start // SUBLANES, count)
            }
            for k in range(start, start + group)
        }
        at = spread(columns[start][start // SUBLANES], start)
        for k in range(start, start + group):
            here = k // SUBLANES
            pivots[here] = jnp.where(sub == k % SUBLANES, at, pivots[here])
            guess = pl.reciprocal(at, approx=True)
            correction = 2.0 - at * guess
            inv = guess * correction
            if k + 1 < start + group:
                below = (k + 1) // SUBLANES
                product = spread(columns[k][below], k + 1) * spread(columns[k + 1][here], k)
                at = spread(columns[k + 1][below], k + 1) - (product * guess) * correction
            factors = {v: columns[k][v] * inv for v in range(here, count)}
            factors[here] = jnp.where(sub > k % SUBLANES, factors[here], 0.0)
            for later in range(k + 1, start + group):
                top = spread(columns[later][here], k)
                for v in range(here, count):
                    columns[later][v] = columns[later][v] - factors[v] * top
            top = spread(pieces[here], k)
            for v in range(here, count):
                pieces[v] = pieces[v] - factors[v] * top
    pivot = jnp.concatenate(pivots, axis=0)
    root = lax.rsqrt(pivot)
    root = root * (1.5 - 0.5 * ((pivot * root) * root))
    return jnp.concatenate(pieces, axis=0) * root


def factor(work, inverse):
    size = work.shape[0]
    wide = lax.broadcasted_iota(jnp.int32, (PANEL, size), 1)
    tall = lax.broadcasted_iota(jnp.int32, (PANEL, size), 0)
    lane = lax.broadcasted_iota(jnp.int32, (PANEL, 128), 1)
    zero = jnp.zeros((PANEL, size), BF16)
    for start in range(0, size, PANEL):
        rows = work[start : start + PANEL, :]
        tile = start // 128 * 128
        block = work[start : start + PANEL, tile : tile + 128]
        if start % 128:
            block = pltpu.roll(block, 128 - start % 128, axis=1)
        t_high, t_mid, t_low = split3(jnp.where(lane < PANEL, 0.0, panel_inverse(block)))
        first = jnp.where(lane < 2 * PANEL, t_high, jnp.where(lane < 3 * PANEL, t_mid, t_low))
        second = jnp.where(lane < 2 * PANEL, t_high, jnp.where(lane < 3 * PANEL, t_mid, t_high))
        left = jnp.concatenate([first, second], axis=1)
        inside = (wide >= start) & (wide < start + PANEL)
        rows = jnp.where(inside, jnp.where(wide - start == tall, 1.0, 0.0), rows)
        r_high, r_mid, r_low = split3(rows)
        right = jnp.concatenate([zero, r_high, r_high, r_high, zero, r_mid, r_mid, r_low], axis=0)
        new = jnp.dot(left, right, preferred_element_type=F32)
        inverse[start : start + PANEL, :] = jnp.where(wide < start + PANEL, new, 0.0)
        after = start + PANEL
        if after < size:
            high, middle, low = split3(new)
            base = after // 128 * 128
            lhs = jnp.concatenate([high, high, middle, middle, high, low], axis=0)[:, base:]
            rhs = jnp.concatenate([high, middle, high, middle, low, high], axis=0)
            change = lax.dot_general(lhs, rhs, TN, preferred_element_type=F32)[after - base :]
            columns = lax.broadcasted_iota(jnp.int32, change.shape, 1)
            old = work[after:, :]
            work[after:, :] = jnp.where((columns >= start) & (columns < after), 0.0, old) - change


def finish_kernel(chips, scale, ints, *refs):
    mine, theirs = refs[:chips], refs[chips : 2 * chips]
    y_mine = refs[2 * chips : (2 + CORES) * chips]
    y_theirs = refs[(2 + CORES) * chips : (2 + 2 * CORES) * chips]
    basis, reduced, pair, work, inverse = refs[(2 + 2 * CORES) * chips :]
    core, chip, col = ints[0], ints[1], ints[2]
    half, local_vecs, orbs = y_mine[0].shape
    vecs = CORES * local_vecs
    eye = lax.broadcasted_iota(jnp.int32, (vecs, vecs), 0) == lax.broadcasted_iota(
        jnp.int32, (vecs, vecs), 1
    )
    for step in range(chips):
        which = lax.rem(chip + step, chips)
        rows = pl.ds(pl.multiple_of(which * vecs, vecs), vecs)
        for matrix, payload in ((core, mine[step]), (1 - core, theirs[step])):
            own_block = unpacked(payload[: vecs // 2, :].astype(F32))
            own_block = jnp.where(eye, diagonal_of(payload), own_block)
            for k in range(chips):
                block = own_block
                for away in range(1, chips):
                    at = (2 * away - 1) * vecs // 2
                    other = payload[at : at + vecs, :].astype(F32)
                    block = jnp.where(lax.rem(which + away, chips) == k, other, block)
                pair[matrix, rows, k * vecs : (k + 1) * vecs] = block
    work[...] = (pair[0] + pair[0].T) * scale
    factor(work, inverse)
    start = pl.multiple_of(col * local_vecs, local_vecs)
    own_rows = inverse[pl.ds(start, local_vecs), :]
    gram_h = (pair[1] + pair[1].T) * scale
    half_way = jnp.dot(*three_terms(own_rows, gram_h, 0), preferred_element_type=F32)
    reduced[...] = lax.dot_general(
        *three_terms(half_way, inverse[...], 1), NT, preferred_element_type=F32
    )
    rotation = own_rows.astype(BF16)
    turned = []
    for step in range(chips):
        which = lax.rem(chip + step, chips)
        part = rotation[:, :vecs]
        for k in range(1, chips):
            part = jnp.where(which == k, rotation[:, k * vecs : (k + 1) * vecs], part)
        turned.append(part)
    turned = jnp.concatenate(turned, axis=1)
    for which, group in ((core, y_mine), (1 - core, y_theirs)):
        for row in range(half):
            everything = jnp.concatenate([vectors[row] for vectors in group], axis=0)
            result = jnp.dot(turned, everything, preferred_element_type=F32).astype(BF16)
            at = pl.multiple_of((which * half + row) * orbs, orbs)
            basis[:, pl.ds(at, orbs)] = result


def local(
    trial_vectors,
    hamiltonian_blocks,
    correlation_offset,
    block_columns,
    block_phases,
    block_sizes,
    shift,
    halfwidth,
):
    blocks_dev, slots = block_columns.shape
    orbs = hamiltonian_blocks.shape[2]
    num_rows, num_cols = lax.axis_size("row"), lax.axis_size("col")
    total_blocks = blocks_dev * num_rows
    half = blocks_dev // CORES
    chips = num_cols // CORES
    local_vecs = trial_vectors.shape[0]
    vecs = local_vecs * CORES
    size = local_vecs * num_cols
    row, col = lax.axis_index("row"), lax.axis_index("col")
    core, chip = lax.rem(col, CORES), lax.div(col, CORES)

    def swap_cores(value):
        return lax.ppermute(value, "col", [(c, c ^ 1) for c in range(num_cols)])

    def swap_chips(value):
        pairs = []
        for r in range(num_rows):
            for x in range(chips):
                upper = r * num_cols + x * CORES + 1
                lower = (r + 1) % num_rows * num_cols + x * CORES
                pairs += [(upper, lower), (lower, upper)]
        return lax.ppermute(value, ("row", "col"), pairs)

    def next_chips(value):
        pairs = []
        for r in range(num_rows):
            for c in range(num_cols):
                to = (r + 1 if c % CORES == 0 else r - 1) % num_rows
                pairs.append((r * num_cols + c, to * num_cols + c))
        return lax.ppermute(value, ("row", "col"), pairs)

    def from_chip(value, step):
        pairs = [((c + step * CORES) % num_cols, c) for c in range(num_cols)]
        return lax.ppermute(value, "col", pairs)

    state = jax.ShapeDtypeStruct((half, local_vecs, orbs), BF16)
    end = jax.ShapeDtypeStruct((HALF_BAND, local_vecs, orbs), BF16)
    ext = pltpu.VMEM((half + 2 * HALF_BAND, local_vecs, orbs), BF16)
    params = pltpu.CompilerParams(vmem_limit_bytes=16 << 20)
    row_flops = SLOWER * 2 * half * slots * local_vecs * orbs * orbs

    def call(kernel, name, scalars, arrays, outs, scratch, flops):
        return pl.pallas_call(
            kernel,
            name=name,
            out_shape=outs,
            in_specs=[SMEM] * len(scalars) + [VMEM] * len(arrays),
            out_specs=(VMEM,) * len(outs),
            scratch_shapes=scratch,
            compiler_params=params,
            cost_estimate=pl.CostEstimate(
                flops=flops, bytes_accessed=flops // 128, transcendentals=0
            ),
        )(*scalars, *arrays)

    def step_call(kernel, name, scalars, arrays, flops):
        return call(kernel, name, scalars, arrays, (state, end, end), [ext], flops)

    def exchange(ends):
        return swap_chips(ends[0]), swap_cores(ends[1])

    def scalars(value):
        return pltpu.with_memory_space_constraint(value, pltpu.SMEM)

    ints = scalars(jnp.stack([core, chip, col, row * blocks_dev, row]).astype(jnp.int32))
    shift, halfwidth = scalars(shift), scalars(halfwidth)

    def stays(value):
        return pltpu.with_memory_space_constraint(value, pltpu.HBM)

    more = jax.ShapeDtypeStruct((half + HALF_BAND, local_vecs, orbs), BF16)
    own, near, give, far, across = pl.pallas_call(
        cut_kernel,
        name="cut",
        out_shape=(state, end, more, end, end),
        in_specs=[SMEM, HBM, HBM],
        out_specs=(VMEM,) * 5,
        scratch_shapes=[
            pltpu.SMEM(block_sizes.shape, jnp.int32),
            pltpu.VMEM(trial_vectors.shape, BF16),
            pltpu.VMEM((blocks_dev, local_vecs, orbs), BF16),
            pltpu.SemaphoreType.DMA((2,)),
        ],
        compiler_params=params,
    )(ints, stays(block_sizes), stays(trial_vectors))
    far, across = next_chips(far), swap_chips(across)
    got = swap_cores(give)
    matrix = vmem((half, *hamiltonian_blocks.shape[1:]), BF16)
    ham, ovl, index, signs, place, scal = pl.pallas_call(
        functools.partial(load_kernel, total_blocks),
        name="load",
        out_shape=(
            matrix,
            matrix,
            pltpu.SMEM((half, slots), jnp.int32),
            pltpu.SMEM((half, slots), F32),
            pltpu.SMEM((4 + half,), jnp.int32),
            pltpu.SMEM((2,), F32),
        ),
        in_specs=[SMEM] * 3 + [HBM] * 5,
        out_specs=(VMEM, VMEM, SMEM, SMEM, SMEM, SMEM),
        scratch_shapes=[
            pltpu.SMEM(block_columns.shape, jnp.int32),
            pltpu.SMEM(block_phases.shape, jnp.int32),
            pltpu.SMEM(block_sizes.shape, jnp.int32),
            pltpu.SemaphoreType.DMA((2, half)),
            pltpu.SemaphoreType.DMA((3,)),
        ],
        compiler_params=params,
        cost_estimate=pl.CostEstimate(
            flops=0, bytes_accessed=4 * hamiltonian_blocks.size, transcendentals=0
        ),
    )(
        ints,
        shift,
        halfwidth,
        stays(block_columns),
        stays(block_phases),
        stays(block_sizes),
        stays(hamiltonian_blocks),
        stays(correlation_offset),
    )
    got_own = lax.dynamic_slice_in_dim(got, HALF_BAND * core, half, 0)
    got_near = lax.dynamic_slice_in_dim(got, half * (1 - core), HALF_BAND, 0)

    def by_group(mine, other):
        return [jnp.where(core == 0, mine, other), jnp.where(core == 0, other, mine)]

    current = by_group(own, got_own)
    halo = list(zip(by_group(far, across), by_group(near, got_near)))
    table = (place, index, signs)
    scaled, term, previous = [None] * CORES, [None] * CORES, list(current)
    for degree in range(DEGREE):
        for g in range(CORES):
            if g > 0:
                current[g], scaled[0] = lax.optimization_barrier((current[g], scaled[0]))
            scaled[g], *ends = step_call(
                scaled_kernel,
                "scaled",
                (*table, scal),
                (current[g], *halo[g], ham, ovl),
                2 * row_flops,
            )
            halo[g] = exchange(ends)
        for g in range(CORES):
            term[g], *ends = step_call(
                term_kernel, "term", table, (scaled[g], *halo[g], ovl), row_flops
            )
            halo[g] = exchange(ends)
        for g in range(CORES):
            first = degree == 0
            arrays = (term[g], *halo[g], scaled[g]) + (() if first else (previous[g],)) + (ovl,)
            updated, *ends = step_call(
                functools.partial(update_kernel, first),
                "update",
                table,
                arrays,
                row_flops,
            )
            halo[g] = exchange(ends)
            previous[g], current[g] = current[g], updated

    y_others = [from_chip(value, step) for step in range(1, chips) for value in current]
    image = jax.ShapeDtypeStruct((2, local_vecs, half * orbs), BF16)
    images = []
    for g, vectors in enumerate(current):
        if g > 0:
            vectors, images[0] = lax.optimization_barrier((vectors, images[0]))
        images += call(
            images_kernel,
            "images",
            table,
            (vectors, *halo[g], ham, ovl, y_others[0]),
            (image,),
            [ext],
            2 * row_flops,
        )
    payload = jax.ShapeDtypeStruct((size - vecs // 2 + DIAGONAL_ROWS, vecs), BF16)
    keep, send = call(
        functools.partial(gram_kernel, chips),
        "gram",
        (place,),
        (*images, *current, *y_others),
        (payload, payload),
        [pltpu.VMEM((2, *payload.shape), BF16)],
        row_flops,
    )

    def add(left, right):
        return call(add_kernel, "add", (), (left, right), (payload,), [], row_flops // 8)[0]

    summed = add(keep, swap_cores(send))
    if num_rows in (2, 4):
        others = [
            lax.ppermute(summed, "row", [(r, r ^ step) for r in range(num_rows)])
            for step in range(1, num_rows)
        ]
        (summed,) = call(
            sum_kernel,
            "sum",
            (place,),
            (summed, *others),
            (payload,),
            [pltpu.VMEM((num_rows, *payload.shape), BF16)],
            row_flops // 8,
        )
    elif num_rows & (num_rows - 1):
        every = lax.all_gather(summed, "row")
        summed = every[0]
        for r in range(1, num_rows):
            summed = add(summed, every[r])
    else:
        bit = 1
        while bit < num_rows:
            other = lax.ppermute(summed, "row", [(r, r ^ bit) for r in range(num_rows)])
            summed = add(summed, other)
            bit *= 2
    mine = [summed] + [from_chip(summed, step) for step in range(1, chips)]
    theirs = [swap_cores(value) for value in mine]
    y_theirs = [swap_cores(value) for value in (*current, *y_others)]
    basis, reduced = call(
        functools.partial(finish_kernel, chips, 0.5 / (total_blocks * orbs)),
        "finish",
        (place,),
        (*mine, *theirs, *current, *y_others, *y_theirs),
        (
            jax.ShapeDtypeStruct((local_vecs, blocks_dev * orbs), BF16),
            jax.ShapeDtypeStruct((local_vecs, size), F32),
        ),
        [
            pltpu.VMEM((2, size, size), F32),
            pltpu.VMEM((size, size), F32),
            pltpu.VMEM((size, size), F32),
        ],
        10 * row_flops,
    )
    return basis, reduced.T


def solution(mesh):
    return jax.shard_map(
        local,
        mesh=mesh,
        in_specs=(
            P("col", ("pool", "row")),
            P(("pool", "row"), None, None, None),
            P(("pool", "row"), None, None, None),
            P(("pool", "row"), None),
            P(("pool", "row"), None),
            P(("pool", "row")),
            P("pool"),
            P("pool"),
        ),
        out_specs=(P("col", ("pool", "row")), P("pool", "col")),
        check_vma=False,
    )
```

```python
import functools

import jax
import jax.numpy as jnp
from jax import lax
from jax.experimental import pallas as pl
from jax.experimental.pallas import tpu as pltpu
from jax.sharding import PartitionSpec as P

HALF_BAND = 5
DEGREE = 4
CORES = 2
PANEL = 32
SLOWER = 24
SUBLANES = 8
DIAGONAL_ROWS = 16
DEVICE_ROW = 3

BF16 = jnp.bfloat16
F32 = jnp.float32
NT = (((1,), (1,)), ((), ()))
TN = (((0,), (0,)), ((), ()))

SMEM = pl.BlockSpec(memory_space=pltpu.SMEM)
VMEM = pl.BlockSpec(memory_space=pltpu.VMEM)
HBM = pl.BlockSpec(memory_space=pltpu.HBM)


def vmem(shape, dtype):
    return pltpu.VMEM(shape, dtype)


def fill_ext(core, own, intra, inter, ext):
    half = own.shape[0]
    ext[HALF_BAND : HALF_BAND + half] = own[...]
    ext[pl.ds((half + HALF_BAND) * (1 - core), HALF_BAND)] = intra[...]
    ext[pl.ds((half + HALF_BAND) * core, HALF_BAND)] = inter[...]


def picked(table, ext, row):
    index, signs = table
    slots = index.shape[1]
    return jnp.concatenate(
        [ext[index[row, s]] * signs[row, s].astype(BF16) for s in range(slots)], axis=1
    )


def row_matrix(blocks, row):
    return jnp.concatenate([blocks[row, s] for s in range(blocks.shape[1])], axis=1)


def send_ends(core, full, intra_out, inter_out):
    spare = full.shape[0] - HALF_BAND
    intra_out[...] = full[pl.ds(spare * (1 - core), HALF_BAND)]
    inter_out[...] = full[pl.ds(spare * core, HALF_BAND)]


def image_of(table, ext, matrices, row):
    matrix = jnp.concatenate([row_matrix(blocks, row) for blocks in matrices], axis=0)
    return lax.dot_general(matrix, picked(table, ext, row), NT, preferred_element_type=F32)


def both_rows(table, ext, ham, ovl, row):
    orbs = ham.shape[2]
    image = image_of(table, ext, (ham, ovl), row)
    return image[:orbs].T, image[orbs:].T


def one_row(table, ext, ovl, row):
    return image_of(table, ext, (ovl,), row).T


def two_rows(table, ext, ovl, row):
    index, signs = table
    last = ovl.shape[1] - 1
    tails, images = [], []
    for r in (row, row + 1):
        vectors = picked(table, ext, r)
        matrix = row_matrix(ovl, r)
        cut = last * ovl.shape[3]
        images.append(
            lax.dot_general(matrix[:, :cut], vectors[:, :cut], NT, preferred_element_type=F32).T
        )
        tails.append(vectors[:, cut:])
    none = jnp.zeros_like(tails[0])
    tails = jnp.concatenate(
        [jnp.concatenate([tails[0], none], axis=1), jnp.concatenate([none, tails[1]], axis=1)],
        axis=0,
    )
    matrix = jnp.concatenate([ovl[row, last], ovl[row + 1, last]], axis=1)
    both = lax.dot_general(matrix, tails, NT, preferred_element_type=F32).T
    vecs = none.shape[0]
    return images[0] + both[:vecs], images[1] + both[vecs:]


def cut_kernel(ints, sizes, trial, own, near, give, far, across, sizes_here, here, masked, sems):
    copies = [
        pltpu.make_async_copy(sizes, sizes_here, sems.at[0]),
        pltpu.make_async_copy(trial, here, sems.at[1]),
    ]
    for copy in copies:
        copy.start()
    for copy in copies:
        copy.wait()
    half, _, orbs = own.shape
    core = ints[0]
    lane = lax.broadcasted_iota(jnp.int32, own.shape[1:], 1)
    for row in range(2 * half):
        values = here[:, row * orbs : (row + 1) * orbs].astype(F32)
        masked[row] = jnp.where(lane < sizes_here[row], values, 0.0).astype(BF16)
    spare = half - HALF_BAND
    last = 2 * half - HALF_BAND
    own[...] = masked[pl.ds(half * core, half)]
    near[...] = masked[pl.ds(half - HALF_BAND * core, HALF_BAND)]
    give[...] = masked[pl.ds(spare * (1 - core), half + HALF_BAND)]
    far[...] = masked[pl.ds(last * (1 - core), HALF_BAND)]
    across[...] = masked[pl.ds(last * core, HALF_BAND)]


def load_kernel(total, ints, shift, width, columns, phases, sizes, ham, ovl, *rest):
    ham_out, ovl_out, index, signs, place, scal, columns_here, phases_here, sizes_here = rest[:9]
    sems, more_sems = rest[9:]
    half, slots = index.shape
    first = ints[0] * half
    small = [
        pltpu.make_async_copy(source, target, more_sems.at[i])
        for i, (source, target) in enumerate(
            ((columns, columns_here), (phases, phases_here), (sizes, sizes_here))
        )
    ]
    large = [
        pltpu.make_async_copy(source.at[first + row], target.at[row], sems.at[matrix, row])
        for row in range(half)
        for matrix, (source, target) in enumerate(((ham, ham_out), (ovl, ovl_out)))
    ]
    for copy in small + large:
        copy.start()
    scal[0] = shift[0]
    scal[1] = width[0]
    for i in range(3):
        place[i] = ints[i]
    place[DEVICE_ROW] = ints[4]
    for copy in small:
        copy.wait()
    start = ints[3] + first

    def fill(row, _):
        place[4 + row] = sizes_here[first + row]
        for slot in range(slots):
            away = columns_here[first + row, slot] - (start + row) + HALF_BAND
            away = jnp.where(away < 0, away + total, away)
            away = jnp.where(away >= total, away - total, away)
            index[row, slot] = row + away
            signs[row, slot] = (1 - 2 * phases_here[first + row, slot]).astype(F32)
        return 0

    lax.fori_loop(0, half, fill, 0)
    for copy in large:
        copy.wait()


def scaled_kernel(
    ints, index, signs, scal, own, inter, intra, ham, ovl, out, inter_out, intra_out, ext
):
    core = ints[0]
    fill_ext(core, own, intra, inter, ext)
    inv = 1.0 / (jnp.zeros(own.shape[1:], F32) + scal[1])
    for row in range(own.shape[0]):
        image_h, image_e = both_rows((index, signs), ext, ham, ovl, row)
        mine = own[row].astype(F32)
        out[row] = ((image_h - scal[0] * (mine + image_e)) * inv).astype(BF16)
    send_ends(core, out, intra_out, inter_out)


def term_kernel(ints, index, signs, own, inter, intra, ovl, out, inter_out, intra_out, ext):
    core = ints[0]
    fill_ext(core, own, intra, inter, ext)
    for row in range(0, own.shape[0], 2):
        for i, image in enumerate(two_rows((index, signs), ext, ovl, row)):
            out[row + i] = (-image).astype(BF16)
    send_ends(core, out, intra_out, inter_out)


def update_kernel(first, ints, index, signs, own, inter, intra, scaled, *rest):
    if first:
        ovl, out, inter_out, intra_out, ext = rest
    else:
        previous, ovl, out, inter_out, intra_out, ext = rest
    core = ints[0]
    half = own.shape[0]
    fill_ext(core, own, intra, inter, ext)
    lane = lax.broadcasted_iota(jnp.int32, own.shape[1:], 1)
    images = []
    for row in range(0, half, 2):
        images += two_rows((index, signs), ext, ovl, row)
    for row, image in enumerate(images):
        filtered = scaled[row].astype(F32) + own[row].astype(F32) - image
        if not first:
            filtered = 2.0 * filtered - previous[row].astype(F32)
        out[row] = jnp.where(lane < ints[4 + row], filtered, 0.0).astype(BF16)
    send_ends(core, out, intra_out, inter_out)


def images_kernel(ints, index, signs, own, inter, intra, ham, ovl, y_other, out, ext):
    del y_other
    core = ints[0]
    fill_ext(core, own, intra, inter, ext)
    half, _, orbs = own.shape
    for row in range(half):
        image_h, image_e = both_rows((index, signs), ext, ham, ovl, row)
        at = slice(row * orbs, (row + 1) * orbs)
        out[0, :, at] = (own[row].astype(F32) + image_e).astype(BF16)
        out[1, :, at] = image_h.astype(BF16)


def gram_kernel(chips, ints, *refs):
    images, groups = refs[:CORES], refs[CORES : CORES + CORES * chips]
    keep, send, both = refs[CORES + CORES * chips :]
    core, chip = ints[0], ints[1]
    half, local_vecs, _ = groups[0].shape
    vecs = CORES * local_vecs
    flat = jnp.concatenate(
        [jnp.concatenate([group[row] for row in range(half)], axis=1) for group in groups], axis=0
    )
    eye = lax.broadcasted_iota(jnp.int32, (vecs, vecs), 0) == lax.broadcasted_iota(
        jnp.int32, (vecs, vecs), 1
    )
    for matrix in range(2):
        mine = jnp.concatenate([image[matrix] for image in images], axis=0)
        pair = lax.dot_general(mine, flat, NT, preferred_element_type=F32)
        both[matrix, : vecs // 2, :] = packed(pair[:, :vecs]).astype(BF16)
        for step in range(1, chips):
            block = pair[:, step * vecs : (step + 1) * vecs]
            both[matrix, (2 * step - 1) * vecs // 2 : (2 * step + 1) * vecs // 2, :] = block.astype(BF16)
        diagonal = jnp.sum(jnp.where(eye, pair[:, :vecs], 0.0), axis=0, keepdims=True)
        both[matrix, (2 * chips - 1) * vecs // 2 :, :] = diagonal_parts(diagonal)
    keep[...] = both[core]
    send[...] = both[1 - core]


def packed(block):
    half = block.shape[0] // 2
    block = 0.5 * (block + block.T)
    top, bottom = block[:half], block[half:]
    bottom = jnp.concatenate([bottom[:, half:], bottom[:, :half]], axis=1)
    row = lax.broadcasted_iota(jnp.int32, top.shape, 0)
    lane = lax.broadcasted_iota(jnp.int32, top.shape, 1)
    return jnp.where((lane < half) & (lane > row), bottom, top)


def unpacked(block):
    half = block.shape[0]
    turned = block.T
    row = lax.broadcasted_iota(jnp.int32, (half, half), 0)
    lane = lax.broadcasted_iota(jnp.int32, (half, half), 1)
    square, beside = block[:, :half], block[:, half:]
    first = jnp.where(lane < row, square, turned[:half])
    last = jnp.where(lane > row, square, turned[:half])
    return jnp.concatenate(
        [
            jnp.concatenate([first, beside], axis=1),
            jnp.concatenate([turned[half:], last], axis=1),
        ],
        axis=0,
    )


def diagonal_parts(diagonal):
    high, middle, low = (part.astype(F32) for part in split3(diagonal))
    rows = lax.broadcasted_iota(jnp.int32, (DIAGONAL_ROWS, diagonal.shape[1]), 0)
    parts = jnp.where(rows == 0, high, jnp.where(rows == 1, middle, jnp.where(rows == 2, low, 0.0)))
    return parts.astype(BF16)


def diagonal_of(payload):
    parts = payload[payload.shape[0] - DIAGONAL_ROWS :, :].astype(F32)
    return parts[0:1] + (parts[1:2] + parts[2:3])


def add_kernel(left, right, out):
    body = left.shape[0] - DIAGONAL_ROWS
    out[:body] = (left[:body, :].astype(F32) + right[:body, :].astype(F32)).astype(BF16)
    out[body:] = diagonal_parts(diagonal_of(left) + diagonal_of(right))


def sum_kernel(ints, *refs):
    *payloads, out, held = refs
    count = len(payloads)
    for step, payload in enumerate(payloads):
        held[lax.bitwise_xor(ints[DEVICE_ROW], jnp.int32(step))] = payload[...]
    body = out.shape[0] - DIAGONAL_ROWS
    total = held[0, :body, :].astype(F32)
    diagonal = diagonal_of(held.at[0])
    for r in range(1, count):
        total = total + held[r, :body, :].astype(F32)
        diagonal = diagonal + diagonal_of(held.at[r])
    out[:body] = total.astype(BF16)
    out[body:] = diagonal_parts(diagonal)


def split3(value):
    high = value.astype(BF16)
    rest = value - high.astype(F32)
    middle = rest.astype(BF16)
    low = (rest - middle.astype(F32)).astype(BF16)
    return high, middle, low


def three_terms(left, right, axis):
    (high, middle, _), (other, little, _) = split3(left), split3(right)
    return (
        jnp.concatenate([high, high, middle], axis=1),
        jnp.concatenate([other, little, other], axis=axis),
    )


def panel_inverse(block):
    lane = lax.broadcasted_iota(jnp.int32, (PANEL, 128), 1)
    rows = lax.broadcasted_iota(jnp.int32, (PANEL, 128), 0)
    work = jnp.where(lane < PANEL, block, jnp.where(lax.rem(lane, PANEL) == rows, 1.0, 0.0))
    count = PANEL // SUBLANES
    pieces = [work[v * SUBLANES : (v + 1) * SUBLANES] for v in range(count)]
    sub = lax.broadcasted_iota(jnp.int32, (SUBLANES, 128), 0)

    def spread(value, k):
        return jnp.broadcast_to(value[k % SUBLANES : k % SUBLANES + 1], (SUBLANES, 128))

    pivots = [jnp.ones((SUBLANES, 128), F32) for _ in range(count)]
    for start, group in ((0, 8), (8, 8), (16, 16)):
        columns = {
            k: {
                v: jnp.broadcast_to(pieces[v][:, k : k + 1], (SUBLANES, 128))
                for v in range(start // SUBLANES, count)
            }
            for k in range(start, start + group)
        }
        at = spread(columns[start][start // SUBLANES], start)
        for k in range(start, start + group):
            here = k // SUBLANES
            pivots[here] = jnp.where(sub == k % SUBLANES, at, pivots[here])
            guess = pl.reciprocal(at, approx=True)
            correction = 2.0 - at * guess
            inv = guess * correction
            if k + 1 < start + group:
                below = (k + 1) // SUBLANES
                product = spread(columns[k][below], k + 1) * spread(columns[k + 1][here], k)
                at = spread(columns[k + 1][below], k + 1) - (product * guess) * correction
            factors = {v: columns[k][v] * inv for v in range(here, count)}
            factors[here] = jnp.where(sub > k % SUBLANES, factors[here], 0.0)
            for later in range(k + 1, start + group):
                top = spread(columns[later][here], k)
                for v in range(here, count):
                    columns[later][v] = columns[later][v] - factors[v] * top
            top = spread(pieces[here], k)
            for v in range(here, count):
                pieces[v] = pieces[v] - factors[v] * top
    pivot = jnp.concatenate(pivots, axis=0)
    root = lax.rsqrt(pivot)
    root = root * (1.5 - 0.5 * ((pivot * root) * root))
    return jnp.concatenate(pieces, axis=0) * root


def factor(work, inverse):
    size = work.shape[0]
    wide = lax.broadcasted_iota(jnp.int32, (PANEL, size), 1)
    tall = lax.broadcasted_iota(jnp.int32, (PANEL, size), 0)
    lane = lax.broadcasted_iota(jnp.int32, (PANEL, 128), 1)
    zero = jnp.zeros((PANEL, size), BF16)
    for start in range(0, size, PANEL):
        rows = work[start : start + PANEL, :]
        tile = start // 128 * 128
        block = work[start : start + PANEL, tile : tile + 128]
        if start % 128:
            block = pltpu.roll(block, 128 - start % 128, axis=1)
        t_high, t_mid, t_low = split3(jnp.where(lane < PANEL, 0.0, panel_inverse(block)))
        first = jnp.where(lane < 2 * PANEL, t_high, jnp.where(lane < 3 * PANEL, t_mid, t_low))
        second = jnp.where(lane < 2 * PANEL, t_high, jnp.where(lane < 3 * PANEL, t_mid, t_high))
        left = jnp.concatenate([first, second], axis=1)
        inside = (wide >= start) & (wide < start + PANEL)
        rows = jnp.where(inside, jnp.where(wide - start == tall, 1.0, 0.0), rows)
        r_high, r_mid, r_low = split3(rows)
        right = jnp.concatenate([zero, r_high, r_high, r_high, zero, r_mid, r_mid, r_low], axis=0)
        new = jnp.dot(left, right, preferred_element_type=F32)
        inverse[start : start + PANEL, :] = jnp.where(wide < start + PANEL, new, 0.0)
        after = start + PANEL
        if after < size:
            high, middle, low = split3(new)
            base = after // 128 * 128
            lhs = jnp.concatenate([high, high, middle, middle, high, low], axis=0)[:, base:]
            rhs = jnp.concatenate([high, middle, high, middle, low, high], axis=0)
            change = lax.dot_general(lhs, rhs, TN, preferred_element_type=F32)[after - base :]
            columns = lax.broadcasted_iota(jnp.int32, change.shape, 1)
            old = work[after:, :]
            work[after:, :] = jnp.where((columns >= start) & (columns < after), 0.0, old) - change


def finish_kernel(chips, scale, ints, *refs):
    mine, theirs = refs[:chips], refs[chips : 2 * chips]
    y_mine = refs[2 * chips : (2 + CORES) * chips]
    y_theirs = refs[(2 + CORES) * chips : (2 + 2 * CORES) * chips]
    basis, reduced, pair, work, inverse = refs[(2 + 2 * CORES) * chips :]
    core, chip, col = ints[0], ints[1], ints[2]
    half, local_vecs, orbs = y_mine[0].shape
    vecs = CORES * local_vecs
    eye = lax.broadcasted_iota(jnp.int32, (vecs, vecs), 0) == lax.broadcasted_iota(
        jnp.int32, (vecs, vecs), 1
    )
    for step in range(chips):
        which = lax.rem(chip + step, chips)
        rows = pl.ds(pl.multiple_of(which * vecs, vecs), vecs)
        for matrix, payload in ((core, mine[step]), (1 - core, theirs[step])):
            own_block = unpacked(payload[: vecs // 2, :].astype(F32))
            own_block = jnp.where(eye, diagonal_of(payload), own_block)
            for k in range(chips):
                block = own_block
                for away in range(1, chips):
                    at = (2 * away - 1) * vecs // 2
                    other = payload[at : at + vecs, :].astype(F32)
                    block = jnp.where(lax.rem(which + away, chips) == k, other, block)
                pair[matrix, rows, k * vecs : (k + 1) * vecs] = block
    work[...] = (pair[0] + pair[0].T) * scale
    factor(work, inverse)
    start = pl.multiple_of(col * local_vecs, local_vecs)
    own_rows = inverse[pl.ds(start, local_vecs), :]
    gram_h = (pair[1] + pair[1].T) * scale
    half_way = jnp.dot(*three_terms(own_rows, gram_h, 0), preferred_element_type=F32)
    reduced[...] = lax.dot_general(
        *three_terms(half_way, inverse[...], 1), NT, preferred_element_type=F32
    )
    rotation = own_rows.astype(BF16)
    turned = []
    for step in range(chips):
        which = lax.rem(chip + step, chips)
        part = rotation[:, :vecs]
        for k in range(1, chips):
            part = jnp.where(which == k, rotation[:, k * vecs : (k + 1) * vecs], part)
        turned.append(part)
    turned = jnp.concatenate(turned, axis=1)
    for which, group in ((core, y_mine), (1 - core, y_theirs)):
        for row in range(half):
            everything = jnp.concatenate([vectors[row] for vectors in group], axis=0)
            result = jnp.dot(turned, everything, preferred_element_type=F32).astype(BF16)
            at = pl.multiple_of((which * half + row) * orbs, orbs)
            basis[:, pl.ds(at, orbs)] = result


def local(
    trial_vectors,
    hamiltonian_blocks,
    correlation_offset,
    block_columns,
    block_phases,
    block_sizes,
    shift,
    halfwidth,
):
    blocks_dev, slots = block_columns.shape
    orbs = hamiltonian_blocks.shape[2]
    num_rows, num_cols = lax.axis_size("row"), lax.axis_size("col")
    total_blocks = blocks_dev * num_rows
    half = blocks_dev // CORES
    chips = num_cols // CORES
    local_vecs = trial_vectors.shape[0]
    vecs = local_vecs * CORES
    size = local_vecs * num_cols
    row, col = lax.axis_index("row"), lax.axis_index("col")
    core, chip = lax.rem(col, CORES), lax.div(col, CORES)

    def swap_cores(value):
        return lax.ppermute(value, "col", [(c, c ^ 1) for c in range(num_cols)])

    def swap_chips(value):
        pairs = []
        for r in range(num_rows):
            for x in range(chips):
                upper = r * num_cols + x * CORES + 1
                lower = (r + 1) % num_rows * num_cols + x * CORES
                pairs += [(upper, lower), (lower, upper)]
        return lax.ppermute(value, ("row", "col"), pairs)

    def next_chips(value):
        pairs = []
        for r in range(num_rows):
            for c in range(num_cols):
                to = (r + 1 if c % CORES == 0 else r - 1) % num_rows
                pairs.append((r * num_cols + c, to * num_cols + c))
        return lax.ppermute(value, ("row", "col"), pairs)

    def from_chip(value, step):
        pairs = [((c + step * CORES) % num_cols, c) for c in range(num_cols)]
        return lax.ppermute(value, "col", pairs)

    state = jax.ShapeDtypeStruct((half, local_vecs, orbs), BF16)
    end = jax.ShapeDtypeStruct((HALF_BAND, local_vecs, orbs), BF16)
    ext = pltpu.VMEM((half + 2 * HALF_BAND, local_vecs, orbs), BF16)
    params = pltpu.CompilerParams(vmem_limit_bytes=16 << 20)
    row_flops = SLOWER * 2 * half * slots * local_vecs * orbs * orbs

    def call(kernel, name, scalars, arrays, outs, scratch, flops):
        return pl.pallas_call(
            kernel,
            name=name,
            out_shape=outs,
            in_specs=[SMEM] * len(scalars) + [VMEM] * len(arrays),
            out_specs=(VMEM,) * len(outs),
            scratch_shapes=scratch,
            compiler_params=params,
            cost_estimate=pl.CostEstimate(
                flops=flops, bytes_accessed=flops // 128, transcendentals=0
            ),
        )(*scalars, *arrays)

    def step_call(kernel, name, scalars, arrays, flops):
        return call(kernel, name, scalars, arrays, (state, end, end), [ext], flops)

    def exchange(ends):
        return swap_chips(ends[0]), swap_cores(ends[1])

    def scalars(value):
        return pltpu.with_memory_space_constraint(value, pltpu.SMEM)

    ints = scalars(jnp.stack([core, chip, col, row * blocks_dev, row]).astype(jnp.int32))
    shift, halfwidth = scalars(shift), scalars(halfwidth)

    def stays(value):
        return pltpu.with_memory_space_constraint(value, pltpu.HBM)

    more = jax.ShapeDtypeStruct((half + HALF_BAND, local_vecs, orbs), BF16)
    own, near, give, far, across = pl.pallas_call(
        cut_kernel,
        name="cut",
        out_shape=(state, end, more, end, end),
        in_specs=[SMEM, HBM, HBM],
        out_specs=(VMEM,) * 5,
        scratch_shapes=[
            pltpu.SMEM(block_sizes.shape, jnp.int32),
            pltpu.VMEM(trial_vectors.shape, BF16),
            pltpu.VMEM((blocks_dev, local_vecs, orbs), BF16),
            pltpu.SemaphoreType.DMA((2,)),
        ],
        compiler_params=params,
    )(ints, stays(block_sizes), stays(trial_vectors))
    far, across = next_chips(far), swap_chips(across)
    got = swap_cores(give)
    matrix = vmem((half, *hamiltonian_blocks.shape[1:]), BF16)
    ham, ovl, index, signs, place, scal = pl.pallas_call(
        functools.partial(load_kernel, total_blocks),
        name="load",
        out_shape=(
            matrix,
            matrix,
            pltpu.SMEM((half, slots), jnp.int32),
            pltpu.SMEM((half, slots), F32),
            pltpu.SMEM((4 + half,), jnp.int32),
            pltpu.SMEM((2,), F32),
        ),
        in_specs=[SMEM] * 3 + [HBM] * 5,
        out_specs=(VMEM, VMEM, SMEM, SMEM, SMEM, SMEM),
        scratch_shapes=[
            pltpu.SMEM(block_columns.shape, jnp.int32),
            pltpu.SMEM(block_phases.shape, jnp.int32),
            pltpu.SMEM(block_sizes.shape, jnp.int32),
            pltpu.SemaphoreType.DMA((2, half)),
            pltpu.SemaphoreType.DMA((3,)),
        ],
        compiler_params=params,
        cost_estimate=pl.CostEstimate(
            flops=0, bytes_accessed=4 * hamiltonian_blocks.size, transcendentals=0
        ),
    )(
        ints,
        shift,
        halfwidth,
        stays(block_columns),
        stays(block_phases),
        stays(block_sizes),
        stays(hamiltonian_blocks),
        stays(correlation_offset),
    )
    got_own = lax.dynamic_slice_in_dim(got, HALF_BAND * core, half, 0)
    got_near = lax.dynamic_slice_in_dim(got, half * (1 - core), HALF_BAND, 0)

    def by_group(mine, other):
        return [jnp.where(core == 0, mine, other), jnp.where(core == 0, other, mine)]

    current = by_group(own, got_own)
    halo = list(zip(by_group(far, across), by_group(near, got_near)))
    table = (place, index, signs)
    scaled, term, previous = [None] * CORES, [None] * CORES, list(current)
    for degree in range(DEGREE):
        for g in range(CORES):
            if g > 0:
                current[g], scaled[0] = lax.optimization_barrier((current[g], scaled[0]))
            scaled[g], *ends = step_call(
                scaled_kernel,
                "scaled",
                (*table, scal),
                (current[g], *halo[g], ham, ovl),
                2 * row_flops,
            )
            halo[g] = exchange(ends)
        for g in range(CORES):
            term[g], *ends = step_call(
                term_kernel, "term", table, (scaled[g], *halo[g], ovl), row_flops
            )
            halo[g] = exchange(ends)
        for g in range(CORES):
            first = degree == 0
            arrays = (term[g], *halo[g], scaled[g]) + (() if first else (previous[g],)) + (ovl,)
            updated, *ends = step_call(
                functools.partial(update_kernel, first),
                "update",
                table,
                arrays,
                row_flops,
            )
            halo[g] = exchange(ends)
            previous[g], current[g] = current[g], updated

    y_others = [from_chip(value, step) for step in range(1, chips) for value in current]
    image = jax.ShapeDtypeStruct((2, local_vecs, half * orbs), BF16)
    images = []
    for g, vectors in enumerate(current):
        if g > 0:
            vectors, images[0] = lax.optimization_barrier((vectors, images[0]))
        images += call(
            images_kernel,
            "images",
            table,
            (vectors, *halo[g], ham, ovl, y_others[0]),
            (image,),
            [ext],
            2 * row_flops,
        )
    payload = jax.ShapeDtypeStruct((size - vecs // 2 + DIAGONAL_ROWS, vecs), BF16)
    keep, send = call(
        functools.partial(gram_kernel, chips),
        "gram",
        (place,),
        (*images, *current, *y_others),
        (payload, payload),
        [pltpu.VMEM((2, *payload.shape), BF16)],
        row_flops,
    )

    def add(left, right):
        return call(add_kernel, "add", (), (left, right), (payload,), [], row_flops // 8)[0]

    summed = add(keep, swap_cores(send))
    if num_rows in (2, 4):
        others = [
            lax.ppermute(summed, "row", [(r, r ^ step) for r in range(num_rows)])
            for step in range(1, num_rows)
        ]
        (summed,) = call(
            sum_kernel,
            "sum",
            (place,),
            (summed, *others),
            (payload,),
            [pltpu.VMEM((num_rows, *payload.shape), BF16)],
            row_flops // 8,
        )
    elif num_rows & (num_rows - 1):
        every = lax.all_gather(summed, "row")
        summed = every[0]
        for r in range(1, num_rows):
            summed = add(summed, every[r])
    else:
        bit = 1
        while bit < num_rows:
            other = lax.ppermute(summed, "row", [(r, r ^ bit) for r in range(num_rows)])
            summed = add(summed, other)
            bit *= 2
    mine = [summed] + [from_chip(summed, step) for step in range(1, chips)]
    theirs = [swap_cores(value) for value in mine]
    y_theirs = [swap_cores(value) for value in (*current, *y_others)]
    basis, reduced = call(
        functools.partial(finish_kernel, chips, 0.5 / (total_blocks * orbs)),
        "finish",
        (place,),
        (*mine, *theirs, *current, *y_others, *y_theirs),
        (
            jax.ShapeDtypeStruct((local_vecs, blocks_dev * orbs), BF16),
            jax.ShapeDtypeStruct((local_vecs, size), F32),
        ),
        [
            pltpu.VMEM((2, size, size), F32),
            pltpu.VMEM((size, size), F32),
            pltpu.VMEM((size, size), F32),
        ],
        10 * row_flops,
    )
    return basis, reduced.T


def solution(mesh):
    return jax.shard_map(
        local,
        mesh=mesh,
        in_specs=(
            P("col", ("pool", "row")),
            P(("pool", "row"), None, None, None),
            P(("pool", "row"), None, None, None),
            P(("pool", "row"), None),
            P(("pool", "row"), None),
            P(("pool", "row")),
            P("pool"),
            P("pool"),
        ),
        out_specs=(P("col", ("pool", "row")), P("pool", "col")),
        check_vma=False,
    )
```
